32 devices in a mesh: wide: 8 (over z, x), narrow: 4 (over y, core).
Axes of the slice: x: 2, y: 2, z: 4, core: 2. Of those that a mesh axis runs over, the one named last changes fastest.
Arguments:
- tokens: bfloat16 [32768, 512], P(('wide', 'narrow')), may hold values from -6 to 6
- memory: bfloat16 [32768, 512], P(('wide', 'narrow')), may hold values from -6 to 6
- slot_cotangent: bfloat16 [32768, 512], P(('wide', 'narrow')), may hold values from -6 to 6
- param_slabs: bfloat16 [37376, 128], P(('wide', 'narrow')), may hold values from -1.5 to 1.5
- segment_ids: int32 [32, 1024], P(('wide', 'narrow')), may hold values from 0 to 3, never falling along the last dimension, each value on 1 to 512 neighbouring positions
- memory_lengths: int32 [32, 4], P(('wide', 'narrow')), may hold values from 1 to 512, 1024 in all within a row
- slot_mask: int32 [32, 1024], P(('wide', 'narrow')), may hold values 0 or 1
Outputs:
- slot_states: bfloat16 [32768, 512], P(('wide', 'narrow'))
- tokens_grad: bfloat16 [32768, 512], P(('wide', 'narrow'))
- memory_grad: bfloat16 [32768, 512], P(('wide', 'narrow'))
- param_grad: float32 [37376, 128], P(('wide', 'narrow'))
The draws below stay inside these ranges and needn't reach their ends.
Inputs may be any that keep to these rules, and one draw needn't show every extreme that they name: `segment_ids`: in each row the ids never fall, every id of 0 to 3 appears, and some sequence has exactly 512 tokens. `memory_lengths`: each row's lengths sum to 1024; the largest is exactly 512.
All inputs are finite; a program needn't handle non-finite values. No bound on the sum of `slot_mask` on one device may be relied on, other than what follows from the above.
Results may differ from the reference program's by a relative error of at most 0.024.
The reference program's roundings to bfloat16 on the way count: a program that leaves them out, or rounds other values in their place, can miss the bound.
Values may be sent and summed in bfloat16 or wider, within the bound.
No kernel may reach another device: no remote copies, remote signals or barrier semaphores. Data moves between devices by JAX's collectives and lax.ppermute only.
A program may use at most 128 MiB of HBM per device.

```python
import math
import jax
import jax.numpy as jnp
import numpy as np
from jax import lax

D = 512
HEADS = 8
HD = 64
FF = 2048
ROW = 1024
SEQS = 4
MOST = 512
MEM = 1024
MEM_MOST = 512
ROWS = 32
TOKENS = 32768
MEMTOK = 32768
PROWS = 37376


def draw_param_slabs(key, part):
    key = jax.random.fold_in(key, 7)
    total_size = PROWS * 128
    positions = jnp.arange(total_size)
    normal_part = jax.random.truncated_normal(key, -2.0, 2.0, (total_size,), jnp.float32)
    even_part = jax.random.uniform(jax.random.fold_in(key, 1), (total_size,), jnp.float32, -1.0, 1.0)
    square = D * D
    attention_factors = [1.4 / math.sqrt(D), 1.4 / math.sqrt(D), 1.0 / math.sqrt(D), 4.0 / math.sqrt(D)]
    segments_table = [(square, factor, 0.0) for factor in attention_factors]
    segments_table = segments_table + segments_table
    segments_table = segments_table + [(D * FF, 1.0 / math.sqrt(D), 0.0), (FF * D, 2.0 / math.sqrt(FF), 0.0), (2 * square, 1.0 / math.sqrt(2 * D), 0.0)]
    segments_table = segments_table + [(D, 0.3, 0.0)] * 6
    segments_table = segments_table + [(D, 0.0, 1.0), (D, 0.3, 0.0)] * 3
    segments_table = segments_table + [(D, 0.3, 0.0), (D, 0.3, 0.0), (FF, 0.3, 0.0)]
    scale_values = jnp.zeros((total_size,), jnp.float32)
    gain_flags = jnp.zeros((total_size,), jnp.float32)
    offset = 0
    for amount, factor, gain_flag in segments_table:
        inside = (positions >= offset) & (positions < offset + amount)
        scale_values = jnp.where(inside, factor, scale_values)
        gain_flags = jnp.where(inside, gain_flag, gain_flags)
        offset += amount
    drawn = jnp.where(gain_flags > 0.5, 1.0 + 0.4 * even_part, scale_values * normal_part)
    return drawn.reshape(PROWS, 128).astype(jnp.bfloat16)


def with_ends(values, rng, least, largest):
    longest = values.shape.index(max(values.shape))
    spots = []
    for shift in (0, 1):
        where = [jax.random.randint(jax.random.fold_in(rng, axis), (), 0, length) for axis, length in enumerate(values.shape)]
        where[longest] = (where[longest] + shift) % values.shape[longest]
        spots.append(tuple(where))
    return values.at[spots[0]].set(least).at[spots[1]].set(largest)


def shard_levels(own_key, extent, cuts, low, largest):
    factor_of = 1.0
    for dim, shards_of in cuts:
        steps = jax.random.uniform(jax.random.fold_in(jax.random.fold_in(own_key, 6), dim), (shards_of,), jnp.float32, low / len(cuts), largest / len(cuts))
        factor_of = factor_of * jnp.repeat(jnp.exp(steps), extent[dim] // shards_of).reshape((-1,) + (1,) * (len(extent) - 1 - dim))
    return factor_of


def split_up(count, total, reach, lean):
    weights = [(1 << 20) // math.isqrt(standing ** lean) + 1 for standing in range(2, count + 1)]
    spare, holding = total - reach - (count - 1), [1] * (count - 1)
    while spare > 0:
        candidates = [i for i in range(count - 1) if holding[i] < reach]
        whole, left = sum([weights[i] for i in candidates]), spare
        for i in candidates:
            more = min(reach - holding[i], max(1, left * weights[i] // whole), spare)
            holding[i] = holding[i] + more
            spare = spare - more
    return np.array([reach] + holding)


def uneven_parts(key, count, total, most, lean):
    if count == 2:
        one = jax.random.randint(key, (), max(1, total - most), min(most, total - 1) + 1)
        return jnp.stack([one, total - one])
    tallies = jnp.asarray(split_up(count, total, most, lean), jnp.int32)
    pairs = (count - 1) // 2
    donor, taker = tallies[1:1 + 2 * pairs:2], tallies[2:2 + 2 * pairs:2]
    slack = jnp.minimum(donor - 1, most - taker)
    passed = jax.random.randint(jax.random.fold_in(key, 1), (pairs,), 0, 1 << 20) % (slack + 1)
    tallies = tallies.at[1:1 + 2 * pairs:2].set(donor - passed).at[2:2 + 2 * pairs:2].set(taker + passed)
    return tallies[jax.random.permutation(jax.random.fold_in(key, 2), count)]


def scatter_about(key, extent, spread, bound, split=(), kind=jnp.bfloat16):
    array = jax.random.normal(key, extent, jnp.float32) * spread
    if len(split) > 0:
        array = shard_levels(key, extent, split, -0.22, 0.18) * array
    return jnp.clip(array, min=-bound, max=bound).astype(kind)


def setup_inputs(seed: int = 0) -> dict:
    key_of = jax.random.split(jax.random.key(seed), 8)
    tokens = scatter_about(key_of[0], (TOKENS, D), 1.0, 6.0, ((0, 32),))
    memory = scatter_about(key_of[1], (MEMTOK, D), 1.0, 6.0, ((0, 32),))
    slot_cotangent = scatter_about(key_of[2], (TOKENS, D), 1.0, 6.0, ((0, 32),))
    param_slabs = draw_param_slabs(jax.random.fold_in(key_of[7], 71), 0)
    segment_ids = jax.vmap(lambda own: jnp.searchsorted(jnp.cumsum(uneven_parts(own, SEQS, ROW, MOST, 1)), jnp.arange(ROW), side="right"))(jax.random.split(key_of[4], ROWS)).reshape((ROWS, ROW)).astype(jnp.int32)
    memory_lengths = jax.vmap(lambda own: uneven_parts(own, SEQS, MEM, MEM_MOST, 1))(jax.random.split(key_of[5], ROWS)).reshape((ROWS, SEQS)).astype(jnp.int32)
    slot_mask = with_ends((jax.random.randint(key_of[6], (ROWS, ROW), 0, 4) < 3).astype(jnp.int32), jax.random.fold_in(key_of[6], 1), 0, 1)
    return {"tokens": tokens, "memory": memory, "slot_cotangent": slot_cotangent, "param_slabs": param_slabs, "segment_ids": segment_ids, "memory_lengths": memory_lengths, "slot_mask": slot_mask}


HIGHEST = lax.Precision.HIGHEST
EPSILON = 1e-05

@jax.custom_vjp
def low(v):
    return lax.optimization_barrier(v.astype(jnp.bfloat16)).astype(jnp.float32)

@jax.custom_vjp
def low_back(v):
    return v

def low_keep(v):
    return (low(v), None)

def low_pass(kept, grad):
    return (grad,)

def back_keep(v):
    return (v, None)

def back_low(kept, grad):
    return (low(grad),)
low.defvjp(low_keep, low_pass)
low_back.defvjp(back_keep, back_low)

def both(values):
    return low(low_back(values))

def entries(model_width, inner_width):
    square = (model_width, model_width)
    vector = (model_width,)
    return [('query_w', square), ('key_w', square), ('value_w', square), ('out_w', square), ('cross_query_w', square), ('cross_key_w', square), ('cross_value_w', square), ('cross_out_w', square), ('inner_w', (model_width, inner_width)), ('outer_w', (inner_width, model_width)), ('slot_w', (2 * model_width, model_width)), ('query_b', vector), ('value_b', vector), ('out_b', vector), ('cross_query_b', vector), ('cross_value_b', vector), ('cross_out_b', vector), ('gain_one', vector), ('shift_one', vector), ('gain_two', vector), ('shift_two', vector), ('gain_three', vector), ('shift_three', vector), ('outer_b', vector), ('slot_b', vector), ('inner_b', (inner_width,))]

def unpack(flat_values, model_width, inner_width):
    params = {}
    offset = 0
    for entry_name, entry_shape in entries(model_width, inner_width):
        amount = math.prod(entry_shape)
        params[entry_name] = flat_values[offset:offset + amount].reshape(entry_shape)
        offset += amount
    return params

def matmul(first_matrix, second_matrix):
    return jnp.dot(first_matrix, second_matrix, precision=HIGHEST)

def layer_norm(values, gain, shift):
    centered = values - lax.optimization_barrier(jnp.mean(values, axis=-1, keepdims=True))
    variance = lax.optimization_barrier(jnp.mean(centered * centered, axis=-1, keepdims=True))
    return centered * lax.rsqrt(variance + EPSILON) * gain + shift

def attend(queries, keys, values, query_ids, key_ids):
    query_heads = queries.reshape(queries.shape[0], HEADS, HD)
    key_heads = keys.reshape(keys.shape[0], HEADS, HD)
    value_heads = values.reshape(values.shape[0], HEADS, HD)
    scores = jnp.einsum('qhd,khd->hqk', query_heads, key_heads, precision=HIGHEST) * HD ** (-0.5)
    allowed = (query_ids[:, None] == key_ids[None, :])[None]
    scores = low_back(jnp.where(allowed, scores, -1000000000.0))
    probs = low(jax.nn.softmax(scores, axis=-1))
    mixed = jnp.einsum('hqk,khd->qhd', probs, value_heads, precision=HIGHEST)
    return both(mixed.reshape(queries.shape[0], HEADS * HD))

def layer_row(flat_values, tokens, memory, segment_row, memory_row_ids, mask_row):
    weights = unpack(flat_values, D, FF)
    queries = both(matmul(tokens, weights['query_w']) + weights['query_b'])
    keys = both(matmul(tokens, weights['key_w']))
    values = both(matmul(tokens, weights['value_w']) + weights['value_b'])
    attended = attend(queries, keys, values, segment_row, segment_row)
    self_branch = low_back(matmul(attended, weights['out_w']) + weights['out_b'])
    h_one = layer_norm(tokens + self_branch, weights['gain_one'], weights['shift_one'])
    cross_queries = both(matmul(low(h_one), weights['cross_query_w']) + weights['cross_query_b'])
    memory_keys = both(matmul(memory, weights['cross_key_w']))
    memory_values = both(matmul(memory, weights['cross_value_w']) + weights['cross_value_b'])
    cross_attended = attend(cross_queries, memory_keys, memory_values, segment_row, memory_row_ids)
    cross_branch = low_back(matmul(cross_attended, weights['cross_out_w']) + weights['cross_out_b'])
    h_two = layer_norm(h_one + cross_branch, weights['gain_two'], weights['shift_two'])
    pre_act = low_back(matmul(low(h_two), weights['inner_w']) + weights['inner_b'])
    activ = both(jax.nn.gelu(pre_act, approximate=True))
    ffn_branch = low_back(matmul(activ, weights['outer_w']) + weights['outer_b'])
    h_three = layer_norm(h_two + ffn_branch, weights['gain_three'], weights['shift_three'])
    h_low = low(h_three)
    later_ids = jnp.concatenate([segment_row[1:], jnp.full((1,), -1, jnp.int32)])
    same_next = segment_row == later_ids
    shifted = jnp.concatenate([h_low[1:], jnp.zeros((1, h_low.shape[1]), h_low.dtype)], axis=0)
    following = jnp.where(same_next[:, None], shifted, 0.0)
    paired = jnp.concatenate([h_low, following], axis=1)
    return mask_row[:, None] * (matmul(paired, weights['slot_w']) + weights['slot_b'])

def reference(tokens, memory, slot_cotangent, param_slabs, segment_ids, memory_lengths, slot_mask):
    flat_all = param_slabs.astype(jnp.float32).reshape(-1)
    used = 10 * D * D + 2 * D * FF + 14 * D + FF
    flat_used = flat_all[:used]
    row_total = segment_ids.shape[0]
    token_rows = tokens.astype(jnp.float32).reshape(row_total, ROW, D)
    memory_rows = memory.astype(jnp.float32).reshape(row_total, MEM, D)
    cotangent_rows = slot_cotangent.astype(jnp.float32).reshape(row_total, ROW, D)
    mask_rows = slot_mask.astype(jnp.float32)
    bounds = jnp.cumsum(memory_lengths, axis=1)
    positions = jnp.arange(MEM, dtype=jnp.int32)
    memory_ids = lax.optimization_barrier(jnp.sum((positions[None, :, None] >= bounds[:, None, :]).astype(jnp.int32), axis=2))

    def one_row(carry, row_items):
        token_row, memory_row, cotangent_row, segment_row, memory_row_ids, mask_row = row_items

        def forward(flat_in, token_in, memory_in):
            return layer_row(flat_in, token_in, memory_in, segment_row, memory_row_ids, mask_row)
        slots, backward = jax.vjp(forward, flat_used, token_row, memory_row)
        grad_flat, grad_tokens, grad_memory = backward(cotangent_row)
        return (carry + grad_flat, (slots.astype(jnp.bfloat16), grad_tokens.astype(jnp.bfloat16), grad_memory.astype(jnp.bfloat16)))
    total_grad, outputs = lax.scan(one_row, jnp.zeros((used,), jnp.float32), (token_rows, memory_rows, cotangent_rows, segment_ids, memory_ids, mask_rows))
    slots, grad_tokens, grad_memory = outputs
    param_grad = jnp.pad(total_grad, (0, flat_all.shape[0] - used)).reshape(-1, 128)
    return (slots.reshape(-1, D), grad_tokens.reshape(-1, D), grad_memory.reshape(-1, D), param_grad)
```

```python
import functools
import math

import jax
import jax.numpy as jnp
from jax import lax
from jax.experimental import pallas as pl
from jax.experimental.pallas import tpu as pltpu
from jax.sharding import PartitionSpec as P

D = 512
HEADS = 8
HD = 64
FF = 2048
EPSILON = 1e-05
AXES = ("wide", "narrow")
QB = 128
PAIRS = HEADS // 2
BIG = -1e30
LOG2E = math.log2(math.e)
Q_SCALE = LOG2E * HD ** (-0.5)

f32 = jnp.float32
bf16 = jnp.bfloat16

ROW_Q, ROW_K, ROW_V, ROW_O = 0, 512, 1024, 1536
ROW_CQ, ROW_CK, ROW_CV, ROW_CO = 2048, 2560, 3072, 3584
ROW_IN, ROW_OUT, ROW_SLOT, ROW_VEC = 4096, 6144, 8192, 9216
VEC_ROWS = 32
VEC_NAMES = (
    "query_b", "value_b", "out_b", "cross_query_b", "cross_value_b", "cross_out_b", "gain_one",
    "shift_one", "gain_two", "shift_two", "gain_three", "shift_three", "outer_b", "slot_b", "inner_b",
)
VEC = {name: place for place, name in enumerate(VEC_NAMES)}

VMEM_LIMIT = 58 * 1024 * 1024


def dot(a, b):
    return jnp.dot(a, b, preferred_element_type=f32)


def dot_nt(a, b):
    return lax.dot_general(a, b, (((1,), (1,)), ((), ())), preferred_element_type=f32)


def dot_tn(a, b):
    return lax.dot_general(a, b, (((0,), (0,)), ((), ())), preferred_element_type=f32)


def column_sum(matrix):
    return jnp.sum(matrix.astype(f32), axis=0, keepdims=True)


def normalize(values):
    centered = values - jnp.mean(values, axis=-1, keepdims=True)
    root = lax.rsqrt(jnp.mean(centered * centered, axis=-1, keepdims=True) + EPSILON)
    return centered * root, root


def normalize_back(grad, normal, root, gain):
    scaled = grad * gain
    first = jnp.mean(scaled, axis=-1, keepdims=True)
    second = jnp.mean(scaled * normal, axis=-1, keepdims=True)
    return root * (scaled - first - normal * second)


CHIP_ROWS = 584
CORE_ROWS = 292
UNIT = 592
UNITS = 16


def unit_begin(unit):
    return 2 * CHIP_ROWS * (unit // 2) + UNIT * (unit % 2)


def unit_parts(begin, rows):
    parts = []
    for unit in range(UNITS):
        low = max(begin, unit_begin(unit))
        high = min(begin + rows, unit_begin(unit + 1))
        if low < high:
            parts.append((unit, low - unit_begin(unit), low - begin, high - low))
    return parts


def group_of(unit):
    return min(unit // 4, 2)


class Place:
    def __init__(self, bounds=None):
        if bounds is not None:
            self.token_bounds = [bounds[i] for i in range(3)]
            self.memory_bounds = [bounds[3 + i] for i in range(3)]
        wide, narrow = lax.axis_index("wide"), lax.axis_index("narrow")
        self.z, self.x = lax.div(wide, 2), lax.rem(wide, 2)
        self.y, self.core = lax.div(narrow, 2), lax.rem(narrow, 2)

    def turned(self, unit):
        z, x, y = unit // 4, unit // 2 % 2, unit % 2
        low = jnp.bitwise_xor(lax.rem(self.z, 2), z % 2) if group_of(unit) == 2 else 0
        return jnp.bitwise_xor(self.x, x), jnp.bitwise_xor(self.y, y), low


class Units:
    count = 8

    def __init__(self, groups, refs):
        self.groups = {
            group: (refs[8 * i : 8 * i + 4], refs[8 * i + 4 : 8 * i + 8])
            for i, group in enumerate(groups)
        }

    def load(self, place, begin, buffer, sem):
        return self.load_parts(place, unit_parts(begin, buffer.shape[0]), buffer, sem)

    def load_vectors(self, place, buffer, sem):
        return self.load_parts(place, [(3, UNIT - 16, 0, 16)], buffer, sem)

    def load_parts(self, place, parts, buffer, sem):
        copies = []
        for unit, source, target, rows in parts:
            halves = self.groups[group_of(unit)]
            far_x, far_y, low = place.turned(unit)
            targets = [
                [
                    buffer.at[
                        pl.ds(target, rows),
                        pl.ds(
                            pl.multiple_of(
                                (jnp.bitwise_xor(place.core, half) * 2 + quarter) * 128, 128
                            ),
                            128,
                        ),
                    ]
                    for quarter in range(2)
                ]
                for half in range(2)
            ]

            def part(half, which, quarter):
                return halves[half][which].at[quarter, low, pl.ds(source, rows), :]

            for which in range(4):

                @pl.when((far_x == which % 2) & (far_y == which // 2))
                def _():
                    for half in range(2):
                        for quarter in range(2):
                            pltpu.make_async_copy(
                                part(half, which, quarter), targets[half][quarter], sem
                            ).start()

            copies += [
                pltpu.make_async_copy(part(half, 0, quarter), targets[half][quarter], sem)
                for half in range(2)
                for quarter in range(2)
            ]
        return copies


class Pieces:
    count = 4

    def __init__(self, groups, refs):
        self.refs = refs[:4]

    def load(self, place, begin, buffer, sem):
        copies = []
        for i, ref in enumerate(self.refs):
            copy = pltpu.make_async_copy(
                ref.at[pl.ds(begin, buffer.shape[0]), :],
                buffer.at[:, i * 128 : (i + 1) * 128],
                sem,
            )
            copy.start()
            copies.append(copy)
        return copies

    def load_vectors(self, place, buffer, sem):
        return self.load(place, ROW_VEC, buffer, sem)


def wait_all(copies):
    for copy in copies:
        copy.wait()


def vector(vec_ref, name):
    return vec_ref[VEC[name] : VEC[name] + 1, :].astype(f32)


class UnitSink:
    def __init__(self, refs):
        self.refs = refs

    def places(self, place, begin, rows):
        for unit, at, source, count in unit_parts(begin, rows):
            if unit in self.refs:
                yield self.refs[unit], (), at, source, count
            elif group_of(unit) + 100 in self.refs:
                far_x, far_y, low = place.turned(unit)
                yield self.refs[group_of(unit) + 100], (far_x + 2 * far_y, low), at, source, count

    def vector_places(self, place):
        far_x, far_y, low = place.turned(3)
        yield self.refs[100], (far_x + 2 * far_y, low), UNIT - 16, 0, 16


class RowSink:
    def __init__(self, refs, first):
        self.refs = refs
        self.first = first

    def places(self, place, begin, rows):
        yield self.refs, (), begin - self.first, 0, rows

    def vector_places(self, place):
        yield self.refs, (), 2048, 0, 16


def put_grad(sink, place, begin, value):
    put_places(place, sink.places(place, begin, value.shape[0]), value)


def put_places(place, places, value):
    low = value.astype(bf16)
    for (send, keep), lead, at, source, count in places:
        for core in range(2):

            @pl.when(place.core == core)
            def _():
                for i in range(4):
                    ref = keep if i // 2 == core else send
                    ref[(i % 2, *lead, pl.ds(at, count), slice(None))] = low[
                        source : source + count, i * 128 : (i + 1) * 128
                    ]


def segment_of(position, bounds):
    return sum([(position >= bound).astype(jnp.int32) for bound in bounds])


def pick(index, choices):
    value = choices[-1]
    for place in range(len(choices) - 2, -1, -1):
        value = jnp.where(index == place, choices[place], value)
    return value


def key_range(first_query, query_bounds, key_bounds, length):
    low = segment_of(first_query, query_bounds)
    high = segment_of(first_query + (QB - 1), query_bounds)
    begin = pick(low, [0, *key_bounds]) // 128
    end = (pick(high, [*key_bounds, length]) + 127) // 128
    return begin * 128, end - begin


def query_marks(first_query, bounds):
    position = first_query + lax.broadcasted_iota(jnp.int32, (QB, 128), 0)
    lane = lax.broadcasted_iota(jnp.int32, (QB, 128), 1)
    hidden = (lane <= len(bounds)) & (lane != segment_of(position, bounds))
    return jnp.where(hidden, BIG, 0.0).astype(bf16)


def key_marks(length, bounds):
    position = lax.broadcasted_iota(jnp.int32, (length, 128), 0)
    lane = lax.broadcasted_iota(jnp.int32, (length, 128), 1)
    return jnp.where(lane == segment_of(position, bounds), 1.0, 0.0).astype(bf16)


def stack_heads(pair):
    lane = lax.broadcasted_iota(jnp.int32, pair.shape, 1)
    nothing = jnp.zeros_like(pair)
    return jnp.concatenate(
        [jnp.where(lane < HD, pair, nothing), jnp.where(lane >= HD, pair, nothing)], axis=0
    )


def by_count(count, most, body):
    for value in range(1, most + 1):

        @pl.when(count == value)
        def _():
            body(value)


def lanes(pair):
    return slice(pair * 128, (pair + 1) * 128)


def marked_keys(k_ref, kx, key_bounds):
    marks = key_marks(k_ref.shape[0], key_bounds)
    for pair in range(PAIRS):
        kx[pair, :, 0:128] = k_ref[:, lanes(pair)]
        kx[pair, :, 128:256] = marks


def attend(q_ref, kx, vt, ot_ref, o_ref, lse_ref, query_bounds, key_bounds):
    length = kx.shape[1]

    def block(index, carry):
        first = pl.multiple_of(index * QB, QB)
        begin, count = key_range(first, query_bounds, key_bounds, length)
        begin = pl.multiple_of(begin, 128)
        queries = pl.ds(first, QB)
        marks = query_marks(first, query_bounds)
        marks = jnp.concatenate([marks, marks], axis=0)

        def run(blocks):
            keys = pl.ds(begin, 128 * blocks)
            scores = []
            for pair in range(PAIRS):
                wide = jnp.concatenate([stack_heads(q_ref[queries, lanes(pair)]), marks], axis=1)
                scores.append(dot_nt(kx[pair, keys, :], wide))
            tops = []
            probs = []
            for pair in range(PAIRS):
                top = jnp.max(scores[pair], axis=0, keepdims=True)
                tops.append(top)
                probs.append(jnp.exp2(scores[pair] - top).astype(bf16))
            mixed = [dot(vt[pair, :, keys], probs[pair]) for pair in range(PAIRS)]
            for pair in range(PAIRS):
                total = mixed[pair][128:129, :]
                scale = 1.0 / total
                lse = tops[pair] + jnp.log2(total)
                one = mixed[pair][0:64, 0:128] * scale[:, 0:128]
                two = mixed[pair][64:128, 128:256] * scale[:, 128:256]
                out = jnp.concatenate([one, two], axis=0)
                ot_ref[lanes(pair), queries] = out.astype(bf16)
                o_ref[queries, lanes(pair)] = out.T.astype(bf16)
                lse_ref[2 * pair : 2 * pair + 1, queries] = lse[:, 0:128]
                lse_ref[2 * pair + 1 : 2 * pair + 2, queries] = lse[:, 128:256]

        by_count(count, length // 128, run)
        return carry

    lax.fori_loop(0, q_ref.shape[0] // QB, block, 0)


def attend_back(
    q_ref, kx, kt, v_ref, do_ref, lse_ref, dq_ref, dk_sum, dv_sum, query_bounds, key_bounds
):
    length = kx.shape[1]
    dk_sum[...] = jnp.zeros_like(dk_sum)
    dv_sum[...] = jnp.zeros_like(dv_sum)

    def block(index, carry):
        first = pl.multiple_of(index * QB, QB)
        begin, count = key_range(first, query_bounds, key_bounds, length)
        begin = pl.multiple_of(begin, 128)
        queries = pl.ds(first, QB)
        marks = query_marks(first, query_bounds)
        marks = jnp.concatenate([marks, marks], axis=0)

        def run(blocks):
            keys = pl.ds(begin, 128 * blocks)

            def products(pair):
                q_two = stack_heads(q_ref[queries, lanes(pair)])
                do_two = stack_heads(do_ref[queries, lanes(pair)])
                scores = dot_nt(kx[pair, keys, :], jnp.concatenate([q_two, marks], axis=1))
                grad_probs = dot_nt(v_ref[keys, lanes(pair)], do_two)
                return q_two, do_two, scores, grad_probs

            now = products(0)
            for pair in range(PAIRS):
                later = products(pair + 1) if pair + 1 < PAIRS else None
                q_two, do_two, scores, grad_probs = now
                lse = jnp.concatenate(
                    [
                        lse_ref[2 * pair : 2 * pair + 1, queries],
                        lse_ref[2 * pair + 1 : 2 * pair + 2, queries],
                    ],
                    axis=1,
                )
                probs = jnp.exp2(scores - lse)
                both = probs * grad_probs
                delta = jnp.sum(both, axis=0, keepdims=True)
                grad_scores = (both - probs * delta).astype(bf16)
                dqt = dot(kt[lanes(pair), keys], grad_scores)
                dk_sum[keys, lanes(pair)] += dot(grad_scores, q_two)
                dv_sum[keys, lanes(pair)] += dot(probs.astype(bf16), do_two)
                dq = jnp.concatenate([dqt[0:64, 0:128], dqt[64:128, 128:256]], axis=0)
                dq_ref[queries, lanes(pair)] = (dq * HD ** (-0.5)).T.astype(bf16)
                now = later

        by_count(count, length // 128, run)
        return carry

    lax.fori_loop(0, q_ref.shape[0] // QB, block, 0)


def values_transposed(v_ref, vt):
    for pair in range(PAIRS):
        vt[pair, 0:128, :] = v_ref[:, lanes(pair)].T
        vt[pair, 128:144, :] = jnp.ones((16, vt.shape[2]), bf16)


def four(values):
    return jnp.concatenate([values] * 4, axis=1)


def rows_of(w, i):
    return w[i * D : (i + 1) * D, :]


def self_forward(source, scalars, x_ref, *rest):
    (q_ref, k_ref, v_ref, ot_ref, lse_ref, r_ref, w, vec, kx, vt, o, sems) = rest[
        source.count_all :
    ]
    place = Place(scalars)
    weights = source(rest)
    copies = weights.load(place, ROW_Q, w, sems.at[0])
    copies += weights.load_vectors(place, vec, sems.at[0])
    wait_all(copies)
    x = x_ref[...]
    k_ref[...] = dot(x, rows_of(w, 1)).astype(bf16)
    q_ref[...] = ((dot(x, rows_of(w, 0)) + vector(vec, "query_b")) * Q_SCALE).astype(bf16)
    v_ref[...] = (dot(x, rows_of(w, 2)) + vector(vec, "value_b")).astype(bf16)
    bounds = place.token_bounds
    marked_keys(k_ref, kx, bounds)
    values_transposed(v_ref, vt)
    attend(q_ref, kx, vt, ot_ref, o, lse_ref, bounds, bounds)
    r_ref[...] = x_ref[...].astype(f32) + dot(o[...], rows_of(w, 3)) + vector(vec, "out_b")


def cross_forward(source, scalars, r1_ref, m_ref, *rest):
    (q_ref, k_ref, v_ref, ot_ref, lse_ref, r_ref, w, vec, kx, vt, o, h, sems) = rest[
        source.count_all :
    ]
    place = Place(scalars)
    weights = source(rest)
    copies = weights.load(place, ROW_CQ, w, sems.at[0])
    wait_all(weights.load_vectors(place, vec, sems.at[1]))
    h[...] = normalize(r1_ref[...])[0] * vector(vec, "gain_one") + vector(vec, "shift_one")
    wait_all(copies)
    k_ref[...] = dot(m_ref[...], rows_of(w, 1)).astype(bf16)
    v_ref[...] = (dot(m_ref[...], rows_of(w, 2)) + vector(vec, "cross_value_b")).astype(bf16)
    q_ref[...] = (
        (dot(h[...].astype(bf16), rows_of(w, 0)) + vector(vec, "cross_query_b")) * Q_SCALE
    ).astype(bf16)
    marked_keys(k_ref, kx, place.memory_bounds)
    values_transposed(v_ref, vt)
    attend(q_ref, kx, vt, ot_ref, o, lse_ref, place.token_bounds, place.memory_bounds)
    r_ref[...] = h[...] + dot(o[...], rows_of(w, 3)) + vector(vec, "cross_out_b")


def gelu_parts(x):
    scale = math.sqrt(2.0 / math.pi)
    square = x * x
    tail = jnp.tanh(scale * x * (1.0 + 0.044715 * square))
    half = 0.5 * (1.0 + tail)
    slope = half + (0.5 * scale) * x * (1.0 - tail * tail) * (1.0 + (3 * 0.044715) * square)
    return x * half, slope


def same_next(first, rows, bounds, length):
    later = first + 1 + lax.broadcasted_iota(jnp.int32, (rows, 128), 0)
    same = later != length
    for bound in bounds:
        same = same & (later != bound)
    return same.astype(f32)


def ffn(source, make_sink, scalars, r2_ref, cot_ref, mask_ref, *rest):
    rest_ = rest[source.count_all :]
    slots_ref, gr2_ref = rest_[:2]
    count = make_sink.count
    sink = make_sink(rest_[2 : 2 + count])
    (w_in, w_out, w_slot, vec, spread, comb, act, slope, h3, gs, gs2, gr3, hlow, h2b, mask, gv_ref,
     sems) = rest_[2 + count :]
    place = Place(scalars)
    weights = source(rest)
    length = r2_ref.shape[0]
    tile = 256
    tiles = length // tile
    in_copies = weights.load(place, ROW_IN, w_out, sems.at[0])
    in_copies += weights.load(place, ROW_VEC, vec, sems.at[0])
    slot_copies = weights.load(place, ROW_SLOT, w_slot, sems.at[1])
    bounds = place.token_bounds
    row = mask_ref[...].astype(f32)
    mask[...] = jnp.broadcast_to(row, (128, length)).T
    spread[0:8, :] = jnp.zeros((8, D), f32)
    for t in range(tiles):
        rows = slice(t * tile, (t + 1) * tile)
        part = cot_ref[rows, :].astype(f32) * four(mask[rows, :])
        gs[rows, :] = part.astype(bf16)
        same = same_next(t * tile, tile, bounds, length)
        spread[8 + t * tile : 8 + (t + 1) * tile, :] = part * four(same)
    for t in range(tiles):
        rows = slice(t * tile, (t + 1) * tile)
        gs2[rows, :] = spread[7 + t * tile : 7 + (t + 1) * tile, :].astype(bf16)
    gv_ref[...] = jnp.zeros_like(gv_ref)

    def add_vector(name, value, at=0):
        at = VEC[name] + at
        gv_ref[at : at + 1, :] += value

    wait_all(in_copies)
    for i in range(4):
        comb[i] = w_out[:, lanes(i)].astype(f32)
        for c in range(4):
            w_in[c, :, lanes(i)] = comb[i, pl.ds(c, D, 4), :].astype(bf16)
    out_copies = weights.load(place, ROW_OUT, w_out, sems.at[0])

    def forward(t, carry):
        first = pl.multiple_of(t * tile, tile)
        rows = pl.ds(first, tile)
        h2 = normalize(r2_ref[rows, :])[0] * vector(vec, "gain_two") + vector(vec, "shift_two")
        low = h2.astype(bf16)
        h2b[rows, :] = low
        for c in range(4):
            bias = vec[VEC["inner_b"] + c : VEC["inner_b"] + c + 1, :].astype(f32)
            value, gate = gelu_parts(dot(low, w_in[c]) + bias)
            act[rows, c * D : (c + 1) * D] = value.astype(bf16)
            slope[rows, c * D : (c + 1) * D] = gate.astype(bf16)
        h3[rows, :] = h2 + dot(act[rows, :], w_out[...]) + vector(vec, "outer_b")
        return carry

    wait_all(out_copies)
    lax.fori_loop(0, tiles, forward, 0)
    wait_all(slot_copies)

    def third(t, carry):
        first = pl.multiple_of(t * tile, tile)
        rows = pl.ds(first, tile)
        normal, root = normalize(h3[rows, :])
        out = normal * vector(vec, "gain_three") + vector(vec, "shift_three")
        spread[rows, :] = out
        hlow[rows, :] = out.astype(bf16)
        grad = dot_nt(gs[rows, :], w_slot[0:D, :]) + dot_nt(gs2[rows, :], w_slot[D : 2 * D, :])
        add_vector("gain_three", column_sum(grad * normal))
        add_vector("shift_three", column_sum(grad))
        gr3[rows, :] = normalize_back(grad, normal, root, vector(vec, "gain_three"))
        return carry

    lax.fori_loop(0, tiles, third, 0)
    spread[length : length + 8, :] = jnp.zeros((8, D), f32)
    for t in range(tiles):
        rows = slice(t * tile, (t + 1) * tile)
        later = spread[t * tile + 1 : (t + 1) * tile + 1, :]
        same = four(same_next(t * tile, tile, bounds, length))
        following = (later * same).astype(bf16)
        raw = (
            dot(hlow[rows, :], w_slot[0:D, :])
            + dot(following, w_slot[D : 2 * D, :])
            + vector(vec, "slot_b")
        )
        slots_ref[rows, :] = (four(mask[rows, :]) * raw).astype(bf16)
    add_vector("slot_b", column_sum(gs[...]))
    put_grad(sink, place, ROW_SLOT, dot_tn(hlow[...], gs[...]))
    put_grad(sink, place, ROW_SLOT + D, dot_tn(hlow[...], gs2[...]))
    gs[...] = gr3[...].astype(bf16)
    add_vector("outer_b", column_sum(gs[...]))
    for c in range(4):
        put_grad(sink, place, ROW_OUT + c * D, dot_tn(act[:, c * D : (c + 1) * D], gs[...]))

    def backward(t, carry):
        first = pl.multiple_of(t * tile, tile)
        rows = pl.ds(first, tile)
        total = gr3[rows, :]
        for c in range(4):
            at = slice(c * D, (c + 1) * D)
            grad = dot_nt(gs[rows, :], w_out[at, :]).astype(bf16)
            pre = (grad.astype(f32) * slope[rows, at].astype(f32)).astype(bf16)
            slope[rows, at] = pre
            add_vector("inner_b", column_sum(pre), c)
            total = total + dot_nt(pre, w_in[c])
        normal, root = normalize(r2_ref[rows, :])
        add_vector("gain_two", column_sum(total * normal))
        add_vector("shift_two", column_sum(total))
        gr2_ref[rows, :] = normalize_back(total, normal, root, vector(vec, "gain_two"))
        return carry

    lax.fori_loop(0, tiles, backward, 0)
    for c in range(4):
        part = dot_tn(h2b[...], slope[:, c * D : (c + 1) * D])
        for i in range(4):
            comb[i, pl.ds(c, D, 4), :] = part[:, lanes(i)]
    put_grad(sink, place, ROW_VEC, gv_ref[...])
    put_grad(sink, place, ROW_IN, jnp.concatenate([comb[i] for i in range(4)], axis=1))


def attend_backward(source, which, row, scalars, gr_ref, q_ref, k_ref, v_ref, lse_ref, *rest):
    (dq, dk, dv, w, kx, kt, dk_sum, dv_sum, do, sems) = rest[source.count_all :]
    place = Place(scalars)
    copies = source(rest).load(place, row, w, sems.at[0])
    key_bounds = place.token_bounds if which == "self" else place.memory_bounds
    marked_keys(k_ref, kx, key_bounds)
    for pair in range(PAIRS):
        kt[lanes(pair), :] = k_ref[:, lanes(pair)].T
    wait_all(copies)
    do[...] = dot_nt(gr_ref[...].astype(bf16), w[...]).astype(bf16)
    attend_back(
        q_ref, kx, kt, v_ref, do, lse_ref, dq, dk_sum, dv_sum, place.token_bounds, key_bounds
    )
    dk[...] = (dk_sum[...] * (1.0 / LOG2E)).astype(bf16)
    dv[...] = dv_sum[...].astype(bf16)


def cross_backward(source, make_sink, scalars, gr2_ref, r1_ref, m_ref, dq, dk, dv, ot_ref, *rest):
    passed = rest[source.count_all : source.count_all + make_sink.passed]
    rest_ = rest[source.count_all + make_sink.passed :]
    mgrad_ref, gr1_ref, gv_ref = rest_[:3]
    count = make_sink.count
    sink = make_sink(rest_[3 : 3 + count])
    (w, vec, grad, h, sems) = rest_[3 + count :]
    place = Place(scalars)
    weights = source(rest)
    copies = weights.load(place, ROW_CQ, w, sems.at[0])
    copies += weights.load_vectors(place, vec, sems.at[0])
    make_sink.pass_on(sink, place, passed)
    gv_ref[...] = jnp.zeros_like(gv_ref)

    def set_vector(name, value):
        gv_ref[VEC[name] : VEC[name] + 1, :] = value

    grad[...] = gr2_ref[...].astype(bf16)
    put_grad(sink, place, ROW_CO, dot(ot_ref[...], grad[...]))
    set_vector("cross_out_b", column_sum(grad[...]))
    wait_all(copies)
    normal, root = normalize(r1_ref[...])
    gain = vector(vec, "gain_one")
    h[...] = (normal * gain + vector(vec, "shift_one")).astype(bf16)
    total = gr2_ref[...] + dot_nt(dq[...], rows_of(w, 0))
    set_vector("gain_one", column_sum(total * normal))
    set_vector("shift_one", column_sum(total))
    gr1_ref[...] = normalize_back(total, normal, root, gain)
    put_grad(sink, place, ROW_CQ, dot_tn(h[...], dq[...]))
    set_vector("cross_query_b", column_sum(dq[...]))
    put_grad(sink, place, ROW_CK, dot_tn(m_ref[...], dk[...]))
    put_grad(sink, place, ROW_CV, dot_tn(m_ref[...], dv[...]))
    set_vector("cross_value_b", column_sum(dv[...]))
    mgrad_ref[...] = (dot_nt(dk[...], rows_of(w, 1)) + dot_nt(dv[...], rows_of(w, 2))).astype(bf16)


def self_backward(source, make_sink, scalars, gr1_ref, x_ref, dq, dk, dv, ot_ref, gv_cross, *rest):
    passed = rest[source.count_all : source.count_all + make_sink.passed]
    rest_ = rest[source.count_all + make_sink.passed :]
    tgrad_ref = rest_[0]
    count = make_sink.count
    sink = make_sink(rest_[1 : 1 + count])
    (w, grad, gv, sems) = rest_[1 + count :]
    place = Place(scalars)
    copies = source(rest).load(place, ROW_Q, w, sems.at[0])
    make_sink.pass_on(sink, place, passed)
    gv[...] = gv_cross[...]

    def set_vector(name, value):
        gv[VEC[name] : VEC[name] + 1, :] = value

    grad[...] = gr1_ref[...].astype(bf16)
    put_grad(sink, place, ROW_O, dot(ot_ref[...], grad[...]))
    set_vector("out_b", column_sum(grad[...]))
    put_grad(sink, place, ROW_Q, dot_tn(x_ref[...], dq[...]))
    set_vector("query_b", column_sum(dq[...]))
    put_grad(sink, place, ROW_K, dot_tn(x_ref[...], dk[...]))
    put_grad(sink, place, ROW_V, dot_tn(x_ref[...], dv[...]))
    set_vector("value_b", column_sum(dv[...]))
    put_places(place, sink.vector_places(place), gv[...])
    wait_all(copies)
    tgrad_ref[...] = (
        gr1_ref[...]
        + dot_nt(dq[...], rows_of(w, 0))
        + dot_nt(dk[...], rows_of(w, 1))
        + dot_nt(dv[...], rows_of(w, 2))
    ).astype(bf16)


def find_bounds(segments_ref, lengths_ref, out_ref):
    segments = segments_ref[...]
    before = jnp.int32(0)
    for i in range(3):
        out_ref[i] = jnp.sum((segments <= i).astype(jnp.int32))
        before = before + lengths_ref[0, i]
        out_ref[3 + i] = before


PAD_ROWS = 304
VEC_AT = ROW_VEC - 31 * CORE_ROWS


def split_shard(slab_ref, keep_ref, send_ref, one_ref, two_ref, full):
    place = Place()
    rows = slab_ref.shape[0]
    full[0:rows, :] = slab_ref[...].astype(f32)
    full[rows : 4 * PAD_ROWS, :] = jnp.zeros((4 * PAD_ROWS - rows, 128), f32)
    for i in range(4):
        part = full[pl.ds(i, PAD_ROWS, 4), :].astype(bf16)
        few_ref = (one_ref, two_ref)[i // 2]
        for core in range(2):

            @pl.when(place.core == core)
            def _():
                (keep_ref if i // 2 == core else send_ref)[i % 2] = part
                first = core * VEC_AT
                few_ref[i % 2] = full[pl.ds(4 * first + i, 16, 4), :].astype(bf16)


def join_unit(keep_ref, got_ref, one_ref, two_ref, unit_ref, full):
    place = Place()
    for i in range(2):
        for core in range(2):

            @pl.when(place.core == core)
            def _():
                first, second = (keep_ref, got_ref) if core == 0 else (got_ref, keep_ref)
                full[0:PAD_ROWS, :] = first[i].astype(f32)
                full[CORE_ROWS : CORE_ROWS + PAD_ROWS, :] = second[i].astype(f32)

        ends = one_ref[i].astype(f32) + two_ref[i].astype(f32)
        full[CHIP_ROWS : CHIP_ROWS + 16, :] = ends

        @pl.when(place.y == 0)
        def _():
            unit_ref[i, 0] = full[0:UNIT, :].astype(bf16)

        @pl.when(place.y == 1)
        def _():
            unit_ref[i, 0, 0:576, :] = full[8:CHIP_ROWS, :].astype(bf16)
            unit_ref[i, 0, 576:UNIT, :] = ends.astype(bf16)


def split_unit(*refs):
    terms, (keep_ref, send_ref, ends_ref, full) = refs[:6], refs[6:]
    place = Place()
    for i in range(2):
        for group in range(3):
            chosen = place.z == group if group < 2 else place.z >= 2
            one, two = terms[2 * group], terms[2 * group + 1]
            for y in range(2):

                @pl.when(chosen & (place.y == y))
                def _():
                    total = one[i].astype(f32) + two[i].astype(f32)
                    full[8 * y : 8 * y + UNIT, :] = total

        ends_ref[i] = full[CHIP_ROWS : CHIP_ROWS + 16, :]
        for core in range(2):

            @pl.when(place.core == core)
            def _():
                keep_ref[i] = full[CORE_ROWS * core : CORE_ROWS * core + PAD_ROWS, :]
                send_ref[i] = full[CORE_ROWS * (1 - core) : CORE_ROWS * (1 - core) + PAD_ROWS, :]


def join_shard(keep_ref, got_ref, one_ref, two_ref, out_ref, full):
    place = Place()
    rows = out_ref.shape[0]
    for i in range(4):
        ends = (one_ref, two_ref)[i // 2]
        for core in range(2):

            @pl.when(place.core == core)
            def _():
                part = keep_ref if i // 2 == core else got_ref
                full[pl.ds(i, PAD_ROWS, 4), :] = part[i % 2]

        @pl.when((place.core == 0) & (place.y == 1))
        def _():
            full[pl.ds(i, 8, 4), :] = ends[i % 2, 0:8, :]

        @pl.when((place.core == 1) & (place.y == 1) & (place.x == 1) & (place.z == 3))
        def _():
            at = pl.ds(4 * VEC_AT + i, 16, 4)
            full[at, :] = full[at, :] + ends[i % 2]

    out_ref[...] = full[0:rows, :]


WHOLE = pl.BlockSpec(memory_space=pltpu.VMEM)


def call(body, name, scalars, blocks, weights, outs, scratch, flops, passed=(), after=()):
    used = 1 + len(blocks) + len(weights) + len(passed)

    def run(*refs):
        body(*refs[:used], *refs[used + len(after) :])

    return pl.pallas_call(
        run,
        name=name,
        out_shape=tuple(jax.ShapeDtypeStruct(s, t) for s, t in outs),
        in_specs=[pl.BlockSpec(memory_space=pltpu.SMEM)]
        + [WHOLE] * len(blocks)
        + [pl.BlockSpec(memory_space=pl.ANY)] * len(weights)
        + [WHOLE] * len(passed)
        + [pl.BlockSpec(memory_space=pl.ANY)] * len(after),
        out_specs=tuple(WHOLE for _ in outs),
        scratch_shapes=scratch,
        compiler_params=pltpu.CompilerParams(vmem_limit_bytes=VMEM_LIMIT),
        cost_estimate=pl.CostEstimate(flops=flops, bytes_accessed=8 << 20, transcendentals=0),
    )(scalars, *blocks, *weights, *passed, *after)


class Source:
    def __init__(self, kind, groups):
        self.kind = kind
        self.groups = groups
        self.count_all = kind.count * (len(groups) if kind is Units else 1)

    def __call__(self, refs):
        return self.kind(self.groups, refs)


class Sinks:
    def __init__(self, entries, first=None, taken=()):
        self.entries = entries
        self.first = first
        self.taken = taken
        self.count = 2 * len(entries)
        self.passed = 2 * len(taken)

    def outs(self):
        return [(shape, bf16) for _, shape in self.entries for _ in range(2)]

    def __call__(self, refs):
        pairs = [(refs[2 * i], refs[2 * i + 1]) for i in range(len(self.entries))]
        if self.first is not None:
            return RowSink(pairs[0], self.first)
        return UnitSink({key: pair for (key, _), pair in zip(self.entries, pairs)})

    def pass_on(self, sink, place, passed):
        for i, (unit, at, count) in enumerate(self.taken):
            far_x, far_y, low = place.turned(unit)
            for source, target in zip(passed[2 * i : 2 * i + 2], sink.refs[group_of(unit) + 100]):
                for quarter in range(2):
                    target[quarter, far_x + 2 * far_y, low, at : at + count, :] = source[
                        quarter, at : at + count, :
                    ]


class Layer:
    def __init__(self, tokens, memory, slot_cotangent, slot_mask, bounds, sources, weights, sinks):
        self.tokens, self.memory = tokens, memory
        self.slot_cotangent, self.slot_mask = slot_cotangent, slot_mask
        self.bounds, self.sources, self.weights, self.sinks = bounds, sources, weights, sinks
        self.act = tokens.shape
        self.keys = memory.shape[0]
        self.sems = [pltpu.SemaphoreType.DMA((2,))]

    def call(self, body, name, which, blocks, outs, scratch, flops, sink=None, **more):
        parts = [self.sources[which]] + ([sink] if sink is not None else [])
        return call(
            functools.partial(body, *parts), name, self.bounds, blocks, self.weights[which], outs,
            scratch + self.sems, flops, **more,
        )

    def attend_outs(self, keys):
        length = self.act[0]
        return [
            (self.act, bf16), ((keys, D), bf16), ((keys, D), bf16), ((D, length), bf16),
            ((HEADS, length), f32), (self.act, f32),
        ]

    def attend_scratch(self, keys):
        return [
            wide(4 * D, D), wide(16, D), wide(PAIRS, keys, 256), wide(PAIRS, 144, keys),
            wide(*self.act),
        ]

    def self_forward(self, after=()):
        self.q, self.k, self.v, self.ot, self.lse, self.r1 = self.call(
            self_forward, "self_forward", "self", [self.tokens], self.attend_outs(self.act[0]),
            self.attend_scratch(self.act[0]), 6_000_000_000, after=after,
        )

    def cross_forward(self, after=()):
        self.cq, self.mk, self.mv, self.cot, self.clse, self.r2 = self.call(
            cross_forward, "cross_forward", "cross", [self.r1, self.memory],
            self.attend_outs(self.keys), self.attend_scratch(self.keys) + [full(*self.act)],
            6_000_000_000, after=after,
        )

    def ffn(self, after=()):
        length, act, sink = self.act[0], self.act, self.sinks["ffn"]
        self.slots, self.gr2, *self.g_ffn = self.call(
            ffn, "ffn", "ffn", [self.r2, self.slot_cotangent, self.slot_mask],
            [(act, bf16), (act, f32)] + sink.outs(),
            [
                wide(4, D, D), wide(FF, D), wide(2 * D, D), wide(VEC_ROWS, D), full(length + 8, D),
                full(4, FF, 128), wide(length, FF), wide(length, FF), full(*act), wide(*act),
                wide(*act), full(*act), wide(*act), wide(*act), full(length, 128), full(128, D),
            ],
            18_000_000_000, sink, after=after,
        )

    def attend_backward(self, which, after=()):
        if which == "self":
            row, blocks, keys = ROW_O, [self.gr1, self.q, self.k, self.v, self.lse], self.act[0]
        else:
            row, blocks, keys = ROW_CO, [self.gr2, self.cq, self.mk, self.mv, self.clse], self.keys
        self.grads = call(
            functools.partial(attend_backward, self.sources[which], which, row),
            "attend_backward_" + which, self.bounds, blocks, self.weights[which],
            [(self.act, bf16), ((keys, D), bf16), ((keys, D), bf16)],
            [
                wide(D, D), wide(PAIRS, keys, 256), wide(D, keys), full(keys, D), full(keys, D),
                wide(*self.act),
            ] + self.sems,
            9_000_000_000, after=after,
        )

    def cross_backward(self, after=()):
        sink = self.sinks["cross"]
        self.memory_grad, self.gr1, self.gv, *self.g_cross = self.call(
            cross_backward, "cross_backward", "cross",
            [self.gr2, self.r1, self.memory, *self.grads, self.cot],
            [((self.keys, D), bf16), (self.act, f32), ((16, D), f32)] + sink.outs(),
            [wide(4 * D, D), wide(16, D), wide(*self.act), wide(*self.act)],
            4_000_000_000, sink, passed=self.g_ffn[: sink.passed], after=after,
        )

    def self_backward(self, after=()):
        sink = self.sinks["self"]
        self.tokens_grad, *self.g_self = self.call(
            self_backward, "self_backward", "self",
            [self.gr1, self.tokens, *self.grads, self.ot, self.gv],
            [(self.act, bf16)] + sink.outs(),
            [wide(4 * D, D), wide(*self.act), full(16, D)],
            4_000_000_000, sink, passed=self.g_cross[: sink.passed], after=after,
        )


def wide(*shape):
    return pltpu.VMEM(shape, bf16)


def full(*shape):
    return pltpu.VMEM(shape, f32)


def plain_layer(args, param_slabs):
    gathered = lax.all_gather(param_slabs, AXES, axis=0, tiled=True)
    total_rows = gathered.shape[0] // 4
    rows = gathered.reshape(total_rows, 4, 128)
    pieces = [rows[:, i, :] for i in range(4)]
    shapes = {"self": 2048 + 16, "cross": 2048, "ffn": 5120 + 128}
    firsts = {"self": 0, "cross": 2048, "ffn": 4096}
    sinks = {name: Sinks([(0, (2, shapes[name], 128))], firsts[name]) for name in shapes}
    source = Source(Pieces, ())
    run = Layer(*args, {n: source for n in shapes}, {n: pieces for n in shapes}, sinks)
    run.self_forward()
    run.cross_forward()
    run.ffn()
    run.attend_backward("cross")
    run.cross_backward()
    run.attend_backward("self")
    run.self_backward()
    send, keep = [
        jnp.concatenate([run.g_self[i][:, :2048], run.g_cross[i], run.g_ffn[i]], axis=1)
        .at[:, ROW_VEC : ROW_VEC + 16]
        .add(run.g_self[i][:, 2048:])
        for i in range(2)
    ]
    first = lax.axis_index("narrow") % 2 == 0
    low = jnp.where(first, keep, send)
    high = jnp.where(first, send, keep)
    flat = jnp.concatenate([low, high], axis=0).transpose(1, 0, 2)
    flat = jnp.pad(flat, ((0, total_rows - flat.shape[0]), (0, 0), (0, 0))).reshape(-1, 128)
    param_grad = lax.psum_scatter(flat, AXES, scatter_dimension=0, tiled=True).astype(f32)
    return run.slots, run.tokens_grad, run.memory_grad, param_grad


def moves(rule):
    number = lambda z, x, y, c: ((z * 2 + x) * 2 + y) * 2 + c
    pairs = []
    for z in range(4):
        for x in range(2):
            for y in range(2):
                for c in range(2):
                    target = rule(z, x, y, c)
                    if target is not None:
                        pairs.append((number(z, x, y, c), number(*target)))
    return pairs


OTHER_CORE = moves(lambda z, x, y, c: (z, x, y, 1 - c))
ALONG_X = moves(lambda z, x, y, c: (z, 1 - x, y, c))
ALONG_Y = moves(lambda z, x, y, c: (z, x, 1 - y, c))
ALONG_BOTH = moves(lambda z, x, y, c: (z, 1 - x, 1 - y, c))
ALONG_Z = moves(lambda z, x, y, c: (z ^ 1, x, y, c))
TWO_ALONG_Z = moves(lambda z, x, y, c: (z ^ 2, x, y, c))


def hops(table):
    return moves(lambda z, x, y, c: (table[z], x, y, c) if z in table else None)


def permute(value, pairs):
    return lax.ppermute(value, AXES, pairs)


def total(*values):
    return sum(value.astype(f32) for value in values).astype(bf16)


def spread_plane(own):
    mine = [own] + [permute(own, pairs) for pairs in (ALONG_X, ALONG_Y, ALONG_BOTH)]
    return mine + [permute(value, OTHER_CORE) for value in mine]


def sum_plane(send, keep, got):
    return [
        permute(total(keep[:, i], got[:, i]), pairs)
        for i, pairs in ((1, ALONG_X), (2, ALONG_Y), (3, ALONG_BOTH))
    ]


def here(keep, got, arrived):
    return total(keep[:, 0], got[:, 0], *arrived)


def chip_layer(args, param_slabs):
    z = lax.axis_index("wide") // 2
    shard_rows = param_slabs.shape[0]
    small = lambda *s: jax.ShapeDtypeStruct(s, bf16)
    real = lambda *s: jax.ShapeDtypeStruct(s, f32)
    keep, send, one, two = pl.pallas_call(
        split_shard, name="split_shard",
        out_shape=(small(2, PAD_ROWS, 128),) * 2 + (small(2, 16, 128),) * 2,
        in_specs=[WHOLE], out_specs=(WHOLE,) * 4, scratch_shapes=[full(4 * PAD_ROWS, 128)],
    )(param_slabs)
    got = permute(send, OTHER_CORE)

    def few(core):
        def rule(z, x, y, c):
            if (y, c) == (1, 0):
                return (z, x, 0, core)
            return (0, 1, 1, core) if (z, x, y, c) == (3, 1, 1, 1) else None

        return moves(rule)

    one, two = permute(one, few(0)), permute(two, few(1))
    (unit,) = pl.pallas_call(
        join_unit, name="join_unit", out_shape=(small(2, 1, UNIT, 128),),
        in_specs=[WHOLE] * 4, out_specs=(WHOLE,), scratch_shapes=[full(2 * PAD_ROWS, 128)],
    )(keep, got, one, two)

    far = permute(unit, TWO_ALONG_Z)
    low, high = jnp.where(z < 2, unit, far), jnp.where(z < 2, far, unit)
    near = permute(low, ALONG_Z)
    even = z % 2 == 0
    plane0, plane1 = jnp.where(even, low, near), jnp.where(even, near, low)
    group0 = spread_plane(plane0)
    plane23 = jnp.concatenate([high, permute(high, ALONG_Z)], axis=1)
    groups = [group0, spread_plane(plane1), spread_plane(plane23)]
    used = {"self": (0,), "cross": (0, 1), "ffn": (1, 2)}
    sources = {name: Source(Units, group) for name, group in used.items()}
    weights = {name: [v for g in group for v in groups[g]] for name, group in used.items()}
    one_unit = (2, UNIT, 128)
    sinks = {
        "ffn": Sinks([(7, one_unit), (102, (2, 4, 2, UNIT, 128))]),
        "cross": Sinks([(3, one_unit), (101, (2, 4, 1, UNIT, 128))], taken=[(7, 0, 576)]),
        "self": Sinks([(100, (2, 4, 1, UNIT, 128))], taken=[(3, 288, 288)]),
    }
    run = Layer(*args, sources, weights, sinks)
    run.self_forward()
    run.cross_forward()
    run.ffn()
    send23, keep23 = run.g_ffn[2:4]
    got23 = permute(send23, OTHER_CORE)
    run.attend_backward("cross")
    run.cross_backward(after=[got23])
    arrived23 = sum_plane(send23, keep23, got23)
    send1, keep1 = run.g_cross[2:4]
    got1 = permute(send1, OTHER_CORE)
    run.attend_backward("self")
    run.self_backward(after=[got1, *arrived23])
    arrived1 = sum_plane(send1, keep1, got1)
    here23 = here(keep23, got23, arrived23)
    send0, keep0 = run.g_self
    got0 = permute(send0, OTHER_CORE)
    arrived0 = sum_plane(send0, keep0, got0)
    mixed23 = total(here23[:, 0], permute(here23[:, 1], ALONG_Z))
    pairs = [mixed23, permute(mixed23, hops({0: 2, 1: 3}))]
    here1 = here(keep1, got1, arrived1)[:, 0]
    mixed1 = total(here1, permute(here1, hops({0: 1, 3: 2})))
    pairs = [mixed1, permute(mixed1, hops({2: 1}))] + pairs
    here0 = here(keep0, got0, arrived0)[:, 0]
    mixed0 = total(here0, permute(here0, hops({1: 0, 3: 2})))
    pairs = [mixed0, permute(mixed0, hops({2: 0}))] + pairs
    keep, send, ends = pl.pallas_call(
        split_unit, name="split_unit",
        out_shape=(real(2, PAD_ROWS, 128),) * 2 + (real(2, 16, 128),),
        in_specs=[WHOLE] * 6, out_specs=(WHOLE,) * 3, scratch_shapes=[full(2 * PAD_ROWS, 128)],
    )(*pairs)
    got = permute(send, OTHER_CORE)

    def last(core):
        def rule(z, x, y, c):
            if (y, c) == (0, core):
                return (z, x, 1, 0)
            return (3, 1, 1, 1) if (z, x, y, c) == (0, 1, 1, core) else None

        return moves(rule)

    (param_grad,) = pl.pallas_call(
        join_shard, name="join_shard", out_shape=(real(shard_rows, 128),),
        in_specs=[WHOLE] * 4, out_specs=(WHOLE,), scratch_shapes=[full(4 * PAD_ROWS, 128)],
    )(keep, got, permute(ends, last(0)), permute(ends, last(1)))
    return run.slots, run.tokens_grad, run.memory_grad, param_grad


def shards(mesh_shape, tokens, memory, slot_cotangent, param_slabs, segment_ids, memory_lengths,
           slot_mask):
    smem = pl.BlockSpec(memory_space=pltpu.SMEM)
    bounds = pl.pallas_call(
        find_bounds, name="find_bounds", out_shape=jax.ShapeDtypeStruct((8,), jnp.int32),
        in_specs=[WHOLE, smem], out_specs=smem,
    )(segment_ids, memory_lengths)
    chips = mesh_shape == (8, 4) and param_slabs.shape[0] == 4 * CORE_ROWS
    args = (tokens, memory, slot_cotangent, slot_mask, bounds)
    return (chip_layer if chips else plain_layer)(args, param_slabs)


def solution(mesh):
    spec = P(AXES, None)
    shape = tuple(mesh.shape[axis] for axis in AXES)
    return jax.shard_map(
        functools.partial(shards, shape),
        mesh=mesh,
        in_specs=(spec,) * 7,
        out_specs=(spec,) * 4,
        check_vma=False,
    )
```

```python
import functools
import math

import jax
import jax.numpy as jnp
from jax import lax
from jax.experimental import pallas as pl
from jax.experimental.pallas import tpu as pltpu
from jax.sharding import PartitionSpec as P

D = 512
HEADS = 8
HD = 64
FF = 2048
EPSILON = 1e-05
AXES = ("wide", "narrow")
QB = 128
PAIRS = HEADS // 2
BIG = -1e30
LOG2E = math.log2(math.e)
Q_SCALE = LOG2E * HD ** (-0.5)

f32 = jnp.float32
bf16 = jnp.bfloat16

ROW_Q, ROW_K, ROW_V, ROW_O = 0, 512, 1024, 1536
ROW_CQ, ROW_CK, ROW_CV, ROW_CO = 2048, 2560, 3072, 3584
ROW_IN, ROW_OUT, ROW_SLOT, ROW_VEC = 4096, 6144, 8192, 9216
VEC_ROWS = 32
VEC_NAMES = (
    "query_b", "value_b", "out_b", "cross_query_b", "cross_value_b", "cross_out_b", "gain_one",
    "shift_one", "gain_two", "shift_two", "gain_three", "shift_three", "outer_b", "slot_b", "inner_b",
)
VEC = {name: place for place, name in enumerate(VEC_NAMES)}

VMEM_LIMIT = 58 * 1024 * 1024


def dot(a, b):
    return jnp.dot(a, b, preferred_element_type=f32)


def dot_nt(a, b):
    return lax.dot_general(a, b, (((1,), (1,)), ((), ())), preferred_element_type=f32)


def dot_tn(a, b):
    return lax.dot_general(a, b, (((0,), (0,)), ((), ())), preferred_element_type=f32)


def column_sum(matrix):
    return jnp.sum(matrix.astype(f32), axis=0, keepdims=True)


def normalize(values):
    centered = values - jnp.mean(values, axis=-1, keepdims=True)
    root = lax.rsqrt(jnp.mean(centered * centered, axis=-1, keepdims=True) + EPSILON)
    return centered * root, root


def normalize_back(grad, normal, root, gain):
    scaled = grad * gain
    first = jnp.mean(scaled, axis=-1, keepdims=True)
    second = jnp.mean(scaled * normal, axis=-1, keepdims=True)
    return root * (scaled - first - normal * second)


CHIP_ROWS = 584
CORE_ROWS = 292
UNIT = 592
UNITS = 16


def unit_begin(unit):
    return 2 * CHIP_ROWS * (unit // 2) + UNIT * (unit % 2)


def unit_parts(begin, rows):
    parts = []
    for unit in range(UNITS):
        low = max(begin, unit_begin(unit))
        high = min(begin + rows, unit_begin(unit + 1))
        if low < high:
            parts.append((unit, low - unit_begin(unit), low - begin, high - low))
    return parts


def group_of(unit):
    return min(unit // 4, 2)


class Place:
    def __init__(self, bounds=None):
        if bounds is not None:
            self.token_bounds = [bounds[i] for i in range(3)]
            self.memory_bounds = [bounds[3 + i] for i in range(3)]
        wide, narrow = lax.axis_index("wide"), lax.axis_index("narrow")
        self.z, self.x = lax.div(wide, 2), lax.rem(wide, 2)
        self.y, self.core = lax.div(narrow, 2), lax.rem(narrow, 2)

    def turned(self, unit):
        z, x, y = unit // 4, unit // 2 % 2, unit % 2
        low = jnp.bitwise_xor(lax.rem(self.z, 2), z % 2) if group_of(unit) == 2 else 0
        return jnp.bitwise_xor(self.x, x), jnp.bitwise_xor(self.y, y), low


class Units:
    count = 8

    def __init__(self, groups, refs):
        self.groups = {
            group: (refs[8 * i : 8 * i + 4], refs[8 * i + 4 : 8 * i + 8])
            for i, group in enumerate(groups)
        }

    def load(self, place, begin, buffer, sem):
        return self.load_parts(place, unit_parts(begin, buffer.shape[0]), buffer, sem)

    def load_vectors(self, place, buffer, sem):
        return self.load_parts(place, [(3, UNIT - 16, 0, 16)], buffer, sem)

    def load_parts(self, place, parts, buffer, sem):
        copies = []
        for unit, source, target, rows in parts:
            halves = self.groups[group_of(unit)]
            far_x, far_y, low = place.turned(unit)
            targets = [
                [
                    buffer.at[
                        pl.ds(target, rows),
                        pl.ds(
                            pl.multiple_of(
                                (jnp.bitwise_xor(place.core, half) * 2 + quarter) * 128, 128
                            ),
                            128,
                        ),
                    ]
                    for quarter in range(2)
                ]
                for half in range(2)
            ]

            def part(half, which, quarter):
                return halves[half][which].at[low, quarter, pl.ds(source, rows), :]

            for which in range(4):

                @pl.when((far_x == which % 2) & (far_y == which // 2))
                def _():
                    for half in range(2):
                        for quarter in range(2):
                            pltpu.make_async_copy(
                                part(half, which, quarter), targets[half][quarter], sem
                            ).start()

            copies += [
                pltpu.make_async_copy(part(half, 0, quarter), targets[half][quarter], sem)
                for half in range(2)
                for quarter in range(2)
            ]
        return copies


class Pieces:
    count = 4

    def __init__(self, groups, refs):
        self.refs = refs[:4]

    def load(self, place, begin, buffer, sem):
        copies = []
        for i, ref in enumerate(self.refs):
            copy = pltpu.make_async_copy(
                ref.at[pl.ds(begin, buffer.shape[0]), :],
                buffer.at[:, i * 128 : (i + 1) * 128],
                sem,
            )
            copy.start()
            copies.append(copy)
        return copies

    def load_vectors(self, place, buffer, sem):
        return self.load(place, ROW_VEC, buffer, sem)


def wait_all(copies):
    for copy in copies:
        copy.wait()


def vector(vec_ref, name):
    return vec_ref[VEC[name] : VEC[name] + 1, :].astype(f32)


class UnitSink:
    def __init__(self, outs):
        self.outs = outs
        self.refs = {key: (send.ref, keep.ref) for key, (send, keep) in outs.items()}

    def places(self, place, begin, rows):
        for unit, at, source, count in unit_parts(begin, rows):
            if unit in self.refs:
                yield self.refs[unit], (), at, source, count
            elif group_of(unit) + 100 in self.refs:
                far_x, far_y, low = place.turned(unit)
                yield self.refs[group_of(unit) + 100], (far_x + 2 * far_y, low), at, source, count

    def send(self, place, units):
        for unit in units:
            far_x, far_y, low = place.turned(unit)
            for result in self.outs[group_of(unit) + 100]:
                result.send(far_x + 2 * far_y, low)

    def vector_places(self, place):
        far_x, far_y, low = place.turned(3)
        yield self.refs[100], (far_x + 2 * far_y, low), UNIT - 16, 0, 16


class RowSink:
    def __init__(self, outs, first):
        self.outs = outs
        self.refs = (outs[0].ref, outs[1].ref)
        self.first = first

    def send(self, place, units):
        pass


    def places(self, place, begin, rows):
        yield self.refs, (), begin - self.first, 0, rows

    def vector_places(self, place):
        yield self.refs, (), 2048, 0, 16


def put_grad(sink, place, begin, value):
    put_places(place, sink.places(place, begin, value.shape[0]), value)


def put_places(place, places, value):
    low = value.astype(bf16)
    for (send, keep), lead, at, source, count in places:
        for core in range(2):

            @pl.when(place.core == core)
            def _():
                for i in range(4):
                    ref = keep if i // 2 == core else send
                    ref[(*lead, i % 2, pl.ds(at, count), slice(None))] = low[
                        source : source + count, i * 128 : (i + 1) * 128
                    ]


def segment_of(position, bounds):
    return sum([(position >= bound).astype(jnp.int32) for bound in bounds])


def pick(index, choices):
    value = choices[-1]
    for place in range(len(choices) - 2, -1, -1):
        value = jnp.where(index == place, choices[place], value)
    return value


def key_range(first_query, query_bounds, key_bounds, length):
    low = segment_of(first_query, query_bounds)
    high = segment_of(first_query + (QB - 1), query_bounds)
    begin = pick(low, [0, *key_bounds]) // 128
    end = (pick(high, [*key_bounds, length]) + 127) // 128
    return begin * 128, end - begin


def query_marks(first_query, bounds):
    position = first_query + lax.broadcasted_iota(jnp.int32, (QB, 128), 0)
    lane = lax.broadcasted_iota(jnp.int32, (QB, 128), 1)
    hidden = (lane <= len(bounds)) & (lane != segment_of(position, bounds))
    return jnp.where(hidden, BIG, 0.0).astype(bf16)


def key_marks(length, bounds):
    position = lax.broadcasted_iota(jnp.int32, (length, 128), 0)
    lane = lax.broadcasted_iota(jnp.int32, (length, 128), 1)
    return jnp.where(lane == segment_of(position, bounds), 1.0, 0.0).astype(bf16)


def stack_heads(pair):
    lane = lax.broadcasted_iota(jnp.int32, pair.shape, 1)
    nothing = jnp.zeros_like(pair)
    return jnp.concatenate(
        [jnp.where(lane < HD, pair, nothing), jnp.where(lane >= HD, pair, nothing)], axis=0
    )


def by_count(count, most, body):
    for value in range(1, most + 1):

        @pl.when(count == value)
        def _():
            body(value)


def lanes(pair):
    return slice(pair * 128, (pair + 1) * 128)


def marked_keys(k_ref, kx, key_bounds):
    marks = key_marks(k_ref.shape[0], key_bounds)
    for pair in range(PAIRS):
        kx[pair, :, 0:128] = k_ref[:, lanes(pair)]
        kx[pair, :, 128:256] = marks


def attend(q_ref, kx, vt, ot_ref, o_ref, lse_ref, query_bounds, key_bounds):
    length = kx.shape[1]

    def block(index, carry):
        first = pl.multiple_of(index * QB, QB)
        begin, count = key_range(first, query_bounds, key_bounds, length)
        begin = pl.multiple_of(begin, 128)
        queries = pl.ds(first, QB)
        marks = query_marks(first, query_bounds)
        marks = jnp.concatenate([marks, marks], axis=0)

        def run(blocks):
            keys = pl.ds(begin, 128 * blocks)
            scores = []
            for pair in range(PAIRS):
                wide = jnp.concatenate([stack_heads(q_ref[queries, lanes(pair)]), marks], axis=1)
                scores.append(dot_nt(kx[pair, keys, :], wide))
            tops = []
            probs = []
            for pair in range(PAIRS):
                top = jnp.max(scores[pair], axis=0, keepdims=True)
                tops.append(top)
                probs.append(jnp.exp2(scores[pair] - top).astype(bf16))
            mixed = [dot(vt[pair, :, keys], probs[pair]) for pair in range(PAIRS)]
            for pair in range(PAIRS):
                total = mixed[pair][128:129, :]
                scale = 1.0 / total
                lse = tops[pair] + jnp.log2(total)
                one = mixed[pair][0:64, 0:128] * scale[:, 0:128]
                two = mixed[pair][64:128, 128:256] * scale[:, 128:256]
                out = jnp.concatenate([one, two], axis=0)
                ot_ref[lanes(pair), queries] = out.astype(bf16)
                o_ref[queries, lanes(pair)] = out.T.astype(bf16)
                lse_ref[2 * pair : 2 * pair + 1, queries] = lse[:, 0:128]
                lse_ref[2 * pair + 1 : 2 * pair + 2, queries] = lse[:, 128:256]

        by_count(count, length // 128, run)
        return carry

    lax.fori_loop(0, q_ref.shape[0] // QB, block, 0)


def attend_back(
    q_ref, kx, kt, v_ref, do_ref, lse_ref, dq_ref, dk_sum, dv_sum, query_bounds, key_bounds
):
    length = kx.shape[1]
    dk_sum[...] = jnp.zeros_like(dk_sum)
    dv_sum[...] = jnp.zeros_like(dv_sum)

    def block(index, carry):
        first = pl.multiple_of(index * QB, QB)
        begin, count = key_range(first, query_bounds, key_bounds, length)
        begin = pl.multiple_of(begin, 128)
        queries = pl.ds(first, QB)
        marks = query_marks(first, query_bounds)
        marks = jnp.concatenate([marks, marks], axis=0)

        def run(blocks):
            keys = pl.ds(begin, 128 * blocks)

            def products(pair):
                q_two = stack_heads(q_ref[queries, lanes(pair)])
                do_two = stack_heads(do_ref[queries, lanes(pair)])
                scores = dot_nt(kx[pair, keys, :], jnp.concatenate([q_two, marks], axis=1))
                grad_probs = dot_nt(v_ref[keys, lanes(pair)], do_two)
                return q_two, do_two, scores, grad_probs

            now = products(0)
            for pair in range(PAIRS):
                later = products(pair + 1) if pair + 1 < PAIRS else None
                q_two, do_two, scores, grad_probs = now
                lse = jnp.concatenate(
                    [
                        lse_ref[2 * pair : 2 * pair + 1, queries],
                        lse_ref[2 * pair + 1 : 2 * pair + 2, queries],
                    ],
                    axis=1,
                )
                probs = jnp.exp2(scores - lse)
                both = probs * grad_probs
                delta = jnp.sum(both, axis=0, keepdims=True)
                grad_scores = (both - probs * delta).astype(bf16)
                dqt = dot(kt[lanes(pair), keys], grad_scores)
                dk_sum[keys, lanes(pair)] += dot(grad_scores, q_two)
                dv_sum[keys, lanes(pair)] += dot(probs.astype(bf16), do_two)
                dq = jnp.concatenate([dqt[0:64, 0:128], dqt[64:128, 128:256]], axis=0)
                dq_ref[queries, lanes(pair)] = (dq * HD ** (-0.5)).T.astype(bf16)
                now = later

        by_count(count, length // 128, run)
        return carry

    lax.fori_loop(0, q_ref.shape[0] // QB, block, 0)


def values_transposed(v_ref, vt):
    for pair in range(PAIRS):
        vt[pair, 0:128, :] = v_ref[:, lanes(pair)].T
        vt[pair, 128:144, :] = jnp.ones((16, vt.shape[2]), bf16)


def four(values):
    return jnp.concatenate([values] * 4, axis=1)


def rows_of(w, i):
    return w[i * D : (i + 1) * D, :]


def add_out(r, x, o, w, bias):
    tile = 256
    for t in range(o.shape[0] // tile):
        rows = slice(t * tile, (t + 1) * tile)
        r.ref[rows, :] = x[rows, :].astype(f32) + dot(o[rows, :], w) + bias
        r.send(pl.ds(t * tile, tile))


def self_forward(source, scalars, x, *rest):
    (q, k, v, ot, lse, r, wq, wk, wv, wo, vec, kx, vt, o, sems) = rest[source.count_all :]
    place = Place(scalars)
    weights = source(rest)
    start(x)
    k_copies = weights.load(place, ROW_K, wk, sems.at[0])
    q_copies = weights.load(place, ROW_Q, wq, sems.at[1])
    q_copies += weights.load_vectors(place, vec, sems.at[1])
    v_copies = weights.load(place, ROW_V, wv, sems.at[2])
    x = x.get()
    wait_all(k_copies)
    k.ref[...] = dot(x[...], wk[...]).astype(bf16)
    k.send()
    wait_all(q_copies)
    q.ref[...] = ((dot(x[...], wq[...]) + vector(vec, "query_b")) * Q_SCALE).astype(bf16)
    q.send()
    wait_all(v_copies)
    v.ref[...] = (dot(x[...], wv[...]) + vector(vec, "value_b")).astype(bf16)
    v.send()
    o_copies = weights.load(place, ROW_O, wo, sems.at[0])
    bounds = place.token_bounds
    marked_keys(k.ref, kx, bounds)
    values_transposed(v.ref, vt)
    attend(q.ref, kx, vt, ot.ref, o, lse.ref, bounds, bounds)
    ot.send()
    wait_all(o_copies)
    add_out(r, x, o, wo[...], vector(vec, "out_b"))


def cross_forward(source, scalars, m, r1, *rest):
    (q, k, v, ot, lse, r, wq, wk, wv, wo, vec, kx, vt, o, h, sems) = rest[source.count_all :]
    place = Place(scalars)
    weights = source(rest)
    start(m)
    k_copies = weights.load(place, ROW_CK, wk, sems.at[0])
    v_copies = weights.load(place, ROW_CV, wv, sems.at[1])
    v_copies += weights.load_vectors(place, vec, sems.at[1])
    m = m.get()
    wait_all(k_copies)
    start(r1)
    q_copies = weights.load(place, ROW_CQ, wq, sems.at[2])
    k.ref[...] = dot(m[...], wk[...]).astype(bf16)
    k.send()
    wait_all(v_copies)
    v.ref[...] = (dot(m[...], wv[...]) + vector(vec, "cross_value_b")).astype(bf16)
    v.send()
    o_copies = weights.load(place, ROW_CO, wo, sems.at[0])
    r1 = r1.get()
    h[...] = normalize(r1[...])[0] * vector(vec, "gain_one") + vector(vec, "shift_one")
    wait_all(q_copies)
    q.ref[...] = (
        (dot(h[...].astype(bf16), wq[...]) + vector(vec, "cross_query_b")) * Q_SCALE
    ).astype(bf16)
    q.send()
    marked_keys(k.ref, kx, place.memory_bounds)
    values_transposed(v.ref, vt)
    attend(q.ref, kx, vt, ot.ref, o, lse.ref, place.token_bounds, place.memory_bounds)
    ot.send()
    wait_all(o_copies)
    add_out(r, h, o, wo[...], vector(vec, "cross_out_b"))


def gelu_parts(x):
    scale = math.sqrt(2.0 / math.pi)
    square = x * x
    tail = jnp.tanh(scale * x * (1.0 + 0.044715 * square))
    half = 0.5 * (1.0 + tail)
    slope = half + (0.5 * scale) * x * (1.0 - tail * tail) * (1.0 + (3 * 0.044715) * square)
    return x * half, slope


def same_next(first, rows, bounds, length):
    later = first + 1 + lax.broadcasted_iota(jnp.int32, (rows, 128), 0)
    same = later != length
    for bound in bounds:
        same = same & (later != bound)
    return same.astype(f32)


def ffn(source, make_sink, scalars, mask_in, cot_in, r2_in, *rest):
    rest_ = rest[source.count_all :]
    hlow_out, gr2 = rest_[:2]
    hlow, gr2_ref = hlow_out.ref, gr2.ref
    count = make_sink.count
    sink = make_sink(rest_[2 : 2 + count])
    (w_in, w_raw, w_out, w_slot, vec, spread, comb, act, slope, h3, gs, gs2, gr3, h2b, mask, gv_ref,
     sems) = rest_[2 + count :]
    place = Place(scalars)
    weights = source(rest)
    start(mask_in, cot_in)
    in_copies = weights.load(place, ROW_IN, w_raw, sems.at[0])
    in_copies += weights.load(place, ROW_VEC, vec, sems.at[0])
    bounds = place.token_bounds
    mask_ref = mask_in.get()
    cot_ref = cot_in.get()
    start(r2_in)
    out_copies = weights.load(place, ROW_OUT, w_out, sems.at[1])
    length = cot_ref.shape[0]
    tile = 256
    tiles = length // tile
    row = mask_ref[...].astype(f32)
    mask[...] = jnp.broadcast_to(row, (128, length)).T
    spread[0:8, :] = jnp.zeros((8, D), f32)
    for t in range(tiles):
        rows = slice(t * tile, (t + 1) * tile)
        part = cot_ref[rows, :].astype(f32) * four(mask[rows, :])
        gs[rows, :] = part.astype(bf16)
        same = same_next(t * tile, tile, bounds, length)
        spread[8 + t * tile : 8 + (t + 1) * tile, :] = part * four(same)
    for t in range(tiles):
        rows = slice(t * tile, (t + 1) * tile)
        gs2[rows, :] = spread[7 + t * tile : 7 + (t + 1) * tile, :].astype(bf16)
    gv_ref[...] = jnp.zeros_like(gv_ref)

    def add_vector(name, value, at=0):
        at = VEC[name] + at
        gv_ref[at : at + 1, :] += value

    wait_all(in_copies)
    for i in range(4):
        comb[i] = w_raw[:, lanes(i)].astype(f32)
        for c in range(4):
            w_in[c, :, lanes(i)] = comb[i, pl.ds(c, D, 4), :].astype(bf16)
    r2_ref = r2_in.get()

    slot_copies = weights.load(place, ROW_SLOT, w_slot, sems.at[2])
    gain_two, shift_two = vector(vec, "gain_two"), vector(vec, "shift_two")
    biases = [vec[VEC["inner_b"] + c : VEC["inner_b"] + c + 1, :].astype(f32) for c in range(4)]

    def inner(t, c):
        rows = slice(t * tile, (t + 1) * tile)
        if c == 0:
            h2 = normalize(r2_ref[rows, :])[0] * gain_two + shift_two
            h3[rows, :] = h2
            h2b[rows, :] = h2.astype(bf16)
        return dot(h2b[rows, :], w_in[c]) + biases[c]

    steps = [(t, c) for t in range(tiles) for c in range(4)]
    ahead = inner(*steps[0])
    wait_all(out_copies)
    for place_in, (t, c) in enumerate(steps):
        pre = ahead
        if place_in + 1 < len(steps):
            ahead = inner(*steps[place_in + 1])
        rows = slice(t * tile, (t + 1) * tile)
        value, gate = gelu_parts(pre)
        act[rows, c * D : (c + 1) * D] = value.astype(bf16)
        slope[rows, c * D : (c + 1) * D] = gate.astype(bf16)
        if c == 3:
            h3[rows, :] = h3[rows, :] + dot(act[rows, :], w_out[...]) + vector(vec, "outer_b")
    wait_all(slot_copies)

    def third(t, carry):
        first = pl.multiple_of(t * tile, tile)
        rows = pl.ds(first, tile)
        normal, root = normalize(h3[rows, :])
        out = normal * vector(vec, "gain_three") + vector(vec, "shift_three")
        hlow[rows, :] = out.astype(bf16)
        grad = dot_nt(gs[rows, :], w_slot[0:D, :]) + dot_nt(gs2[rows, :], w_slot[D : 2 * D, :])
        add_vector("gain_three", column_sum(grad * normal))
        add_vector("shift_three", column_sum(grad))
        gr3[rows, :] = normalize_back(grad, normal, root, vector(vec, "gain_three"))
        return carry

    lax.fori_loop(0, tiles, third, 0)
    hlow_out.send()
    add_vector("slot_b", column_sum(gs[...]))
    put_grad(sink, place, ROW_SLOT, dot_tn(hlow[...], gs[...]))
    put_grad(sink, place, ROW_SLOT + D, dot_tn(hlow[...], gs2[...]))
    gs[...] = gr3[...].astype(bf16)
    add_vector("outer_b", column_sum(gs[...]))
    for c in range(4):
        put_grad(sink, place, ROW_OUT + c * D, dot_tn(act[:, c * D : (c + 1) * D], gs[...]))
    sink.send(place, range(11, 15))

    def backward(t, carry):
        first = pl.multiple_of(t * tile, tile)
        rows = pl.ds(first, tile)
        total = gr3[rows, :]
        for c in range(4):
            at = slice(c * D, (c + 1) * D)
            grad = dot_nt(gs[rows, :], w_out[at, :]).astype(bf16)
            pre = (grad.astype(f32) * slope[rows, at].astype(f32)).astype(bf16)
            slope[rows, at] = pre
            add_vector("inner_b", column_sum(pre), c)
            total = total + dot_nt(pre, w_in[c])
        normal, root = normalize(r2_ref[rows, :])
        add_vector("gain_two", column_sum(total * normal))
        add_vector("shift_two", column_sum(total))
        gr2_ref[rows, :] = normalize_back(total, normal, root, vector(vec, "gain_two"))
        return carry

    lax.fori_loop(0, tiles, backward, 0)
    gr2.send()
    put_grad(sink, place, ROW_VEC, gv_ref[...])
    sink.send(place, [15])
    for c in range(4):
        part = dot_tn(h2b[...], slope[:, c * D : (c + 1) * D])
        for i in range(4):
            comb[i, pl.ds(c, D, 4), :] = part[:, lanes(i)]
    put_grad(sink, place, ROW_IN, jnp.concatenate([comb[i] for i in range(4)], axis=1))
    sink.send(place, range(8, 11))


def slot_forward(source, scalars, mask_in, hlow_in, *rest):
    (slots, w, vec, spread, mask, sems) = rest[source.count_all :]
    place = Place(scalars)
    weights = source(rest)
    copies = weights.load(place, ROW_SLOT, w, sems.at[0])
    copies += weights.load(place, ROW_VEC, vec, sems.at[0])
    start(mask_in, hlow_in)
    hlow = hlow_in.get()
    length = hlow.shape[0]
    tile = 256
    mask[...] = jnp.broadcast_to(mask_in.get()[...].astype(f32), (128, length)).T
    spread[0:length, :] = hlow[...].astype(f32)
    spread[length : length + 8, :] = jnp.zeros((8, D), f32)
    wait_all(copies)
    for t in range(length // tile):
        rows = slice(t * tile, (t + 1) * tile)
        later = spread[t * tile + 1 : (t + 1) * tile + 1, :]
        same = four(same_next(t * tile, tile, place.token_bounds, length))
        raw = (
            dot(hlow[rows, :], w[0:D, :])
            + dot((later * same).astype(bf16), w[D : 2 * D, :])
            + vector(vec, "slot_b")
        )
        slots.ref[rows, :] = (four(mask[rows, :]) * raw).astype(bf16)
        slots.send(pl.ds(t * tile, tile))


def attend_backward(place, key_bounds, w, gr_low, v_in, q_in, lse_in, dq, dk, dv, scratch,
                    later):
    (kx, kt, dk_sum, dv_sum, do) = scratch
    do[...] = dot_nt(gr_low[...], w).astype(bf16)
    v_ref, q_ref, lse_ref = v_in.get(), q_in.get(), lse_in.get()
    start(*later)
    attend_back(
        q_ref, kx, kt, v_ref, do, lse_ref, dq.ref, dk_sum, dv_sum, place.token_bounds, key_bounds
    )
    dk.ref[...] = (dk_sum[...] * (1.0 / LOG2E)).astype(bf16)
    dv.ref[...] = dv_sum[...].astype(bf16)
    for out in (dq, dk, dv):
        if isinstance(out, Out):
            out.send()


def keys_ready(place, key_bounds, k_in, kx, kt):
    k_ref = k_in.get()
    marked_keys(k_ref, kx, key_bounds)
    for pair in range(PAIRS):
        kt[lanes(pair), :] = k_ref[:, lanes(pair)].T


class Held:
    def __init__(self, ref):
        self.ref = ref


def cross_backward(source, make_sink, scalars, k_in, gr2_in, v_in, q_in, lse_in, ot_in, r1_in, m_in,
                   *rest):
    passed = rest[source.count_all : source.count_all + make_sink.passed]
    rest_ = rest[source.count_all + make_sink.passed :]
    dk, dv, gr1, gv = rest_[:4]
    count = make_sink.count
    sink = make_sink(rest_[4 : 4 + count])
    (wq, wo, vec, grad, h, dq, *scratch, sems) = rest_[4 + count :]
    place = Place(scalars)
    weights = source(rest)
    start(k_in, gr2_in)
    o_copies = weights.load(place, ROW_CO, wo, sems.at[0])
    keys_ready(place, place.memory_bounds, k_in, *scratch[:2])
    start(v_in, q_in, lse_in)
    q_copies = weights.load(place, ROW_CQ, wq, sems.at[1])
    q_copies += weights.load_vectors(place, vec, sems.at[1])
    gv.ref[...] = jnp.zeros_like(gv.ref)

    def set_vector(name, value):
        gv.ref[VEC[name] : VEC[name] + 1, :] = value

    gr2_ref = gr2_in.get()
    grad[...] = gr2_ref[...].astype(bf16)
    wait_all(o_copies)
    attend_backward(
        place, place.memory_bounds, wo[...], grad, v_in, q_in, lse_in, Held(dq), dk, dv, scratch,
        [r1_in, ot_in, m_in, *passed],
    )
    set_vector("cross_out_b", column_sum(grad[...]))
    ot_ref, r1_ref = ot_in.get(), r1_in.get()
    wait_all(q_copies)
    normal, root = normalize(r1_ref[...])
    gain = vector(vec, "gain_one")
    h[...] = (normal * gain + vector(vec, "shift_one")).astype(bf16)
    total = gr2_ref[...] + dot_nt(dq[...], wq[...])
    set_vector("gain_one", column_sum(total * normal))
    set_vector("shift_one", column_sum(total))
    gr1.ref[...] = normalize_back(total, normal, root, gain)
    gr1.send()
    make_sink.pass_on(sink, place, passed)
    m_ref = m_in.get()
    put_grad(sink, place, ROW_CO, dot(ot_ref[...], grad[...]))
    put_grad(sink, place, ROW_CV, dot_tn(m_ref[...], dv.ref[...]))
    sink.send(place, [6, 7])
    set_vector("cross_value_b", column_sum(dv.ref[...]))
    put_grad(sink, place, ROW_CK, dot_tn(m_ref[...], dk.ref[...]))
    sink.send(place, [5])
    put_grad(sink, place, ROW_CQ, dot_tn(h[...], dq[...]))
    sink.send(place, [4])
    set_vector("cross_query_b", column_sum(dq[...]))


def memory_gradient(source, scalars, dk_in, dv_in, *rest):
    (mgrad, w, sems) = rest[source.count_all :]
    copies = source(rest).load(Place(), ROW_CK, w, sems.at[0])
    start(dk_in, dv_in)
    dk, dv = dk_in.get(), dv_in.get()
    wait_all(copies)
    tile = 256
    for t in range(dk.shape[0] // tile):
        rows = slice(t * tile, (t + 1) * tile)
        value = dot_nt(dk[rows, :], rows_of(w, 0)) + dot_nt(dv[rows, :], rows_of(w, 1))
        mgrad.ref[rows, :] = value.astype(bf16)
        mgrad.send(pl.ds(t * tile, tile))


def self_backward(source, make_sink, scalars, k_in, gr1_in, v_in, q_in, lse_in, ot_in, x_in, gv_in,
                  *rest):
    passed = rest[source.count_all : source.count_all + make_sink.passed]
    rest_ = rest[source.count_all + make_sink.passed :]
    dq, dk, dv = rest_[:3]
    count = make_sink.count
    sink = make_sink(rest_[3 : 3 + count])
    (w, grad, gv, *scratch, sems) = rest_[3 + count :]
    place = Place(scalars)
    start(k_in, gr1_in)
    copies = source(rest).load(place, ROW_O, w, sems.at[0])
    keys_ready(place, place.token_bounds, k_in, *scratch[:2])
    start(v_in, q_in, lse_in)
    gr1_ref = gr1_in.get()
    grad[...] = gr1_ref[...].astype(bf16)
    wait_all(copies)
    attend_backward(
        place, place.token_bounds, w[...], grad, v_in, q_in, lse_in, dq, dk, dv, scratch,
        [ot_in, x_in, gv_in, *passed],
    )
    ot_ref, x_ref = ot_in.get(), x_in.get()
    gv[...] = gv_in.get()[...]

    def set_vector(name, value):
        gv[VEC[name] : VEC[name] + 1, :] = value

    make_sink.pass_on(sink, place, passed)
    put_grad(sink, place, ROW_O, dot(ot_ref[...], grad[...]))
    set_vector("out_b", column_sum(grad[...]))
    put_grad(sink, place, ROW_V, dot_tn(x_ref[...], dv.ref[...]))
    sink.send(place, [2])
    set_vector("value_b", column_sum(dv.ref[...]))
    set_vector("query_b", column_sum(dq.ref[...]))
    put_places(place, sink.vector_places(place), gv[...])
    sink.send(place, [3])
    put_grad(sink, place, ROW_K, dot_tn(x_ref[...], dk.ref[...]))
    sink.send(place, [1])
    put_grad(sink, place, ROW_Q, dot_tn(x_ref[...], dq.ref[...]))
    sink.send(place, [0])


def token_gradient(source, scalars, dq_in, dk_in, dv_in, gr1_in, *rest):
    (tgrad, w, sems) = rest[source.count_all :]
    copies = source(rest).load(Place(), ROW_Q, w, sems.at[0])
    start(dq_in, dk_in, dv_in, gr1_in)
    dq, dk, dv, gr1_ref = dq_in.get(), dk_in.get(), dv_in.get(), gr1_in.get()
    wait_all(copies)
    tile = 256
    for t in range(dq.shape[0] // tile):
        rows = slice(t * tile, (t + 1) * tile)
        tgrad.ref[rows, :] = (
            gr1_ref[rows, :]
            + dot_nt(dq[rows, :], rows_of(w, 0))
            + dot_nt(dk[rows, :], rows_of(w, 1))
            + dot_nt(dv[rows, :], rows_of(w, 2))
        ).astype(bf16)
        tgrad.send(pl.ds(t * tile, tile))


def find_bounds(segments_ref, lengths_ref, out_ref):
    segments = segments_ref[...]
    before = jnp.int32(0)
    for i in range(3):
        out_ref[i] = jnp.sum((segments <= i).astype(jnp.int32))
        before = before + lengths_ref[0, i]
        out_ref[3 + i] = before


PAD_ROWS = 304
VEC_AT = ROW_VEC - 31 * CORE_ROWS


def split_shard(slab_ref, keep_ref, send_ref, one_ref, two_ref, full):
    place = Place()
    rows = slab_ref.shape[0]
    full[0:rows, :] = slab_ref[...].astype(f32)
    full[rows : 4 * PAD_ROWS, :] = jnp.zeros((4 * PAD_ROWS - rows, 128), f32)
    for i in range(4):
        part = full[pl.ds(i, PAD_ROWS, 4), :].astype(bf16)
        few_ref = (one_ref, two_ref)[i // 2]
        for core in range(2):

            @pl.when(place.core == core)
            def _():
                (keep_ref if i // 2 == core else send_ref)[i % 2] = part
                first = core * VEC_AT
                few_ref[i % 2] = full[pl.ds(4 * first + i, 16, 4), :].astype(bf16)


def join_unit(keep_ref, got_ref, one_ref, two_ref, unit_ref, full):
    place = Place()
    for i in range(2):
        for core in range(2):

            @pl.when(place.core == core)
            def _():
                first, second = (keep_ref, got_ref) if core == 0 else (got_ref, keep_ref)
                full[0:PAD_ROWS, :] = first[i].astype(f32)
                full[CORE_ROWS : CORE_ROWS + PAD_ROWS, :] = second[i].astype(f32)

        ends = one_ref[i].astype(f32) + two_ref[i].astype(f32)
        full[CHIP_ROWS : CHIP_ROWS + 16, :] = ends

        @pl.when(place.y == 0)
        def _():
            unit_ref[0, i] = full[0:UNIT, :].astype(bf16)

        @pl.when(place.y == 1)
        def _():
            unit_ref[0, i, 0:576, :] = full[8:CHIP_ROWS, :].astype(bf16)
            unit_ref[0, i, 576:UNIT, :] = ends.astype(bf16)


def split_unit(*refs):
    terms, (keep_ref, send_ref, ends_ref, full) = refs[:6], refs[6:]
    place = Place()
    for i in range(2):
        for group in range(3):
            chosen = place.z == group if group < 2 else place.z >= 2
            one, two = terms[2 * group], terms[2 * group + 1]
            for y in range(2):

                @pl.when(chosen & (place.y == y))
                def _():
                    total = one[i].astype(f32) + two[i].astype(f32)
                    full[8 * y : 8 * y + UNIT, :] = total

        ends_ref[i] = full[CHIP_ROWS : CHIP_ROWS + 16, :]
        for core in range(2):

            @pl.when(place.core == core)
            def _():
                keep_ref[i] = full[CORE_ROWS * core : CORE_ROWS * core + PAD_ROWS, :]
                send_ref[i] = full[CORE_ROWS * (1 - core) : CORE_ROWS * (1 - core) + PAD_ROWS, :]


def join_shard(keep_ref, got_ref, one_ref, two_ref, out_ref, full):
    place = Place()
    rows = out_ref.shape[0]
    for i in range(4):
        ends = (one_ref, two_ref)[i // 2]
        for core in range(2):

            @pl.when(place.core == core)
            def _():
                part = keep_ref if i // 2 == core else got_ref
                full[pl.ds(i, PAD_ROWS, 4), :] = part[i % 2]

        @pl.when((place.core == 0) & (place.y == 1))
        def _():
            full[pl.ds(i, 8, 4), :] = ends[i % 2, 0:8, :]

        @pl.when((place.core == 1) & (place.y == 1) & (place.x == 1) & (place.z == 3))
        def _():
            at = pl.ds(4 * VEC_AT + i, 16, 4)
            full[at, :] = full[at, :] + ends[i % 2]

    out_ref[...] = full[0:rows, :]


WHOLE = pl.BlockSpec(memory_space=pltpu.VMEM)


class In:
    def __init__(self, source, buffer, sem):
        self.buffer = buffer
        self.copy = pltpu.make_async_copy(source, buffer, sem)
        self.started = False

    def start(self):
        self.copy.start()
        self.started = True

    def get(self):
        if not self.started:
            self.start()
        self.copy.wait()
        return self.buffer


def start(*arrays):
    for array in arrays:
        array.start()


class Out:
    def __init__(self, target, ref, sem):
        self.target, self.ref, self.sem = target, ref, sem
        self.copies = []

    def send(self, *index):
        source, target = (self.ref.at[index], self.target.at[index]) if index else (self.ref, self.target)
        copy = pltpu.make_async_copy(source, target, self.sem)
        copy.start()
        self.copies.append(copy)

    def finish(self):
        if not self.copies:
            self.send()
        wait_all(self.copies)


def call(body, name, scalars, blocks, weights, outs, scratch, microseconds, passed=(), after=()):
    ins = [*blocks, *passed]
    buffers = [pltpu.VMEM(v.shape, v.dtype) for v in ins] + [pltpu.VMEM(s, t) for s, t in outs]
    sems = [pltpu.SemaphoreType.DMA((len(ins),)), pltpu.SemaphoreType.DMA((len(outs),))]

    def run(*refs):
        refs = list(refs)
        take = lambda n: [refs.pop(0) for _ in range(n)]
        scalars_ref, *in_refs = take(1 + len(ins))
        weight_refs, _, out_refs = take(len(weights)), take(len(after)), take(len(outs))
        in_buffers, out_buffers = take(len(ins)), take(len(outs))
        in_sems, out_sems = take(2)
        arrays = [In(in_refs[i], in_buffers[i], in_sems.at[i]) for i in range(len(ins))]
        results = [Out(out_refs[i], out_buffers[i], out_sems.at[i]) for i in range(len(outs))]
        body(
            scalars_ref, *arrays[: len(blocks)], *weight_refs, *arrays[len(blocks) :], *results, *refs
        )
        for result in results:
            result.finish()

    anywhere = pl.BlockSpec(memory_space=pl.ANY)
    return pl.pallas_call(
        run,
        name=name,
        out_shape=tuple(jax.ShapeDtypeStruct(s, t) for s, t in outs),
        in_specs=[pl.BlockSpec(memory_space=pltpu.SMEM)]
        + [anywhere] * (len(ins) + len(weights) + len(after)),
        out_specs=(anywhere,) * len(outs),
        scratch_shapes=buffers + sems + scratch,
        compiler_params=pltpu.CompilerParams(vmem_limit_bytes=VMEM_LIMIT),
        cost_estimate=pl.CostEstimate(
            flops=microseconds * 1_150_000_000,
            bytes_accessed=microseconds * 3_690_000,
            transcendentals=0,
        ),
    )(scalars, *ins, *weights, *after)


class Source:
    def __init__(self, kind, groups):
        self.kind = kind
        self.groups = groups
        self.count_all = kind.count * (len(groups) if kind is Units else 1)

    def __call__(self, refs):
        return self.kind(self.groups, refs)


class Sinks:
    def __init__(self, entries, first=None, taken=()):
        self.entries = entries
        self.first = first
        self.taken = taken
        self.count = 2 * len(entries)
        self.passed = 2 * len(taken)

    def outs(self):
        return [(shape, bf16) for _, shape in self.entries for _ in range(2)]

    def __call__(self, refs):
        pairs = [(refs[2 * i], refs[2 * i + 1]) for i in range(len(self.entries))]
        if self.first is not None:
            return RowSink(pairs[0], self.first)
        return UnitSink({key: pair for (key, _), pair in zip(self.entries, pairs)})

    def pass_on(self, sink, place, passed):
        for i, (unit, at, count) in enumerate(self.taken):
            far_x, far_y, low = place.turned(unit)
            arrays = [array.get() for array in passed[2 * i : 2 * i + 2]]
            for source, target in zip(arrays, sink.refs[group_of(unit) + 100]):
                for quarter in range(2):
                    target[far_x + 2 * far_y, low, quarter, at : at + count, :] = source[
                        quarter, at : at + count, :
                    ]


class Layer:
    def __init__(self, tokens, memory, slot_cotangent, slot_mask, bounds, sources, weights, sinks):
        self.tokens, self.memory = tokens, memory
        self.slot_cotangent, self.slot_mask = slot_cotangent, slot_mask
        self.bounds, self.sources, self.weights, self.sinks = bounds, sources, weights, sinks
        self.act = tokens.shape
        self.keys = memory.shape[0]
        self.sems = [pltpu.SemaphoreType.DMA((3,))]

    def call(self, body, name, which, blocks, outs, scratch, microseconds, sink=None, **more):
        parts = [self.sources[which]] + ([sink] if sink is not None else [])
        return call(
            functools.partial(body, *parts), name, self.bounds, blocks, self.weights[which], outs,
            scratch + self.sems, microseconds, **more,
        )

    def attend_outs(self, keys):
        length = self.act[0]
        return [
            (self.act, bf16), ((keys, D), bf16), ((keys, D), bf16), ((D, length), bf16),
            ((HEADS, length), f32), (self.act, f32),
        ]

    def attend_scratch(self, keys):
        return [
            wide(D, D), wide(D, D), wide(D, D), wide(D, D), wide(16, D), wide(PAIRS, keys, 256),
            wide(PAIRS, 144, keys),
            wide(*self.act),
        ]

    def self_forward(self, after=()):
        self.q, self.k, self.v, self.ot, self.lse, self.r1 = self.call(
            self_forward, "self_forward", "self", [self.tokens], self.attend_outs(self.act[0]),
            self.attend_scratch(self.act[0]), 18, after=after,
        )

    def cross_forward(self, after=()):
        self.cq, self.mk, self.mv, self.cot, self.clse, self.r2 = self.call(
            cross_forward, "cross_forward", "cross", [self.memory, self.r1],
            self.attend_outs(self.keys), self.attend_scratch(self.keys) + [full(*self.act)],
            19, after=after,
        )

    def ffn(self, after=()):
        length, act, sink = self.act[0], self.act, self.sinks["ffn"]
        self.hlow, self.gr2, *self.g_ffn = self.call(
            ffn, "ffn", "ffn", [self.slot_mask, self.slot_cotangent, self.r2],
            [(act, bf16), (act, f32)] + sink.outs(),
            [
                wide(4, D, D), wide(FF, D), wide(FF, D), wide(2 * D, D), wide(VEC_ROWS, D),
                full(length + 8, D),
                full(4, FF, 128), wide(length, FF), wide(length, FF), full(*act), wide(*act),
                wide(*act), full(*act), wide(*act), full(length, 128), full(128, D),
            ],
            34, sink, after=after,
        )

    def slot_forward(self, after=()):
        length = self.act[0]
        (self.slots,) = self.call(
            slot_forward, "slot_forward", "ffn", [self.slot_mask, self.hlow], [(self.act, bf16)],
            [wide(2 * D, D), wide(VEC_ROWS, D), full(length + 8, D), full(length, 128)], 6,
            after=after,
        )

    def back_scratch(self, keys):
        return [
            wide(PAIRS, keys, 256), wide(D, keys), full(keys, D), full(keys, D), wide(*self.act)
        ]

    def cross_backward(self, after=()):
        sink = self.sinks["cross"]
        self.mdk, self.mdv, self.gr1, self.gv, *self.g_cross = self.call(
            cross_backward, "cross_backward", "cross",
            [self.mk, self.gr2, self.mv, self.cq, self.clse, self.cot, self.r1, self.memory],
            [((self.keys, D), bf16)] * 2 + [(self.act, f32), ((16, D), f32)] + sink.outs(),
            [wide(D, D), wide(D, D), wide(16, D)] + [wide(*self.act)] * 3
            + self.back_scratch(self.keys),
            28, sink, passed=self.g_ffn[: sink.passed], after=after,
        )

    def self_backward(self, after=()):
        sink = self.sinks["self"]
        length = self.act[0]
        self.dq, self.dk, self.dv, *self.g_self = self.call(
            self_backward, "self_backward", "self",
            [self.k, self.gr1, self.v, self.q, self.lse, self.ot, self.tokens, self.gv],
            [(self.act, bf16)] * 3 + sink.outs(),
            [wide(D, D), wide(*self.act), full(16, D)] + self.back_scratch(length),
            26, sink, passed=self.g_cross[: sink.passed], after=after,
        )

    def memory_gradient(self, after=()):
        (self.memory_grad,) = self.call(
            memory_gradient, "memory_gradient", "cross", [self.mdk, self.mdv],
            [((self.keys, D), bf16)], [wide(2 * D, D)], 5, after=after,
        )

    def token_gradient(self, after=()):
        (self.tokens_grad,) = self.call(
            token_gradient, "token_gradient", "self", [self.dq, self.dk, self.dv, self.gr1],
            [(self.act, bf16)], [wide(3 * D, D)], 6, after=after,
        )


def wide(*shape):
    return pltpu.VMEM(shape, bf16)


def full(*shape):
    return pltpu.VMEM(shape, f32)


def plain_layer(args, param_slabs):
    gathered = lax.all_gather(param_slabs, AXES, axis=0, tiled=True)
    total_rows = gathered.shape[0] // 4
    rows = gathered.reshape(total_rows, 4, 128)
    pieces = [rows[:, i, :] for i in range(4)]
    shapes = {"self": 2048 + 16, "cross": 2048, "ffn": 5120 + 128}
    firsts = {"self": 0, "cross": 2048, "ffn": 4096}
    sinks = {name: Sinks([(0, (2, shapes[name], 128))], firsts[name]) for name in shapes}
    source = Source(Pieces, ())
    run = Layer(*args, {n: source for n in shapes}, {n: pieces for n in shapes}, sinks)
    run.self_forward()
    run.cross_forward()
    run.ffn()
    run.cross_backward()
    run.self_backward()
    run.slot_forward()
    run.memory_gradient()
    run.token_gradient()
    send, keep = [
        jnp.concatenate([run.g_self[i][:, :2048], run.g_cross[i], run.g_ffn[i]], axis=1)
        .at[:, ROW_VEC : ROW_VEC + 16]
        .add(run.g_self[i][:, 2048:])
        for i in range(2)
    ]
    first = lax.axis_index("narrow") % 2 == 0
    low = jnp.where(first, keep, send)
    high = jnp.where(first, send, keep)
    flat = jnp.concatenate([low, high], axis=0).transpose(1, 0, 2)
    flat = jnp.pad(flat, ((0, total_rows - flat.shape[0]), (0, 0), (0, 0))).reshape(-1, 128)
    param_grad = lax.psum_scatter(flat, AXES, scatter_dimension=0, tiled=True).astype(f32)
    return run.slots, run.tokens_grad, run.memory_grad, param_grad


def moves(rule):
    number = lambda z, x, y, c: ((z * 2 + x) * 2 + y) * 2 + c
    pairs = []
    for z in range(4):
        for x in range(2):
            for y in range(2):
                for c in range(2):
                    target = rule(z, x, y, c)
                    if target is not None:
                        pairs.append((number(z, x, y, c), number(*target)))
    return pairs


OTHER_CORE = moves(lambda z, x, y, c: (z, x, y, 1 - c))
ALONG_X = moves(lambda z, x, y, c: (z, 1 - x, y, c))
ALONG_Y = moves(lambda z, x, y, c: (z, x, 1 - y, c))
ALONG_BOTH = moves(lambda z, x, y, c: (z, 1 - x, 1 - y, c))
ALONG_Z = moves(lambda z, x, y, c: (z ^ 1, x, y, c))
TWO_ALONG_Z = moves(lambda z, x, y, c: (z ^ 2, x, y, c))


def hops(table):
    return moves(lambda z, x, y, c: (table[z], x, y, c) if z in table else None)


def permute(value, pairs):
    return lax.ppermute(value, AXES, pairs)


def total(*values):
    return sum(value.astype(f32) for value in values).astype(bf16)


def spread_plane(own):
    return [own] + [permute(own, pairs) for pairs in (ALONG_X, ALONG_Y, ALONG_BOTH)]


def to_other_core(values):
    return [permute(value, OTHER_CORE) for value in values]


def sum_plane(keep, got):
    return [
        permute(total(keep[i], got[i]), pairs)
        for i, pairs in ((1, ALONG_X), (2, ALONG_Y), (3, ALONG_BOTH))
    ]


def here(keep, got, arrived):
    return total(keep[0], got[0], *arrived)


def hold(arrays, after):
    anywhere = pl.BlockSpec(memory_space=pl.ANY)
    return pl.pallas_call(
        lambda *refs: None, name="hold",
        out_shape=tuple(jax.ShapeDtypeStruct(v.shape, v.dtype) for v in arrays),
        in_specs=[anywhere] * (len(arrays) + len(after)), out_specs=(anywhere,) * len(arrays),
        input_output_aliases={i: i for i in range(len(arrays))},
    )(*arrays, *after)


def chip_layer(args, param_slabs):
    z = lax.axis_index("wide") // 2
    shard_rows = param_slabs.shape[0]
    small = lambda *s: jax.ShapeDtypeStruct(s, bf16)
    real = lambda *s: jax.ShapeDtypeStruct(s, f32)
    keep, send, one, two = pl.pallas_call(
        split_shard, name="split_shard",
        out_shape=(small(2, PAD_ROWS, 128),) * 2 + (small(2, 16, 128),) * 2,
        in_specs=[WHOLE], out_specs=(WHOLE,) * 4, scratch_shapes=[full(4 * PAD_ROWS, 128)],
    )(param_slabs)
    got = permute(send, OTHER_CORE)

    def few(core):
        def rule(z, x, y, c):
            if (y, c) == (1, 0):
                return (z, x, 0, core)
            return (0, 1, 1, core) if (z, x, y, c) == (3, 1, 1, 1) else None

        return moves(rule)

    one, two = permute(one, few(0)), permute(two, few(1))
    (unit,) = pl.pallas_call(
        join_unit, name="join_unit", out_shape=(small(1, 2, UNIT, 128),),
        in_specs=[WHOLE] * 4, out_specs=(WHOLE,), scratch_shapes=[full(2 * PAD_ROWS, 128)],
    )(keep, got, one, two)

    first = permute(unit, hops({0: 2, 1: 0, 3: 1}))
    plane0 = jnp.where(z == 0, unit, first)
    second = permute(jnp.where(z == 1, unit, plane0), hops({0: 1, 1: 2, 2: 3}))
    plane0 = jnp.where(z % 2 == 1, second, plane0)
    (unit,) = hold([unit], [plane0])
    mine0 = spread_plane(plane0)
    third = permute(second, hops({2: 3}))
    fourth = permute(unit, hops({2: 0}))
    plane1 = jnp.where(z < 2, jnp.where(z == 0, first, unit), jnp.where(z == 2, second, third))
    high = jnp.where(z < 2, jnp.where(z == 0, fourth, first), unit)
    plane1, high = hold([plane1, high], mine0[1:])
    groups = [mine0 + to_other_core(mine0), None, None]
    mine1 = spread_plane(plane1)
    near = permute(high, ALONG_Z)
    used = {"self": (0,), "cross": (0, 1), "ffn": (1, 2)}
    sources = {name: Source(Units, group) for name, group in used.items()}
    weights = {"self": groups[0]}
    one_unit = (2, UNIT, 128)
    sinks = {
        "ffn": Sinks([(7, one_unit), (102, (4, 2, 2, UNIT, 128))]),
        "cross": Sinks([(3, one_unit), (101, (4, 1, 2, UNIT, 128))], taken=[(7, 0, 576)]),
        "self": Sinks([(100, (4, 1, 2, UNIT, 128))], taken=[(3, 288, 288)]),
    }
    run = Layer(*args, sources, weights, sinks)
    run.self_forward()
    *mine1[1:], near = hold(mine1[1:] + [near], [run.r1])
    groups[1] = mine1 + to_other_core(mine1)
    weights["cross"] = groups[0] + groups[1]
    mine23 = spread_plane(jnp.concatenate([high, near], axis=0))
    run.cross_forward()
    mine23[1:] = hold(mine23[1:], [run.r2])
    groups[2] = mine23 + to_other_core(mine23)
    weights["ffn"] = groups[1] + groups[2]
    run.ffn()
    send23, keep23 = run.g_ffn[2:4]
    got23 = permute(send23, OTHER_CORE)
    arrived23 = sum_plane(keep23, got23)
    run.cross_backward()
    send1, keep1 = run.g_cross[2:4]
    (send1,) = hold([send1], arrived23)
    got1 = permute(send1, OTHER_CORE)
    arrived1 = sum_plane(keep1, got1)
    here23 = here(keep23, got23, arrived23)
    across23 = permute(here23[1], ALONG_Z)
    run.self_backward()
    send0, keep0 = run.g_self
    (send0,) = hold([send0], [*arrived1, across23])
    got0 = permute(send0, OTHER_CORE)
    here1 = here(keep1, got1, arrived1)[0]
    across1 = permute(here1, hops({0: 1, 3: 2}))
    arrived0 = sum_plane(keep0, got0)
    run.memory_gradient()
    run.token_gradient(after=arrived0)
    run.slot_forward()
    mixed23 = total(here23[0], across23)
    mixed1 = total(here1, across1)
    rest = permute(jnp.where(z < 2, mixed23, mixed1), hops({0: 2, 1: 3, 2: 1}))
    here0 = here(keep0, got0, arrived0)[0]
    (here0,) = hold([here0], [across1, run.memory_grad])
    mixed0 = total(here0, permute(here0, hops({1: 0, 3: 2})))
    (mixed0,) = hold([mixed0], [rest, run.tokens_grad])
    (last0,) = hold([permute(mixed0, hops({2: 0}))], [run.slots])
    pairs = [mixed0, last0, mixed1, rest, mixed23, rest]
    keep, send, ends = pl.pallas_call(
        split_unit, name="split_unit",
        out_shape=(real(2, PAD_ROWS, 128),) * 2 + (real(2, 16, 128),),
        in_specs=[WHOLE] * 6, out_specs=(WHOLE,) * 3, scratch_shapes=[full(2 * PAD_ROWS, 128)],
    )(*pairs)
    got = permute(send, OTHER_CORE)

    def last(core):
        def rule(z, x, y, c):
            if (y, c) == (0, core):
                return (z, x, 1, 0)
            return (3, 1, 1, 1) if (z, x, y, c) == (0, 1, 1, core) else None

        return moves(rule)

    (param_grad,) = pl.pallas_call(
        join_shard, name="join_shard", out_shape=(real(shard_rows, 128),),
        in_specs=[WHOLE] * 4, out_specs=(WHOLE,), scratch_shapes=[full(4 * PAD_ROWS, 128)],
    )(keep, got, permute(ends, last(0)), permute(ends, last(1)))
    return run.slots, run.tokens_grad, run.memory_grad, param_grad


def shards(mesh_shape, tokens, memory, slot_cotangent, param_slabs, segment_ids, memory_lengths,
           slot_mask):
    smem = pl.BlockSpec(memory_space=pltpu.SMEM)
    bounds = pl.pallas_call(
        find_bounds, name="find_bounds", out_shape=jax.ShapeDtypeStruct((8,), jnp.int32),
        in_specs=[WHOLE, smem], out_specs=smem,
    )(segment_ids, memory_lengths)
    chips = mesh_shape == (8, 4) and param_slabs.shape[0] == 4 * CORE_ROWS
    args = (tokens, memory, slot_cotangent, slot_mask, bounds)
    return (chip_layer if chips else plain_layer)(args, param_slabs)


def solution(mesh):
    spec = P(AXES, None)
    shape = tuple(mesh.shape[axis] for axis in AXES)
    return jax.shard_map(
        functools.partial(shards, shape),
        mesh=mesh,
        in_specs=(spec,) * 7,
        out_specs=(spec,) * 4,
        check_vma=False,
    )
```

```python
import functools
import math

import jax
import jax.numpy as jnp
from jax import lax
from jax.experimental import pallas as pl
from jax.experimental.pallas import tpu as pltpu
from jax.sharding import PartitionSpec as P

D = 512
HEADS = 8
HD = 64
FF = 2048
EPSILON = 1e-05
AXES = ("wide", "narrow")
QB = 128
PAIRS = HEADS // 2
BIG = -1e30
LOG2E = math.log2(math.e)
Q_SCALE = LOG2E * HD ** (-0.5)

f32 = jnp.float32
bf16 = jnp.bfloat16

ROW_Q, ROW_K, ROW_V, ROW_O = 0, 512, 1024, 1536
ROW_CQ, ROW_CK, ROW_CV, ROW_CO = 2048, 2560, 3072, 3584
ROW_IN, ROW_OUT, ROW_SLOT, ROW_VEC = 4096, 6144, 8192, 9216
VEC_ROWS = 32
VEC_NAMES = (
    "query_b", "value_b", "out_b", "cross_query_b", "cross_value_b", "cross_out_b", "gain_one",
    "shift_one", "gain_two", "shift_two", "gain_three", "shift_three", "outer_b", "slot_b", "inner_b",
)
VEC = {name: place for place, name in enumerate(VEC_NAMES)}

VMEM_LIMIT = 58 * 1024 * 1024


def dot(a, b):
    return jnp.dot(a, b, preferred_element_type=f32)


def dot_nt(a, b):
    return lax.dot_general(a, b, (((1,), (1,)), ((), ())), preferred_element_type=f32)


def dot_tn(a, b):
    return lax.dot_general(a, b, (((0,), (0,)), ((), ())), preferred_element_type=f32)


def column_sum(matrix):
    return jnp.sum(matrix.astype(f32), axis=0, keepdims=True)


def normalize(values):
    centered = values - jnp.mean(values, axis=-1, keepdims=True)
    root = lax.rsqrt(jnp.mean(centered * centered, axis=-1, keepdims=True) + EPSILON)
    return centered * root, root


def normalize_back(grad, normal, root, gain):
    scaled = grad * gain
    first = jnp.mean(scaled, axis=-1, keepdims=True)
    second = jnp.mean(scaled * normal, axis=-1, keepdims=True)
    return root * (scaled - first - normal * second)


CHIP_ROWS = 584
CORE_ROWS = 292
UNIT = 592
UNITS = 16


def unit_begin(unit):
    return 2 * CHIP_ROWS * (unit // 2) + UNIT * (unit % 2)


def unit_parts(begin, rows):
    parts = []
    for unit in range(UNITS):
        low = max(begin, unit_begin(unit))
        high = min(begin + rows, unit_begin(unit + 1))
        if low < high:
            parts.append((unit, low - unit_begin(unit), low - begin, high - low))
    return parts


SUM_UNIT = 608


def own_parts(begin, rows):
    parts = []
    for unit in range(UNITS):
        low = max(begin, CHIP_ROWS * unit)
        high = min(begin + rows, CHIP_ROWS * (unit + 1))
        if low < high:
            parts.append((unit, low - CHIP_ROWS * unit, low - begin, high - low))
    return parts


def group_of(unit):
    return min(unit // 4, 2)


class Place:
    def __init__(self, bounds=None):
        if bounds is not None:
            self.token_bounds = [bounds[i] for i in range(3)]
            self.memory_bounds = [bounds[3 + i] for i in range(3)]
        wide, narrow = lax.axis_index("wide"), lax.axis_index("narrow")
        self.z, self.x = lax.div(wide, 2), lax.rem(wide, 2)
        self.y, self.core = lax.div(narrow, 2), lax.rem(narrow, 2)

    def turned(self, unit):
        z, x, y = unit // 4, unit // 2 % 2, unit % 2
        low = jnp.bitwise_xor(lax.rem(self.z, 2), z % 2) if group_of(unit) == 2 else 0
        return jnp.bitwise_xor(self.x, x), jnp.bitwise_xor(self.y, y), low


class Units:
    count = 8

    def __init__(self, groups, refs):
        self.groups = {
            group: (refs[8 * i : 8 * i + 4], refs[8 * i + 4 : 8 * i + 8])
            for i, group in enumerate(groups)
        }

    def load(self, place, begin, buffer, sem):
        return self.load_parts(place, unit_parts(begin, buffer.shape[0]), buffer, sem)

    def load_vectors(self, place, buffer, sem):
        return self.load_parts(place, [(3, UNIT - 16, 0, 16)], buffer, sem)

    def load_parts(self, place, parts, buffer, sem):
        copies = []
        for unit, source, target, rows in parts:
            halves = self.groups[group_of(unit)]
            far_x, far_y, low = place.turned(unit)
            targets = [
                [
                    buffer.at[
                        pl.ds(target, rows),
                        pl.ds(
                            pl.multiple_of(
                                (jnp.bitwise_xor(place.core, half) * 2 + quarter) * 128, 128
                            ),
                            128,
                        ),
                    ]
                    for quarter in range(2)
                ]
                for half in range(2)
            ]

            def part(half, which, quarter):
                return halves[half][which].at[low, quarter, pl.ds(source, rows), :]

            for which in range(4):

                @pl.when((far_x == which % 2) & (far_y == which // 2))
                def _():
                    for half in range(2):
                        for quarter in range(2):
                            pltpu.make_async_copy(
                                part(half, which, quarter), targets[half][quarter], sem
                            ).start()

            copies += [
                pltpu.make_async_copy(part(half, 0, quarter), targets[half][quarter], sem)
                for half in range(2)
                for quarter in range(2)
            ]
        return copies


class Pieces:
    count = 4

    def __init__(self, groups, refs):
        self.refs = refs[:4]

    def load(self, place, begin, buffer, sem):
        copies = []
        for i, ref in enumerate(self.refs):
            copy = pltpu.make_async_copy(
                ref.at[pl.ds(begin, buffer.shape[0]), :],
                buffer.at[:, i * 128 : (i + 1) * 128],
                sem,
            )
            copy.start()
            copies.append(copy)
        return copies

    def load_vectors(self, place, buffer, sem):
        return self.load(place, ROW_VEC, buffer, sem)


def wait_all(copies):
    for copy in copies:
        copy.wait()


def vector(vec_ref, name):
    return vec_ref[VEC[name] : VEC[name] + 1, :].astype(f32)


class UnitSink:
    def __init__(self, outs):
        self.outs = outs
        self.refs = {key: (send.ref, keep.ref) for key, (send, keep) in outs.items()}

    def places(self, place, begin, rows):
        for unit, at, source, count in own_parts(begin, rows):
            if unit in self.refs:
                yield self.refs[unit], (), at, source, count
            elif group_of(unit) + 100 in self.refs:
                far_x, far_y, low = place.turned(unit)
                yield self.refs[group_of(unit) + 100], (far_x + 2 * far_y, low), at, source, count

    def send(self, place, units):
        for unit in units:
            far_x, far_y, low = place.turned(unit)
            for result in self.outs[group_of(unit) + 100]:
                result.send(far_x + 2 * far_y, low)

    def vector_places(self, place):
        far_x, far_y, low = place.turned(3)
        yield self.refs[100], (far_x + 2 * far_y, low), CHIP_ROWS, 0, 16


class RowSink:
    def __init__(self, outs, first):
        self.outs = outs
        self.refs = (outs[0].ref, outs[1].ref)
        self.first = first

    def send(self, place, units):
        pass


    def places(self, place, begin, rows):
        yield self.refs, (), begin - self.first, 0, rows

    def vector_places(self, place):
        yield self.refs, (), 2048, 0, 16


def put_grad(sink, place, begin, value):
    put_places(place, sink.places(place, begin, value.shape[0]), value)


def put_places(place, places, value):
    for (send, keep), lead, at, source, count in places:
        low = value[source : source + count, :].astype(bf16)
        for core in range(2):

            @pl.when(place.core == core)
            def _():
                for i in range(4):
                    ref = keep if i // 2 == core else send
                    ref[(*lead, i % 2, pl.ds(at, count), slice(None))] = low[:, lanes(i)]


def segment_of(position, bounds):
    return sum([(position >= bound).astype(jnp.int32) for bound in bounds])


def pick(index, choices):
    value = choices[-1]
    for place in range(len(choices) - 2, -1, -1):
        value = jnp.where(index == place, choices[place], value)
    return value


def key_range(first_query, query_bounds, key_bounds, length):
    low = segment_of(first_query, query_bounds)
    high = segment_of(first_query + (QB - 1), query_bounds)
    begin = pick(low, [0, *key_bounds]) // 128
    end = (pick(high, [*key_bounds, length]) + 127) // 128
    return begin * 128, end - begin


def query_marks(first_query, bounds):
    position = first_query + lax.broadcasted_iota(jnp.int32, (QB, 128), 0)
    lane = lax.broadcasted_iota(jnp.int32, (QB, 128), 1)
    hidden = (lane <= len(bounds)) & (lane != segment_of(position, bounds))
    return jnp.where(hidden, BIG, 0.0).astype(bf16)


def key_marks(length, bounds):
    position = lax.broadcasted_iota(jnp.int32, (length, 128), 0)
    lane = lax.broadcasted_iota(jnp.int32, (length, 128), 1)
    return jnp.where(lane == segment_of(position, bounds), 1.0, 0.0).astype(bf16)


def stack_heads(pair):
    lane = lax.broadcasted_iota(jnp.int32, pair.shape, 1)
    nothing = jnp.zeros_like(pair)
    return jnp.concatenate(
        [jnp.where(lane < HD, pair, nothing), jnp.where(lane >= HD, pair, nothing)], axis=0
    )


def by_count(count, most, body):
    for value in range(1, most + 1):

        @pl.when(count == value)
        def _():
            body(value)


def lanes(pair):
    return slice(pair * 128, (pair + 1) * 128)


def marked_keys(k_ref, kx, key_bounds):
    marks = key_marks(k_ref.shape[0], key_bounds)
    for pair in range(PAIRS):
        kx[pair, :, 0:128] = k_ref[:, lanes(pair)]
        kx[pair, :, 128:256] = marks


def attend(q_ref, kx, vt, ot_ref, o_ref, lse_ref, query_bounds, key_bounds):
    length = kx.shape[1]

    def block(index, carry):
        first = pl.multiple_of(index * QB, QB)
        begin, count = key_range(first, query_bounds, key_bounds, length)
        begin = pl.multiple_of(begin, 128)
        queries = pl.ds(first, QB)
        marks = query_marks(first, query_bounds)
        marks = jnp.concatenate([marks, marks], axis=0)

        def run(blocks):
            keys = pl.ds(begin, 128 * blocks)
            scores = []
            for pair in range(PAIRS):
                wide = jnp.concatenate([stack_heads(q_ref[queries, lanes(pair)]), marks], axis=1)
                scores.append(dot_nt(kx[pair, keys, :], wide))
            tops = []
            probs = []
            for pair in range(PAIRS):
                top = jnp.max(scores[pair], axis=0, keepdims=True)
                tops.append(top)
                probs.append(jnp.exp2(scores[pair] - top).astype(bf16))
            mixed = [dot(vt[pair, :, keys], probs[pair]) for pair in range(PAIRS)]
            for pair in range(PAIRS):
                total = mixed[pair][128:129, :]
                scale = 1.0 / total
                lse = tops[pair] + jnp.log2(total)
                one = mixed[pair][0:64, 0:128] * scale[:, 0:128]
                two = mixed[pair][64:128, 128:256] * scale[:, 128:256]
                out = jnp.concatenate([one, two], axis=0)
                ot_ref[lanes(pair), queries] = out.astype(bf16)
                o_ref[queries, lanes(pair)] = out.T.astype(bf16)
                lse_ref[2 * pair : 2 * pair + 1, queries] = lse[:, 0:128]
                lse_ref[2 * pair + 1 : 2 * pair + 2, queries] = lse[:, 128:256]

        by_count(count, length // 128, run)
        return carry

    lax.fori_loop(0, q_ref.shape[0] // QB, block, 0)


def attend_back(
    q_ref, kx, kt, v_ref, do_ref, lse_ref, dq_ref, dk_sum, dv_sum, query_bounds, key_bounds
):
    length = kx.shape[1]
    dk_sum[...] = jnp.zeros_like(dk_sum)
    dv_sum[...] = jnp.zeros_like(dv_sum)

    def block(index, carry):
        first = pl.multiple_of(index * QB, QB)
        begin, count = key_range(first, query_bounds, key_bounds, length)
        begin = pl.multiple_of(begin, 128)
        queries = pl.ds(first, QB)
        marks = query_marks(first, query_bounds)
        marks = jnp.concatenate([marks, marks], axis=0)

        def run(blocks):
            keys = pl.ds(begin, 128 * blocks)

            def products(pair):
                q_two = stack_heads(q_ref[queries, lanes(pair)])
                do_two = stack_heads(do_ref[queries, lanes(pair)])
                scores = dot_nt(kx[pair, keys, :], jnp.concatenate([q_two, marks], axis=1))
                grad_probs = dot_nt(v_ref[keys, lanes(pair)], do_two)
                return q_two, do_two, scores, grad_probs

            now = products(0)
            for pair in range(PAIRS):
                later = products(pair + 1) if pair + 1 < PAIRS else None
                q_two, do_two, scores, grad_probs = now
                lse = jnp.concatenate(
                    [
                        lse_ref[2 * pair : 2 * pair + 1, queries],
                        lse_ref[2 * pair + 1 : 2 * pair + 2, queries],
                    ],
                    axis=1,
                )
                probs = jnp.exp2(scores - lse)
                both = probs * grad_probs
                delta = jnp.sum(both, axis=0, keepdims=True)
                grad_scores = (both - probs * delta).astype(bf16)
                dqt = dot(kt[lanes(pair), keys], grad_scores)
                dk_sum[keys, lanes(pair)] += dot(grad_scores, q_two)
                dv_sum[keys, lanes(pair)] += dot(probs.astype(bf16), do_two)
                dq = jnp.concatenate([dqt[0:64, 0:128], dqt[64:128, 128:256]], axis=0)
                dq_ref[queries, lanes(pair)] = (dq * HD ** (-0.5)).T.astype(bf16)
                now = later

        by_count(count, length // 128, run)
        return carry

    lax.fori_loop(0, q_ref.shape[0] // QB, block, 0)


def values_transposed(v_ref, vt):
    for pair in range(PAIRS):
        vt[pair, 0:128, :] = v_ref[:, lanes(pair)].T
        vt[pair, 128:144, :] = jnp.ones((16, vt.shape[2]), bf16)


def four(values):
    return jnp.concatenate([values] * 4, axis=1)


def rows_of(w, i):
    return w[i * D : (i + 1) * D, :]


def add_out(r, x, o, w, bias):
    tile = 256
    for t in range(o.shape[0] // tile):
        rows = slice(t * tile, (t + 1) * tile)
        r.ref[rows, :] = x[rows, :].astype(f32) + dot(o[rows, :], w) + bias
        r.send(pl.ds(t * tile, tile))


def self_forward(source, scalars, x, *rest):
    (q, k, v, ot, lse, r, wq, wk, wv, wo, vec, kx, vt, o, sems) = rest[source.count_all :]
    place = Place(scalars)
    weights = source(rest)
    start(x)
    k_copies = weights.load(place, ROW_K, wk, sems.at[0])
    q_copies = weights.load(place, ROW_Q, wq, sems.at[1])
    q_copies += weights.load_vectors(place, vec, sems.at[1])
    v_copies = weights.load(place, ROW_V, wv, sems.at[2])
    x = x.get()
    wait_all(k_copies)
    k.ref[...] = dot(x[...], wk[...]).astype(bf16)
    k.send()
    wait_all(q_copies)
    q.ref[...] = ((dot(x[...], wq[...]) + vector(vec, "query_b")) * Q_SCALE).astype(bf16)
    q.send()
    wait_all(v_copies)
    v.ref[...] = (dot(x[...], wv[...]) + vector(vec, "value_b")).astype(bf16)
    v.send()
    o_copies = weights.load(place, ROW_O, wo, sems.at[0])
    bounds = place.token_bounds
    marked_keys(k.ref, kx, bounds)
    values_transposed(v.ref, vt)
    attend(q.ref, kx, vt, ot.ref, o, lse.ref, bounds, bounds)
    ot.send()
    wait_all(o_copies)
    add_out(r, x, o, wo[...], vector(vec, "out_b"))


def cross_forward(source, scalars, m, r1, *rest):
    (q, k, v, ot, lse, r, wq, wk, wv, wo, vec, kx, vt, o, h, sems) = rest[source.count_all :]
    place = Place(scalars)
    weights = source(rest)
    start(m)
    k_copies = weights.load(place, ROW_CK, wk, sems.at[0])
    v_copies = weights.load(place, ROW_CV, wv, sems.at[1])
    v_copies += weights.load_vectors(place, vec, sems.at[1])
    m = m.get()
    wait_all(k_copies)
    start(r1)
    q_copies = weights.load(place, ROW_CQ, wq, sems.at[2])
    k.ref[...] = dot(m[...], wk[...]).astype(bf16)
    k.send()
    wait_all(v_copies)
    v.ref[...] = (dot(m[...], wv[...]) + vector(vec, "cross_value_b")).astype(bf16)
    v.send()
    o_copies = weights.load(place, ROW_CO, wo, sems.at[0])
    r1 = r1.get()
    h[...] = normalize(r1[...])[0] * vector(vec, "gain_one") + vector(vec, "shift_one")
    wait_all(q_copies)
    q.ref[...] = (
        (dot(h[...].astype(bf16), wq[...]) + vector(vec, "cross_query_b")) * Q_SCALE
    ).astype(bf16)
    q.send()
    marked_keys(k.ref, kx, place.memory_bounds)
    values_transposed(v.ref, vt)
    attend(q.ref, kx, vt, ot.ref, o, lse.ref, place.token_bounds, place.memory_bounds)
    ot.send()
    wait_all(o_copies)
    add_out(r, h, o, wo[...], vector(vec, "cross_out_b"))


def gelu_parts(x):
    scale = math.sqrt(2.0 / math.pi)
    square = x * x
    half = 0.5 + 0.5 * jnp.tanh(x * (scale + (scale * 0.044715) * square))
    value = x * half
    slope = half + value * (1.0 - half) * (2.0 * scale + (6.0 * scale * 0.044715) * square)
    return value, slope


def same_next(first, rows, bounds, length):
    later = first + 1 + lax.broadcasted_iota(jnp.int32, (rows, 128), 0)
    same = later != length
    for bound in bounds:
        same = same & (later != bound)
    return same.astype(f32)


def prepare(source, scalars, mask_in, cot_in, r2_in, *rest):
    (gs, gs2, h2, vec, mask, spread, sems) = rest[source.count_all :]
    place = Place(scalars)
    start(mask_in, cot_in, r2_in)
    copies = source(rest).load_vectors(place, vec, sems.at[0])
    bounds = place.token_bounds
    length = h2.ref.shape[0]
    tile = 256
    mask[...] = jnp.broadcast_to(mask_in.get()[...].astype(f32), (128, length)).T
    cot_ref = cot_in.get()
    spread[0:8, :] = jnp.zeros((8, D), f32)
    for t in range(length // tile):
        rows = slice(t * tile, (t + 1) * tile)
        part = cot_ref[rows, :].astype(f32) * four(mask[rows, :])
        gs.ref[rows, :] = part.astype(bf16)
        same = same_next(t * tile, tile, bounds, length)
        spread[8 + t * tile : 8 + (t + 1) * tile, :] = part * four(same)
        gs2.ref[rows, :] = spread[7 + t * tile : 7 + (t + 1) * tile, :].astype(bf16)
    gs.send()
    gs2.send()
    wait_all(copies)
    h2.ref[...] = normalize(r2_in.get()[...])[0] * vector(vec, "gain_two") + vector(vec, "shift_two")


def ffn(source, make_sink, scalars, h2_in, gs_in, gs2_in, r2_in, *rest):
    rest_ = rest[source.count_all :]
    hlow_out, gr2 = rest_[:2]
    hlow, gr2_ref = hlow_out.ref, gr2.ref
    count = make_sink.count
    sink = make_sink(rest_[2 : 2 + count])
    (w_in, w_raw, w_out, w_slot, vec, comb, act, slope, h3, gf, gr3, h2b, gv_ref, sems) = rest_[
        2 + count :
    ]
    place = Place(scalars)
    weights = source(rest)
    in_copies = weights.load(place, ROW_IN, w_raw, sems.at[0])
    in_copies += weights.load(place, ROW_VEC, vec, sems.at[0])
    start(h2_in)
    length = gr2_ref.shape[0]
    tile = 256
    tiles = length // tile
    gv_ref[...] = jnp.zeros_like(gv_ref)

    def add_vector(name, value, at=0):
        at = VEC[name] + at
        gv_ref[at : at + 1, :] += value

    wait_all(in_copies)
    for i in range(4):
        comb[i] = w_raw[:, lanes(i)].astype(f32)
        for c in range(4):
            w_in[c, :, lanes(i)] = comb[i, pl.ds(c, D, 4), :].astype(bf16)
    out_copies = weights.load(place, ROW_OUT, w_out, sems.at[1])
    h2_ref = h2_in.get()
    slot_copies = weights.load(place, ROW_SLOT, w_slot, sems.at[2])
    start(gs_in, gs2_in, r2_in)
    biases = [vec[VEC["inner_b"] + c : VEC["inner_b"] + c + 1, :].astype(f32) for c in range(4)]

    def inner(t, c):
        rows = slice(t * tile, (t + 1) * tile)
        if c == 0:
            h2b[rows, :] = h2_ref[rows, :].astype(bf16)
        return dot(h2b[rows, :], w_in[c]) + biases[c]

    steps = [(t, c) for t in range(tiles) for c in range(4)]
    ahead = inner(*steps[0])
    wait_all(out_copies)
    for place_in, (t, c) in enumerate(steps):
        pre = ahead
        if place_in + 1 < len(steps):
            ahead = inner(*steps[place_in + 1])
        rows = slice(t * tile, (t + 1) * tile)
        value, gate = gelu_parts(pre)
        act[rows, c * D : (c + 1) * D] = value.astype(bf16)
        slope[rows, c * D : (c + 1) * D] = gate.astype(bf16)
        if c == 3:
            h3[rows, :] = h2_ref[rows, :] + dot(act[rows, :], w_out[...]) + vector(vec, "outer_b")
    wait_all(slot_copies)
    gs, gs2, r2_ref = gs_in.get(), gs2_in.get(), r2_in.get()

    def third(t, carry):
        first = pl.multiple_of(t * tile, tile)
        rows = pl.ds(first, tile)
        normal, root = normalize(h3[rows, :])
        out = normal * vector(vec, "gain_three") + vector(vec, "shift_three")
        hlow[rows, :] = out.astype(bf16)
        grad = dot_nt(gs[rows, :], w_slot[0:D, :]) + dot_nt(gs2[rows, :], w_slot[D : 2 * D, :])
        add_vector("gain_three", column_sum(grad * normal))
        add_vector("shift_three", column_sum(grad))
        gr3[rows, :] = normalize_back(grad, normal, root, vector(vec, "gain_three"))
        return carry

    lax.fori_loop(0, tiles, third, 0)
    hlow_out.send()
    add_vector("slot_b", column_sum(gs[...]))
    put_grad(sink, place, ROW_SLOT, dot_tn(hlow[...], gs[...]))
    put_grad(sink, place, ROW_SLOT + D, dot_tn(hlow[...], gs2[...]))
    gf[...] = gr3[...].astype(bf16)
    add_vector("outer_b", column_sum(gf[...]))
    for c in range(4):
        put_grad(sink, place, ROW_OUT + c * D, dot_tn(act[:, c * D : (c + 1) * D], gf[...]))
    sink.send(place, range(11, 15))

    def backward(t, carry):
        first = pl.multiple_of(t * tile, tile)
        rows = pl.ds(first, tile)
        total = gr3[rows, :]
        for c in range(4):
            at = slice(c * D, (c + 1) * D)
            grad = dot_nt(gf[rows, :], w_out[at, :]).astype(bf16)
            pre = (grad.astype(f32) * slope[rows, at].astype(f32)).astype(bf16)
            slope[rows, at] = pre
            add_vector("inner_b", column_sum(pre), c)
            total = total + dot_nt(pre, w_in[c])
        normal, root = normalize(r2_ref[rows, :])
        add_vector("gain_two", column_sum(total * normal))
        add_vector("shift_two", column_sum(total))
        gr2_ref[rows, :] = normalize_back(total, normal, root, vector(vec, "gain_two"))
        return carry

    lax.fori_loop(0, tiles, backward, 0)
    gr2.send()
    put_grad(sink, place, ROW_VEC, gv_ref[...])
    sink.send(place, [15])
    for c in range(4):
        part = dot_tn(h2b[...], slope[:, c * D : (c + 1) * D])
        for i in range(4):
            comb[i, pl.ds(c, D, 4), :] = part[:, lanes(i)]
    put_grad(sink, place, ROW_IN, jnp.concatenate([comb[i] for i in range(4)], axis=1))
    sink.send(place, range(8, 11))


def slot_forward(source, scalars, mask_in, hlow_in, *rest):
    (slots, w, vec, spread, mask, sems) = rest[source.count_all :]
    place = Place(scalars)
    weights = source(rest)
    copies = weights.load(place, ROW_SLOT, w, sems.at[0])
    copies += weights.load(place, ROW_VEC, vec, sems.at[0])
    start(mask_in, hlow_in)
    hlow = hlow_in.get()
    length = hlow.shape[0]
    tile = 256
    mask[...] = jnp.broadcast_to(mask_in.get()[...].astype(f32), (128, length)).T
    spread[0:length, :] = hlow[...].astype(f32)
    spread[length : length + 8, :] = jnp.zeros((8, D), f32)
    wait_all(copies)
    for t in range(length // tile):
        rows = slice(t * tile, (t + 1) * tile)
        later = spread[t * tile + 1 : (t + 1) * tile + 1, :]
        same = four(same_next(t * tile, tile, place.token_bounds, length))
        raw = (
            dot(hlow[rows, :], w[0:D, :])
            + dot((later * same).astype(bf16), w[D : 2 * D, :])
            + vector(vec, "slot_b")
        )
        slots.ref[rows, :] = (four(mask[rows, :]) * raw).astype(bf16)
        slots.send(pl.ds(t * tile, tile))


def attend_backward(place, key_bounds, w, gr_low, v_in, q_in, lse_in, dq, dk, dv, scratch,
                    later):
    (kx, kt, dk_sum, dv_sum, do) = scratch
    do[...] = dot_nt(gr_low[...], w).astype(bf16)
    v_ref, q_ref, lse_ref = v_in.get(), q_in.get(), lse_in.get()
    start(*later)
    attend_back(
        q_ref, kx, kt, v_ref, do, lse_ref, dq.ref, dk_sum, dv_sum, place.token_bounds, key_bounds
    )
    dk.ref[...] = (dk_sum[...] * (1.0 / LOG2E)).astype(bf16)
    dv.ref[...] = dv_sum[...].astype(bf16)
    for out in (dq, dk, dv):
        if isinstance(out, Out):
            out.send()


def keys_ready(place, key_bounds, k_in, kx, kt):
    k_ref = k_in.get()
    marked_keys(k_ref, kx, key_bounds)
    for pair in range(PAIRS):
        kt[lanes(pair), :] = k_ref[:, lanes(pair)].T


class Held:
    def __init__(self, ref):
        self.ref = ref


def cross_backward(source, make_sink, scalars, k_in, gr2_in, v_in, q_in, lse_in, ot_in, r1_in, m_in,
                   *rest):
    passed = rest[source.count_all : source.count_all + make_sink.passed]
    rest_ = rest[source.count_all + make_sink.passed :]
    dk, dv, gr1, gv = rest_[:4]
    count = make_sink.count
    sink = make_sink(rest_[4 : 4 + count])
    (wq, wo, vec, grad, h, dq, *scratch, sems) = rest_[4 + count :]
    place = Place(scalars)
    weights = source(rest)
    start(k_in, gr2_in)
    o_copies = weights.load(place, ROW_CO, wo, sems.at[0])
    keys_ready(place, place.memory_bounds, k_in, *scratch[:2])
    start(v_in, q_in, lse_in)
    q_copies = weights.load(place, ROW_CQ, wq, sems.at[1])
    q_copies += weights.load_vectors(place, vec, sems.at[1])
    gv.ref[...] = jnp.zeros_like(gv.ref)

    def set_vector(name, value):
        gv.ref[VEC[name] : VEC[name] + 1, :] = value

    gr2_ref = gr2_in.get()
    grad[...] = gr2_ref[...].astype(bf16)
    wait_all(o_copies)
    attend_backward(
        place, place.memory_bounds, wo[...], grad, v_in, q_in, lse_in, Held(dq), dk, dv, scratch,
        [r1_in, ot_in, m_in, *passed],
    )
    set_vector("cross_out_b", column_sum(grad[...]))
    ot_ref, r1_ref = ot_in.get(), r1_in.get()
    wait_all(q_copies)
    normal, root = normalize(r1_ref[...])
    gain = vector(vec, "gain_one")
    h[...] = (normal * gain + vector(vec, "shift_one")).astype(bf16)
    total = gr2_ref[...] + dot_nt(dq[...], wq[...])
    set_vector("gain_one", column_sum(total * normal))
    set_vector("shift_one", column_sum(total))
    gr1.ref[...] = normalize_back(total, normal, root, gain)
    gr1.send()
    make_sink.pass_on(sink, place, passed)
    m_ref = m_in.get()
    put_grad(sink, place, ROW_CO, dot(ot_ref[...], grad[...]))
    put_grad(sink, place, ROW_CV, dot_tn(m_ref[...], dv.ref[...]))
    sink.send(place, [6, 7])
    set_vector("cross_value_b", column_sum(dv.ref[...]))
    put_grad(sink, place, ROW_CK, dot_tn(m_ref[...], dk.ref[...]))
    sink.send(place, [5])
    put_grad(sink, place, ROW_CQ, dot_tn(h[...], dq[...]))
    sink.send(place, [4])
    set_vector("cross_query_b", column_sum(dq[...]))


def memory_gradient(source, scalars, dk_in, dv_in, *rest):
    (mgrad, w, sems) = rest[source.count_all :]
    copies = source(rest).load(Place(), ROW_CK, w, sems.at[0])
    start(dk_in, dv_in)
    dk, dv = dk_in.get(), dv_in.get()
    wait_all(copies)
    tile = 256
    for t in range(dk.shape[0] // tile):
        rows = slice(t * tile, (t + 1) * tile)
        value = dot_nt(dk[rows, :], rows_of(w, 0)) + dot_nt(dv[rows, :], rows_of(w, 1))
        mgrad.ref[rows, :] = value.astype(bf16)
        mgrad.send(pl.ds(t * tile, tile))


def self_backward(source, make_sink, scalars, k_in, gr1_in, v_in, q_in, lse_in, ot_in, x_in, gv_in,
                  *rest):
    passed = rest[source.count_all : source.count_all + make_sink.passed]
    rest_ = rest[source.count_all + make_sink.passed :]
    dq, dk, dv = rest_[:3]
    count = make_sink.count
    sink = make_sink(rest_[3 : 3 + count])
    (w, grad, gv, *scratch, sems) = rest_[3 + count :]
    place = Place(scalars)
    start(k_in, gr1_in)
    copies = source(rest).load(place, ROW_O, w, sems.at[0])
    keys_ready(place, place.token_bounds, k_in, *scratch[:2])
    start(v_in, q_in, lse_in)
    gr1_ref = gr1_in.get()
    grad[...] = gr1_ref[...].astype(bf16)
    wait_all(copies)
    attend_backward(
        place, place.token_bounds, w[...], grad, v_in, q_in, lse_in, dq, dk, dv, scratch,
        [ot_in, x_in, gv_in, *passed],
    )
    ot_ref, x_ref = ot_in.get(), x_in.get()
    gv[...] = gv_in.get()[...]

    def set_vector(name, value):
        gv[VEC[name] : VEC[name] + 1, :] = value

    make_sink.pass_on(sink, place, passed)
    put_grad(sink, place, ROW_O, dot(ot_ref[...], grad[...]))
    set_vector("out_b", column_sum(grad[...]))
    put_grad(sink, place, ROW_V, dot_tn(x_ref[...], dv.ref[...]))
    sink.send(place, [2])
    set_vector("value_b", column_sum(dv.ref[...]))
    set_vector("query_b", column_sum(dq.ref[...]))
    put_places(place, sink.vector_places(place), gv[...])
    sink.send(place, [3])
    put_grad(sink, place, ROW_K, dot_tn(x_ref[...], dk.ref[...]))
    sink.send(place, [1])
    put_grad(sink, place, ROW_Q, dot_tn(x_ref[...], dq.ref[...]))
    sink.send(place, [0])


def token_gradient(source, scalars, dq_in, dk_in, dv_in, gr1_in, *rest):
    (tgrad, w, sems) = rest[source.count_all :]
    copies = source(rest).load(Place(), ROW_Q, w, sems.at[0])
    start(dq_in, dk_in, dv_in, gr1_in)
    dq, dk, dv, gr1_ref = dq_in.get(), dk_in.get(), dv_in.get(), gr1_in.get()
    wait_all(copies)
    tile = 256
    for t in range(dq.shape[0] // tile):
        rows = slice(t * tile, (t + 1) * tile)
        tgrad.ref[rows, :] = (
            gr1_ref[rows, :]
            + dot_nt(dq[rows, :], rows_of(w, 0))
            + dot_nt(dk[rows, :], rows_of(w, 1))
            + dot_nt(dv[rows, :], rows_of(w, 2))
        ).astype(bf16)
        tgrad.send(pl.ds(t * tile, tile))


def find_bounds(segments_ref, lengths_ref, out_ref):
    segments = segments_ref[...]
    before = jnp.int32(0)
    for i in range(3):
        out_ref[i] = jnp.sum((segments <= i).astype(jnp.int32))
        before = before + lengths_ref[0, i]
        out_ref[3 + i] = before


PAD_ROWS = 304
VEC_AT = ROW_VEC - 31 * CORE_ROWS


def split_shard(slab_ref, keep_ref, send_ref, one_ref, two_ref, full):
    place = Place()
    rows = slab_ref.shape[0]
    full[0:rows, :] = slab_ref[...].astype(f32)
    full[rows : 4 * PAD_ROWS, :] = jnp.zeros((4 * PAD_ROWS - rows, 128), f32)
    for i in range(4):
        part = full[pl.ds(i, PAD_ROWS, 4), :].astype(bf16)
        few_ref = (one_ref, two_ref)[i // 2]
        for core in range(2):

            @pl.when(place.core == core)
            def _():
                (keep_ref if i // 2 == core else send_ref)[i % 2] = part
                first = core * VEC_AT
                few_ref[i % 2] = full[pl.ds(4 * first + i, 16, 4), :].astype(bf16)


def join_unit(_, keep_ref, got_ref, one_ref, two_ref, unit_ref, full):
    place = Place()
    for i in range(2):
        for core in range(2):

            @pl.when(place.core == core)
            def _():
                first, second = (keep_ref, got_ref) if core == 0 else (got_ref, keep_ref)
                full[0:PAD_ROWS, :] = first[i].astype(f32)
                full[CORE_ROWS : CORE_ROWS + PAD_ROWS, :] = second[i].astype(f32)

        ends = one_ref[i].astype(f32) + two_ref[i].astype(f32)
        full[CHIP_ROWS : CHIP_ROWS + 16, :] = ends

        @pl.when(place.y == 0)
        def _():
            unit_ref[0, i] = full[0:UNIT, :].astype(bf16)

        @pl.when(place.y == 1)
        def _():
            unit_ref[0, i, 0:576, :] = full[8:CHIP_ROWS, :].astype(bf16)
            unit_ref[0, i, 576:UNIT, :] = ends.astype(bf16)


def split_unit(here0, across0, mixed1, rest, mixed23, keep, send, far_keep, far_send, vec, full):
    place = Place()
    for i in range(2):
        plane0 = here0[i].astype(f32) + across0[i].astype(f32)

        def rows(core):
            return full[CORE_ROWS * core : CORE_ROWS * core + PAD_ROWS, :]

        full[...] = plane0
        vec[i] = plane0[CHIP_ROWS : CHIP_ROWS + 16, :]
        for core in range(2):

            @pl.when(place.core == core)
            def _():
                far_keep[i] = rows(core).astype(bf16)
                far_send[i] = rows(1 - core).astype(bf16)

        for mixed, chosen in ((mixed1, place.z == 1), (mixed23, place.z >= 2)):

            @pl.when(chosen)
            def _():
                full[...] = mixed[i].astype(f32) + rest[i].astype(f32)

        for core in range(2):

            @pl.when(place.core == core)
            def _():
                keep[i] = rows(core)
                send[i] = rows(1 - core)

        @pl.when(place.z == 0)
        def _():
            far_keep[i, 0:16, :] = vec[i].astype(bf16)
            far_send[i, 0:16, :] = vec[i].astype(bf16)


def join_shard(keep, got, far_keep, far_got, one, two, out_ref, full):
    place = Place()
    rows = out_ref.shape[0]
    last = (place.core == 1) & (place.y == 1) & (place.x == 1) & (place.z == 3)
    for i in range(4):
        for core in range(2):

            @pl.when(place.core == core)
            def _():
                part, far = (keep, far_keep) if i // 2 == core else (got, far_got)
                full[pl.ds(i, PAD_ROWS, 4), :] = part[i % 2]

                @pl.when(place.z == 0)
                def _():
                    full[pl.ds(i, PAD_ROWS, 4), :] = part[i % 2] + far[i % 2].astype(f32)

        @pl.when(last)
        def _():
            at = pl.ds(4 * VEC_AT + i, 16, 4)
            near = (far_got, far_keep)[i // 2]
            full[at, :] = (
                full[at, :] + near[i % 2, 0:16, :].astype(f32) + (one, two)[i // 2][i % 2]
            )

    out_ref[...] = full[0:rows, :]


WHOLE = pl.BlockSpec(memory_space=pltpu.VMEM)


class In:
    def __init__(self, source, buffer, sem):
        self.buffer = buffer
        self.copy = pltpu.make_async_copy(source, buffer, sem)
        self.started = False

    def start(self):
        self.copy.start()
        self.started = True

    def get(self):
        if not self.started:
            self.start()
        self.copy.wait()
        return self.buffer


def start(*arrays):
    for array in arrays:
        array.start()


class Out:
    def __init__(self, target, ref, sem):
        self.target, self.ref, self.sem = target, ref, sem
        self.copies = []

    def send(self, *index):
        source, target = (self.ref.at[index], self.target.at[index]) if index else (self.ref, self.target)
        copy = pltpu.make_async_copy(source, target, self.sem)
        copy.start()
        self.copies.append(copy)

    def finish(self):
        if not self.copies:
            self.send()
        wait_all(self.copies)


def call(body, name, scalars, blocks, weights, outs, scratch, microseconds, passed=(), after=()):
    ins = [*blocks, *passed]
    buffers = [pltpu.VMEM(v.shape, v.dtype) for v in ins] + [pltpu.VMEM(s, t) for s, t in outs]
    sems = [pltpu.SemaphoreType.DMA((len(ins),)), pltpu.SemaphoreType.DMA((len(outs),))]

    def run(*refs):
        refs = list(refs)
        take = lambda n: [refs.pop(0) for _ in range(n)]
        scalars_ref, *in_refs = take(1 + len(ins))
        weight_refs, _, out_refs = take(len(weights)), take(len(after)), take(len(outs))
        in_buffers, out_buffers = take(len(ins)), take(len(outs))
        in_sems, out_sems = take(2)
        arrays = [In(in_refs[i], in_buffers[i], in_sems.at[i]) for i in range(len(ins))]
        results = [Out(out_refs[i], out_buffers[i], out_sems.at[i]) for i in range(len(outs))]
        body(
            scalars_ref, *arrays[: len(blocks)], *weight_refs, *arrays[len(blocks) :], *results, *refs
        )
        for result in results:
            result.finish()

    anywhere = pl.BlockSpec(memory_space=pl.ANY)
    return pl.pallas_call(
        run,
        name=name,
        out_shape=tuple(jax.ShapeDtypeStruct(s, t) for s, t in outs),
        in_specs=[pl.BlockSpec(memory_space=pltpu.SMEM)]
        + [anywhere] * (len(ins) + len(weights) + len(after)),
        out_specs=(anywhere,) * len(outs),
        scratch_shapes=buffers + sems + scratch,
        compiler_params=pltpu.CompilerParams(vmem_limit_bytes=VMEM_LIMIT),
        cost_estimate=pl.CostEstimate(
            flops=microseconds * 1_150_000_000,
            bytes_accessed=microseconds * 3_690_000,
            transcendentals=0,
        ),
    )(scalars, *ins, *weights, *after)


class Source:
    def __init__(self, kind, groups):
        self.kind = kind
        self.groups = groups
        self.count_all = kind.count * (len(groups) if kind is Units else 1)

    def __call__(self, refs):
        return self.kind(self.groups, refs)


class Sinks:
    def __init__(self, entries, first=None, taken=()):
        self.entries = entries
        self.first = first
        self.taken = taken
        self.count = 2 * len(entries)
        self.passed = 2 * len(taken)

    def outs(self):
        return [(shape, bf16) for _, shape in self.entries for _ in range(2)]

    def __call__(self, refs):
        pairs = [(refs[2 * i], refs[2 * i + 1]) for i in range(len(self.entries))]
        if self.first is not None:
            return RowSink(pairs[0], self.first)
        return UnitSink({key: pair for (key, _), pair in zip(self.entries, pairs)})

    def pass_on(self, sink, place, passed):
        for i, (unit, at, count) in enumerate(self.taken):
            far_x, far_y, low = place.turned(unit)
            arrays = [array.get() for array in passed[2 * i : 2 * i + 2]]
            for source, target in zip(arrays, sink.refs[group_of(unit) + 100]):
                for quarter in range(2):
                    target[far_x + 2 * far_y, low, quarter, at : at + count, :] = source[
                        quarter, at : at + count, :
                    ]


class Layer:
    def __init__(self, tokens, memory, slot_cotangent, slot_mask, bounds, sources, weights, sinks):
        self.tokens, self.memory = tokens, memory
        self.slot_cotangent, self.slot_mask = slot_cotangent, slot_mask
        self.bounds, self.sources, self.weights, self.sinks = bounds, sources, weights, sinks
        self.act = tokens.shape
        self.keys = memory.shape[0]
        self.sems = [pltpu.SemaphoreType.DMA((3,))]

    def call(self, body, name, which, blocks, outs, scratch, microseconds, sink=None, **more):
        parts = [self.sources[which]] + ([sink] if sink is not None else [])
        return call(
            functools.partial(body, *parts), name, self.bounds, blocks, self.weights[which], outs,
            scratch + self.sems, microseconds, **more,
        )

    def attend_outs(self, keys):
        length = self.act[0]
        return [
            (self.act, bf16), ((keys, D), bf16), ((keys, D), bf16), ((D, length), bf16),
            ((HEADS, length), f32), (self.act, f32),
        ]

    def attend_scratch(self, keys):
        return [
            wide(D, D), wide(D, D), wide(D, D), wide(D, D), wide(16, D), wide(PAIRS, keys, 256),
            wide(PAIRS, 144, keys),
            wide(*self.act),
        ]

    def self_forward(self, after=()):
        self.q, self.k, self.v, self.ot, self.lse, self.r1 = self.call(
            self_forward, "self_forward", "self", [self.tokens], self.attend_outs(self.act[0]),
            self.attend_scratch(self.act[0]), 18, after=after,
        )

    def cross_forward(self, after=()):
        self.cq, self.mk, self.mv, self.cot, self.clse, self.r2 = self.call(
            cross_forward, "cross_forward", "cross", [self.memory, self.r1],
            self.attend_outs(self.keys), self.attend_scratch(self.keys) + [full(*self.act)],
            19, after=after,
        )

    def prepare(self, after=()):
        length, act = self.act[0], self.act
        self.gs, self.gs2, self.h2 = self.call(
            prepare, "prepare", "self", [self.slot_mask, self.slot_cotangent, self.r2],
            [(act, bf16), (act, bf16), (act, f32)],
            [wide(16, D), full(length, 128), full(length + 8, D)], 5, after=after,
        )

    def ffn(self, after=()):
        length, act, sink = self.act[0], self.act, self.sinks["ffn"]
        self.hlow, self.gr2, *self.g_ffn = self.call(
            ffn, "ffn", "ffn", [self.h2, self.gs, self.gs2, self.r2],
            [(act, bf16), (act, f32)] + sink.outs(),
            [
                wide(4, D, D), wide(FF, D), wide(FF, D), wide(2 * D, D), wide(VEC_ROWS, D),
                full(4, FF, 128), wide(length, FF), wide(length, FF), full(*act), wide(*act),
                full(*act), wide(*act), full(128, D),
            ],
            34, sink, after=after,
        )

    def slot_forward(self, after=()):
        length = self.act[0]
        (self.slots,) = self.call(
            slot_forward, "slot_forward", "ffn", [self.slot_mask, self.hlow], [(self.act, bf16)],
            [wide(2 * D, D), wide(VEC_ROWS, D), full(length + 8, D), full(length, 128)], 6,
            after=after,
        )

    def back_scratch(self, keys):
        return [
            wide(PAIRS, keys, 256), wide(D, keys), full(keys, D), full(keys, D), wide(*self.act)
        ]

    def cross_backward(self, after=()):
        sink = self.sinks["cross"]
        self.mdk, self.mdv, self.gr1, self.gv, *self.g_cross = self.call(
            cross_backward, "cross_backward", "cross",
            [self.mk, self.gr2, self.mv, self.cq, self.clse, self.cot, self.r1, self.memory],
            [((self.keys, D), bf16)] * 2 + [(self.act, f32), ((16, D), f32)] + sink.outs(),
            [wide(D, D), wide(D, D), wide(16, D)] + [wide(*self.act)] * 3
            + self.back_scratch(self.keys),
            28, sink, passed=self.g_ffn[: sink.passed], after=after,
        )

    def self_backward(self, after=()):
        sink = self.sinks["self"]
        length = self.act[0]
        self.dq, self.dk, self.dv, *self.g_self = self.call(
            self_backward, "self_backward", "self",
            [self.k, self.gr1, self.v, self.q, self.lse, self.ot, self.tokens, self.gv],
            [(self.act, bf16)] * 3 + sink.outs(),
            [wide(D, D), wide(*self.act), full(16, D)] + self.back_scratch(length),
            26, sink, passed=self.g_cross[: sink.passed], after=after,
        )

    def memory_gradient(self, after=()):
        (self.memory_grad,) = self.call(
            memory_gradient, "memory_gradient", "cross", [self.mdk, self.mdv],
            [((self.keys, D), bf16)], [wide(2 * D, D)], 5, after=after,
        )

    def token_gradient(self, after=()):
        (self.tokens_grad,) = self.call(
            token_gradient, "token_gradient", "self", [self.dq, self.dk, self.dv, self.gr1],
            [(self.act, bf16)], [wide(3 * D, D)], 6, after=after,
        )


def wide(*shape):
    return pltpu.VMEM(shape, bf16)


def full(*shape):
    return pltpu.VMEM(shape, f32)


def plain_layer(args, param_slabs):
    gathered = lax.all_gather(param_slabs, AXES, axis=0, tiled=True)
    total_rows = gathered.shape[0] // 4
    rows = gathered.reshape(total_rows, 4, 128)
    pieces = [rows[:, i, :] for i in range(4)]
    shapes = {"self": 2048 + 16, "cross": 2048, "ffn": 5120 + 128}
    firsts = {"self": 0, "cross": 2048, "ffn": 4096}
    sinks = {name: Sinks([(0, (2, shapes[name], 128))], firsts[name]) for name in shapes}
    source = Source(Pieces, ())
    run = Layer(*args, {n: source for n in shapes}, {n: pieces for n in shapes}, sinks)
    run.self_forward()
    run.cross_forward()
    run.prepare()
    run.ffn()
    run.cross_backward()
    run.self_backward()
    run.slot_forward()
    run.memory_gradient()
    run.token_gradient()
    send, keep = [
        jnp.concatenate([run.g_self[i][:, :2048], run.g_cross[i], run.g_ffn[i]], axis=1)
        .at[:, ROW_VEC : ROW_VEC + 16]
        .add(run.g_self[i][:, 2048:])
        for i in range(2)
    ]
    first = lax.axis_index("narrow") % 2 == 0
    low = jnp.where(first, keep, send)
    high = jnp.where(first, send, keep)
    flat = jnp.concatenate([low, high], axis=0).transpose(1, 0, 2)
    flat = jnp.pad(flat, ((0, total_rows - flat.shape[0]), (0, 0), (0, 0))).reshape(-1, 128)
    param_grad = lax.psum_scatter(flat, AXES, scatter_dimension=0, tiled=True).astype(f32)
    return run.slots, run.tokens_grad, run.memory_grad, param_grad


def moves(rule):
    number = lambda z, x, y, c: ((z * 2 + x) * 2 + y) * 2 + c
    pairs = []
    for z in range(4):
        for x in range(2):
            for y in range(2):
                for c in range(2):
                    target = rule(z, x, y, c)
                    if target is not None:
                        pairs.append((number(z, x, y, c), number(*target)))
    return pairs


OTHER_CORE = moves(lambda z, x, y, c: (z, x, y, 1 - c))
ALONG_X = moves(lambda z, x, y, c: (z, 1 - x, y, c))
ALONG_Y = moves(lambda z, x, y, c: (z, x, 1 - y, c))
ALONG_BOTH = moves(lambda z, x, y, c: (z, 1 - x, 1 - y, c))
ALONG_Z = moves(lambda z, x, y, c: (z ^ 1, x, y, c))
TWO_ALONG_Z = moves(lambda z, x, y, c: (z ^ 2, x, y, c))


def hops(table):
    return moves(lambda z, x, y, c: (table[z], x, y, c) if z in table else None)


def permute(value, pairs):
    return lax.ppermute(value, AXES, pairs)


def total(*values):
    return sum(value.astype(f32) for value in values).astype(bf16)


def spread_plane(own):
    return [own] + [permute(own, pairs) for pairs in (ALONG_X, ALONG_Y, ALONG_BOTH)]


def to_other_core(values):
    return [permute(value, OTHER_CORE) for value in values]


def sum_plane(keep, got):
    return [
        permute(total(keep[i], got[i]), pairs)
        for i, pairs in ((1, ALONG_X), (2, ALONG_Y), (3, ALONG_BOTH))
    ]


def here(keep, got, arrived):
    return total(keep[0], got[0], *arrived)


def hold(arrays, after):
    anywhere = pl.BlockSpec(memory_space=pl.ANY)
    return pl.pallas_call(
        lambda *refs: None, name="hold",
        out_shape=tuple(jax.ShapeDtypeStruct(v.shape, v.dtype) for v in arrays),
        in_specs=[anywhere] * (len(arrays) + len(after)), out_specs=(anywhere,) * len(arrays),
        input_output_aliases={i: i for i in range(len(arrays))},
    )(*arrays, *after)


def chip_layer(args, param_slabs):
    z = lax.axis_index("wide") // 2
    shard_rows = param_slabs.shape[0]
    small = lambda *s: jax.ShapeDtypeStruct(s, bf16)
    real = lambda *s: jax.ShapeDtypeStruct(s, f32)
    keep, send, one, two = pl.pallas_call(
        split_shard, name="split_shard",
        out_shape=(small(2, PAD_ROWS, 128),) * 2 + (small(2, 16, 128),) * 2,
        in_specs=[WHOLE], out_specs=(WHOLE,) * 4, scratch_shapes=[full(4 * PAD_ROWS, 128)],
    )(param_slabs)
    got = permute(send, OTHER_CORE)

    def few(core):
        def rule(z, x, y, c):
            if (y, c) == (1, 0):
                return (z, x, 0, core)
            return (0, 1, 1, core) if (z, x, y, c) == (3, 1, 1, 1) else None

        return moves(rule)

    one, two = permute(one, few(0)), permute(two, few(1))
    (unit,) = pl.pallas_call(
        join_unit, name="join_unit", out_shape=(small(1, 2, UNIT, 128),),
        in_specs=[pl.BlockSpec(memory_space=pltpu.SMEM)] + [WHOLE] * 4, out_specs=(WHOLE,),
        scratch_shapes=[full(2 * PAD_ROWS, 128)],
    )(args[4], keep, got, one, two)

    first = permute(unit, hops({0: 2, 1: 0, 3: 1}))
    plane0 = jnp.where(z == 0, unit, first)
    second = permute(jnp.where(z == 1, unit, plane0), hops({0: 1, 1: 2, 2: 3}))
    plane0 = jnp.where(z % 2 == 1, second, plane0)
    (unit,) = hold([unit], [plane0])
    mine0 = spread_plane(plane0)
    third = permute(second, hops({2: 3}))
    fourth = permute(unit, hops({2: 0}))
    plane1 = jnp.where(z < 2, jnp.where(z == 0, first, unit), jnp.where(z == 2, second, third))
    high = jnp.where(z < 2, jnp.where(z == 0, fourth, first), unit)
    *mine0[1:], plane1, high = hold([*mine0[1:], plane1, high], [])
    groups = [mine0 + to_other_core(mine0), None, None]
    mine1 = spread_plane(plane1)
    near = permute(high, ALONG_Z)
    used = {"self": (0,), "cross": (0, 1), "ffn": (1, 2)}
    sources = {name: Source(Units, group) for name, group in used.items()}
    weights = {"self": groups[0]}
    one_unit = (2, SUM_UNIT, 128)
    sinks = {
        "ffn": Sinks([(7, one_unit), (102, (4, 2, 2, SUM_UNIT, 128))]),
        "cross": Sinks([(3, one_unit), (101, (4, 1, 2, SUM_UNIT, 128))], taken=[(7, 8, 576)]),
        "self": Sinks([(100, (4, 1, 2, SUM_UNIT, 128))], taken=[(3, 296, 288)]),
    }
    run = Layer(*args, sources, weights, sinks)
    run.self_forward()
    *mine1[1:], near = hold(mine1[1:] + [near], [run.r1])
    groups[1] = mine1 + to_other_core(mine1)
    weights["cross"] = groups[0] + groups[1]
    mine23 = spread_plane(jnp.concatenate([high, near], axis=0))
    run.cross_forward()
    run.prepare()
    mine23[1:] = hold(mine23[1:], [run.h2])
    groups[2] = mine23 + to_other_core(mine23)
    weights["ffn"] = groups[1] + groups[2]
    run.ffn()
    send23, keep23 = run.g_ffn[2:4]
    got23 = permute(send23, OTHER_CORE)
    arrived23 = sum_plane(keep23, got23)
    run.cross_backward()
    send1, keep1 = run.g_cross[2:4]
    (send1,) = hold([send1], arrived23)
    got1 = permute(send1, OTHER_CORE)
    arrived1 = sum_plane(keep1, got1)
    here23 = here(keep23, got23, arrived23)
    across23 = permute(here23[1], ALONG_Z)
    run.self_backward()
    send0, keep0 = run.g_self
    (send0,) = hold([send0], [*arrived1, across23])
    got0 = permute(send0, OTHER_CORE)
    here1 = here(keep1, got1, arrived1)[0]
    across1 = permute(here1, hops({0: 1, 3: 2}))
    arrived0 = sum_plane(keep0, got0)
    run.memory_gradient()
    run.token_gradient(after=arrived0)
    run.slot_forward()
    mixed23 = total(here23[0], across23)
    mixed1 = total(here1, across1)
    rest = permute(jnp.where(z < 2, mixed23, mixed1), hops({0: 2, 1: 3, 2: 1}))
    here0 = here(keep0, got0, arrived0)[0]
    (here0,) = hold([here0], [across1, run.memory_grad])
    across0 = permute(here0, hops({1: 0, 3: 2}))
    (across0,) = hold([across0], [rest, run.tokens_grad])
    keep, send, far_keep, far_send, vec = pl.pallas_call(
        split_unit, name="split_unit",
        out_shape=(real(2, PAD_ROWS, 128),) * 2 + (small(2, PAD_ROWS, 128),) * 2
        + (real(2, 16, 128),),
        in_specs=[WHOLE] * 5, out_specs=(WHOLE,) * 5, scratch_shapes=[full(SUM_UNIT, 128)],
    )(here0, across0, mixed1, rest, mixed23)

    def down(other):
        def rule(z, x, y, c):
            if z == 2:
                return (0, x, y, c ^ other)
            return (3, 1, 1, 1) if (z, x, y, c) == (0, 1, 1, 1 - other) else None

        return moves(rule)

    one, two = [
        permute(vec, moves(lambda z, x, y, c: (3, 1, 1, 1) if (z, x, y, c) == (2, 1, 1, core) else None))
        for core in range(2)
    ]
    far_keep, far_got = permute(far_keep, down(0)), permute(far_send, down(1))
    got = permute(send, OTHER_CORE)
    (got,) = hold([got], [run.slots])
    (param_grad,) = pl.pallas_call(
        join_shard, name="join_shard", out_shape=(real(shard_rows, 128),),
        in_specs=[WHOLE] * 6, out_specs=(WHOLE,), scratch_shapes=[full(4 * PAD_ROWS, 128)],
    )(keep, got, far_keep, far_got, one, two)
    return run.slots, run.tokens_grad, run.memory_grad, param_grad


def shards(mesh_shape, tokens, memory, slot_cotangent, param_slabs, segment_ids, memory_lengths,
           slot_mask):
    smem = pl.BlockSpec(memory_space=pltpu.SMEM)
    bounds = pl.pallas_call(
        find_bounds, name="find_bounds", out_shape=jax.ShapeDtypeStruct((8,), jnp.int32),
        in_specs=[WHOLE, smem], out_specs=smem,
    )(segment_ids, memory_lengths)
    chips = mesh_shape == (8, 4) and param_slabs.shape[0] == 4 * CORE_ROWS
    args = (tokens, memory, slot_cotangent, slot_mask, bounds)
    return (chip_layer if chips else plain_layer)(args, param_slabs)


def solution(mesh):
    spec = P(AXES, None)
    shape = tuple(mesh.shape[axis] for axis in AXES)
    return jax.shard_map(
        functools.partial(shards, shape),
        mesh=mesh,
        in_specs=(spec,) * 7,
        out_specs=(spec,) * 4,
        check_vma=False,
    )
```

```python
import functools
import math

import jax
import jax.numpy as jnp
from jax import lax
from jax.experimental import pallas as pl
from jax.experimental.pallas import tpu as pltpu
from jax.sharding import PartitionSpec as P

D = 512
HEADS = 8
HD = 64
FF = 2048
EPSILON = 1e-05
AXES = ("wide", "narrow")
QB = 128
PAIRS = HEADS // 2
BIG = -1e30
LOG2E = math.log2(math.e)
Q_SCALE = LOG2E * HD ** (-0.5)

f32 = jnp.float32
bf16 = jnp.bfloat16

ROW_Q, ROW_K, ROW_V, ROW_O = 0, 512, 1024, 1536
ROW_CQ, ROW_CK, ROW_CV, ROW_CO = 2048, 2560, 3072, 3584
ROW_IN, ROW_OUT, ROW_SLOT, ROW_VEC = 4096, 6144, 8192, 9216
VEC_ROWS = 32
VEC_NAMES = (
    "query_b", "value_b", "out_b", "cross_query_b", "cross_value_b", "cross_out_b", "gain_one",
    "shift_one", "gain_two", "shift_two", "gain_three", "shift_three", "outer_b", "slot_b", "inner_b",
)
VEC = {name: place for place, name in enumerate(VEC_NAMES)}

VMEM_LIMIT = 58 * 1024 * 1024


def dot(a, b):
    return jnp.dot(a, b, preferred_element_type=f32)


def dot_nt(a, b):
    return lax.dot_general(a, b, (((1,), (1,)), ((), ())), preferred_element_type=f32)


def dot_tn(a, b):
    return lax.dot_general(a, b, (((0,), (0,)), ((), ())), preferred_element_type=f32)


def column_sum(matrix):
    return jnp.sum(matrix.astype(f32), axis=0, keepdims=True)


def normalize(values):
    centered = values - jnp.mean(values, axis=-1, keepdims=True)
    root = lax.rsqrt(jnp.mean(centered * centered, axis=-1, keepdims=True) + EPSILON)
    return centered * root, root


def normalize_back(grad, normal, root, gain):
    scaled = grad * gain
    first = jnp.mean(scaled, axis=-1, keepdims=True)
    second = jnp.mean(scaled * normal, axis=-1, keepdims=True)
    return root * (scaled - first - normal * second)


CHIP_ROWS = 584
CORE_ROWS = 292
UNIT = 592
UNITS = 16


def unit_begin(unit):
    return 2 * CHIP_ROWS * (unit // 2) + UNIT * (unit % 2)


def unit_parts(begin, rows):
    parts = []
    for unit in range(UNITS):
        low = max(begin, unit_begin(unit))
        high = min(begin + rows, unit_begin(unit + 1))
        if low < high:
            parts.append((unit, low - unit_begin(unit), low - begin, high - low))
    return parts


SUM_UNIT = 608


def own_parts(begin, rows):
    parts = []
    for unit in range(UNITS):
        low = max(begin, CHIP_ROWS * unit)
        high = min(begin + rows, CHIP_ROWS * (unit + 1))
        if low < high:
            parts.append((unit, low - CHIP_ROWS * unit, low - begin, high - low))
    return parts


def group_of(unit):
    return min(unit // 4, 2)


class Place:
    def __init__(self, bounds=None):
        if bounds is not None:
            self.token_bounds = [bounds[i] for i in range(3)]
            self.memory_bounds = [bounds[3 + i] for i in range(3)]
        wide, narrow = lax.axis_index("wide"), lax.axis_index("narrow")
        self.z, self.x = lax.div(wide, 2), lax.rem(wide, 2)
        self.y, self.core = lax.div(narrow, 2), lax.rem(narrow, 2)

    def turned(self, unit):
        z, x, y = unit // 4, unit // 2 % 2, unit % 2
        low = jnp.bitwise_xor(lax.rem(self.z, 2), z % 2) if group_of(unit) == 2 else 0
        return jnp.bitwise_xor(self.x, x), jnp.bitwise_xor(self.y, y), low


class Units:
    count = 8

    def __init__(self, groups, refs):
        self.groups = {
            group: (refs[8 * i : 8 * i + 4], refs[8 * i + 4 : 8 * i + 8])
            for i, group in enumerate(groups)
        }

    def load(self, place, begin, buffer, sem):
        return self.load_parts(place, unit_parts(begin, buffer.shape[0]), buffer, sem)

    def load_vectors(self, place, buffer, sem):
        return self.load_parts(place, [(3, UNIT - 16, 0, 16)], buffer, sem)

    def load_parts(self, place, parts, buffer, sem):
        copies = []
        for unit, source, target, rows in parts:
            halves = self.groups[group_of(unit)]
            far_x, far_y, low = place.turned(unit)
            targets = [
                [
                    buffer.at[
                        pl.ds(target, rows),
                        pl.ds(
                            pl.multiple_of(
                                (jnp.bitwise_xor(place.core, half) * 2 + quarter) * 128, 128
                            ),
                            128,
                        ),
                    ]
                    for quarter in range(2)
                ]
                for half in range(2)
            ]

            def part(half, which, quarter):
                return halves[half][which].at[low, quarter, pl.ds(source, rows), :]

            for which in range(4):

                @pl.when((far_x == which % 2) & (far_y == which // 2))
                def _():
                    for half in range(2):
                        for quarter in range(2):
                            pltpu.make_async_copy(
                                part(half, which, quarter), targets[half][quarter], sem
                            ).start()

            copies += [
                pltpu.make_async_copy(part(half, 0, quarter), targets[half][quarter], sem)
                for half in range(2)
                for quarter in range(2)
            ]
        return copies


class Pieces:
    count = 4

    def __init__(self, groups, refs):
        self.refs = refs[:4]

    def load(self, place, begin, buffer, sem):
        copies = []
        for i, ref in enumerate(self.refs):
            copy = pltpu.make_async_copy(
                ref.at[pl.ds(begin, buffer.shape[0]), :],
                buffer.at[:, i * 128 : (i + 1) * 128],
                sem,
            )
            copy.start()
            copies.append(copy)
        return copies

    def load_vectors(self, place, buffer, sem):
        return self.load(place, ROW_VEC, buffer, sem)


def wait_all(copies):
    for copy in copies:
        copy.wait()


def vector(vec_ref, name):
    return vec_ref[VEC[name] : VEC[name] + 1, :].astype(f32)


class UnitSink:
    def __init__(self, pairs):
        self.pairs = pairs

    def places(self, place, begin, rows):
        for unit, at, source, count in own_parts(begin, rows):
            if unit in self.pairs:
                yield self.pairs[unit].ref, (), at, source, count
            elif group_of(unit) + 100 in self.pairs:
                far_x, far_y, low = place.turned(unit)
                yield self.pairs[group_of(unit) + 100].ref, (far_x + 2 * far_y, low), at, source, count

    def send(self, place, units):
        for unit in units:
            far_x, far_y, low = place.turned(unit)
            self.pairs[group_of(unit) + 100].send(far_x + 2 * far_y, low)

    def vector_places(self, place):
        far_x, far_y, low = place.turned(3)
        yield self.pairs[100].ref, (far_x + 2 * far_y, low), CHIP_ROWS, 0, 16


class RowSink:
    def __init__(self, pair, first):
        self.ref = pair.ref
        self.first = first

    def send(self, place, units):
        pass

    def places(self, place, begin, rows):
        yield self.ref, (), begin - self.first, 0, rows

    def vector_places(self, place):
        yield self.ref, (), 2048, 0, 16


def put_grad(sink, place, begin, value):
    put_places(place, sink.places(place, begin, value.shape[0]), value)


def put_places(place, places, value):
    for ref, lead, at, source, count in places:
        low = value[source : source + count, :].astype(bf16)
        for i in range(4):
            kept = 1 - jnp.bitwise_xor(place.core, i // 2)
            ref[(kept, *lead, i % 2, pl.ds(at, count), slice(None))] = low[:, lanes(i)]


def segment_of(position, bounds):
    return sum([(position >= bound).astype(jnp.int32) for bound in bounds])


def pick(index, choices):
    value = choices[-1]
    for place in range(len(choices) - 2, -1, -1):
        value = jnp.where(index == place, choices[place], value)
    return value


def key_range(first_query, query_bounds, key_bounds, length):
    low = segment_of(first_query, query_bounds)
    high = segment_of(first_query + (QB - 1), query_bounds)
    begin = pick(low, [0, *key_bounds]) // 128
    end = (pick(high, [*key_bounds, length]) + 127) // 128
    return begin * 128, end - begin


def query_marks(first_query, bounds):
    position = first_query + lax.broadcasted_iota(jnp.int32, (QB, 128), 0)
    lane = lax.broadcasted_iota(jnp.int32, (QB, 128), 1)
    hidden = (lane <= len(bounds)) & (lane != segment_of(position, bounds))
    return jnp.where(hidden, BIG, 0.0).astype(bf16)


def key_marks(length, bounds):
    position = lax.broadcasted_iota(jnp.int32, (length, 128), 0)
    lane = lax.broadcasted_iota(jnp.int32, (length, 128), 1)
    return jnp.where(lane == segment_of(position, bounds), 1.0, 0.0).astype(bf16)


def stack_heads(pair):
    lane = lax.broadcasted_iota(jnp.int32, pair.shape, 1)
    nothing = jnp.zeros_like(pair)
    return jnp.concatenate(
        [jnp.where(lane < HD, pair, nothing), jnp.where(lane >= HD, pair, nothing)], axis=0
    )


def by_count(count, most, body):
    for value in range(1, most + 1):

        @pl.when(count == value)
        def _():
            body(value)


def lanes(pair):
    return slice(pair * 128, (pair + 1) * 128)


def marked_keys(k_ref, kx, key_bounds):
    marks = key_marks(k_ref.shape[0], key_bounds)
    for pair in range(PAIRS):
        kx[pair, :, 0:128] = k_ref[:, lanes(pair)]
        kx[pair, :, 128:256] = marks


def attend(q_ref, kx, vt, ot_ref, o_ref, lse_ref, query_bounds, key_bounds):
    length = kx.shape[1]

    def block(index, carry):
        first = pl.multiple_of(index * QB, QB)
        begin, count = key_range(first, query_bounds, key_bounds, length)
        begin = pl.multiple_of(begin, 128)
        queries = pl.ds(first, QB)
        marks = query_marks(first, query_bounds)
        marks = jnp.concatenate([marks, marks], axis=0)

        def run(blocks):
            keys = pl.ds(begin, 128 * blocks)
            scores = []
            for pair in range(PAIRS):
                wide = jnp.concatenate([stack_heads(q_ref[queries, lanes(pair)]), marks], axis=1)
                scores.append(dot_nt(kx[pair, keys, :], wide))
            tops = []
            probs = []
            for pair in range(PAIRS):
                top = jnp.max(scores[pair], axis=0, keepdims=True)
                tops.append(top)
                probs.append(jnp.exp2(scores[pair] - top).astype(bf16))
            mixed = [dot(vt[pair, :, keys], probs[pair]) for pair in range(PAIRS)]
            for pair in range(PAIRS):
                total = mixed[pair][128:129, :]
                scale = 1.0 / total
                lse = tops[pair] + jnp.log2(total)
                one = mixed[pair][0:64, 0:128] * scale[:, 0:128]
                two = mixed[pair][64:128, 128:256] * scale[:, 128:256]
                out = jnp.concatenate([one, two], axis=0)
                ot_ref[lanes(pair), queries] = out.astype(bf16)
                o_ref[queries, lanes(pair)] = out.T.astype(bf16)
                lse_ref[2 * pair : 2 * pair + 1, queries] = lse[:, 0:128]
                lse_ref[2 * pair + 1 : 2 * pair + 2, queries] = lse[:, 128:256]

        by_count(count, length // 128, run)
        return carry

    lax.fori_loop(0, q_ref.shape[0] // QB, block, 0)


def attend_back(
    q_ref, kx, kt, v_ref, do_ref, lse_ref, dq_ref, dk_sum, dv_sum, query_bounds, key_bounds
):
    length = kx.shape[1]
    dk_sum[...] = jnp.zeros_like(dk_sum)
    dv_sum[...] = jnp.zeros_like(dv_sum)

    def block(index, carry):
        first = pl.multiple_of(index * QB, QB)
        begin, count = key_range(first, query_bounds, key_bounds, length)
        begin = pl.multiple_of(begin, 128)
        queries = pl.ds(first, QB)
        marks = query_marks(first, query_bounds)
        marks = jnp.concatenate([marks, marks], axis=0)

        def run(blocks):
            keys = pl.ds(begin, 128 * blocks)

            def products(pair):
                q_two = stack_heads(q_ref[queries, lanes(pair)])
                do_two = stack_heads(do_ref[queries, lanes(pair)])
                scores = dot_nt(kx[pair, keys, :], jnp.concatenate([q_two, marks], axis=1))
                grad_probs = dot_nt(v_ref[keys, lanes(pair)], do_two)
                return q_two, do_two, scores, grad_probs

            def gradients(pair):
                _, _, scores, grad_probs = ready[pair]
                lse = jnp.concatenate(
                    [
                        lse_ref[2 * pair : 2 * pair + 1, queries],
                        lse_ref[2 * pair + 1 : 2 * pair + 2, queries],
                    ],
                    axis=1,
                )
                probs = jnp.exp2(scores - lse)
                both = probs * grad_probs
                delta = jnp.sum(both, axis=0, keepdims=True)
                return (both - probs * delta).astype(bf16), probs.astype(bf16)

            ready = {pair: products(pair) for pair in (0, 1)}
            made = {0: gradients(0)}
            for pair in range(PAIRS):
                if pair + 2 < PAIRS:
                    ready[pair + 2] = products(pair + 2)
                if pair + 1 < PAIRS:
                    made[pair + 1] = gradients(pair + 1)
                q_two, do_two = ready[pair][:2]
                grad_scores, probs = made[pair]
                dqt = dot(kt[lanes(pair), keys], grad_scores)
                dk_sum[keys, lanes(pair)] += dot(grad_scores, q_two)
                dv_sum[keys, lanes(pair)] += dot(probs, do_two)
                dq = jnp.concatenate([dqt[0:64, 0:128], dqt[64:128, 128:256]], axis=0)
                dq_ref[queries, lanes(pair)] = (dq * HD ** (-0.5)).T.astype(bf16)

        by_count(count, length // 128, run)
        return carry

    lax.fori_loop(0, q_ref.shape[0] // QB, block, 0)


def values_transposed(v_ref, vt):
    for pair in range(PAIRS):
        vt[pair, 0:128, :] = v_ref[:, lanes(pair)].T
        vt[pair, 128:144, :] = jnp.ones((16, vt.shape[2]), bf16)


def four(values):
    return jnp.concatenate([values] * 4, axis=1)


def rows_of(w, i):
    return w[i * D : (i + 1) * D, :]


def add_out(r, x, o, w, bias):
    tile = 256
    for t in range(o.shape[0] // tile):
        rows = slice(t * tile, (t + 1) * tile)
        r.ref[rows, :] = x[rows, :].astype(f32) + dot(o[rows, :], w) + bias
        r.send(pl.ds(t * tile, tile))


def self_forward(source, scalars, x, *rest):
    (q, k, v, ot, lse, r, wq, wk, wv, wo, vec, kx, vt, o, sems) = rest[source.count_all :]
    place = Place(scalars)
    weights = source(rest)
    start(x)
    k_copies = weights.load(place, ROW_K, wk, sems.at[0])
    q_copies = weights.load(place, ROW_Q, wq, sems.at[1])
    q_copies += weights.load_vectors(place, vec, sems.at[1])
    v_copies = weights.load(place, ROW_V, wv, sems.at[2])
    x = x.get()
    wait_all(k_copies)
    k.ref[...] = dot(x[...], wk[...]).astype(bf16)
    k.send()
    wait_all(q_copies)
    q.ref[...] = ((dot(x[...], wq[...]) + vector(vec, "query_b")) * Q_SCALE).astype(bf16)
    q.send()
    wait_all(v_copies)
    v.ref[...] = (dot(x[...], wv[...]) + vector(vec, "value_b")).astype(bf16)
    v.send()
    o_copies = weights.load(place, ROW_O, wo, sems.at[0])
    bounds = place.token_bounds
    marked_keys(k.ref, kx, bounds)
    values_transposed(v.ref, vt)
    attend(q.ref, kx, vt, ot.ref, o, lse.ref, bounds, bounds)
    ot.send()
    wait_all(o_copies)
    add_out(r, x, o, wo[...], vector(vec, "out_b"))


def cross_forward(source, scalars, m, r1, *rest):
    (q, k, v, ot, lse, r, wq, wk, wv, wo, vec, kx, vt, o, h, sems) = rest[source.count_all :]
    place = Place(scalars)
    weights = source(rest)
    start(m)
    k_copies = weights.load(place, ROW_CK, wk, sems.at[0])
    v_copies = weights.load(place, ROW_CV, wv, sems.at[1])
    v_copies += weights.load_vectors(place, vec, sems.at[1])
    m = m.get()
    wait_all(k_copies)
    start(r1)
    q_copies = weights.load(place, ROW_CQ, wq, sems.at[2])
    k.ref[...] = dot(m[...], wk[...]).astype(bf16)
    k.send()
    wait_all(v_copies)
    v.ref[...] = (dot(m[...], wv[...]) + vector(vec, "cross_value_b")).astype(bf16)
    v.send()
    o_copies = weights.load(place, ROW_CO, wo, sems.at[0])
    r1 = r1.get()
    h[...] = normalize(r1[...])[0] * vector(vec, "gain_one") + vector(vec, "shift_one")
    wait_all(q_copies)
    q.ref[...] = (
        (dot(h[...].astype(bf16), wq[...]) + vector(vec, "cross_query_b")) * Q_SCALE
    ).astype(bf16)
    q.send()
    marked_keys(k.ref, kx, place.memory_bounds)
    values_transposed(v.ref, vt)
    attend(q.ref, kx, vt, ot.ref, o, lse.ref, place.token_bounds, place.memory_bounds)
    ot.send()
    wait_all(o_copies)
    add_out(r, h, o, wo[...], vector(vec, "cross_out_b"))


def gelu_parts(x):
    scale = math.sqrt(2.0 / math.pi)
    square = x * x
    half = 0.5 + 0.5 * jnp.tanh(x * (scale + (scale * 0.044715) * square))
    value = x * half
    slope = half + value * (1.0 - half) * (2.0 * scale + (6.0 * scale * 0.044715) * square)
    return value, slope


def same_next(first, rows, bounds, length):
    later = first + 1 + lax.broadcasted_iota(jnp.int32, (rows, 128), 0)
    same = later != length
    for bound in bounds:
        same = same & (later != bound)
    return same.astype(f32)


def prepare(source, scalars, mask_in, cot_in, r2_in, *rest):
    (gs, gs2, h2, vec, mask, spread, sems) = rest[source.count_all :]
    place = Place(scalars)
    start(mask_in, cot_in, r2_in)
    copies = source(rest).load_vectors(place, vec, sems.at[0])
    bounds = place.token_bounds
    length = h2.ref.shape[0]
    tile = 256
    mask[...] = jnp.broadcast_to(mask_in.get()[...].astype(f32), (128, length)).T
    cot_ref = cot_in.get()
    spread[0:8, :] = jnp.zeros((8, D), f32)
    for t in range(length // tile):
        rows = slice(t * tile, (t + 1) * tile)
        part = cot_ref[rows, :].astype(f32) * four(mask[rows, :])
        gs.ref[rows, :] = part.astype(bf16)
        same = same_next(t * tile, tile, bounds, length)
        spread[8 + t * tile : 8 + (t + 1) * tile, :] = part * four(same)
        gs2.ref[rows, :] = spread[7 + t * tile : 7 + (t + 1) * tile, :].astype(bf16)
    gs.send()
    gs2.send()
    wait_all(copies)
    h2.ref[...] = normalize(r2_in.get()[...])[0] * vector(vec, "gain_two") + vector(vec, "shift_two")


def ffn(source, make_sink, scalars, h2_in, gs_in, gs2_in, r2_in, *rest):
    rest_ = rest[source.count_all :]
    hlow_out, gr2 = rest_[:2]
    hlow, gr2_ref = hlow_out.ref, gr2.ref
    count = make_sink.count
    sink = make_sink(rest_[2 : 2 + count])
    (w_in, w_raw, w_out, w_slot, vec, comb, act, slope, h3, gf, gr3, h2b, gv_ref, sems) = rest_[
        2 + count :
    ]
    place = Place(scalars)
    weights = source(rest)
    in_copies = weights.load(place, ROW_IN, w_raw, sems.at[0])
    in_copies += weights.load(place, ROW_VEC, vec, sems.at[0])
    start(h2_in)
    length = gr2_ref.shape[0]
    tile = 256
    tiles = length // tile
    gv_ref[...] = jnp.zeros_like(gv_ref)

    def add_vector(name, value, at=0):
        at = VEC[name] + at
        gv_ref[at : at + 1, :] += value

    wait_all(in_copies)
    for i in range(4):
        comb[i] = w_raw[:, lanes(i)].astype(f32)
        for c in range(4):
            w_in[c, :, lanes(i)] = comb[i, pl.ds(c, D, 4), :].astype(bf16)
    out_copies = weights.load(place, ROW_OUT, w_out, sems.at[1])
    h2_ref = h2_in.get()
    slot_copies = weights.load(place, ROW_SLOT, w_slot, sems.at[2])
    start(gs_in, gs2_in, r2_in)
    biases = [vec[VEC["inner_b"] + c : VEC["inner_b"] + c + 1, :].astype(f32) for c in range(4)]

    def inner(t, c):
        rows = slice(t * tile, (t + 1) * tile)
        if c == 0:
            h2b[rows, :] = h2_ref[rows, :].astype(bf16)
        return dot(h2b[rows, :], w_in[c]) + biases[c]

    steps = [(t, c) for t in range(tiles) for c in range(4)]
    ahead = inner(*steps[0])
    wait_all(out_copies)
    for place_in, (t, c) in enumerate(steps):
        pre = ahead
        if place_in + 1 < len(steps):
            ahead = inner(*steps[place_in + 1])
        rows = slice(t * tile, (t + 1) * tile)
        value, gate = gelu_parts(pre)
        act[rows, c * D : (c + 1) * D] = value.astype(bf16)
        slope[rows, c * D : (c + 1) * D] = gate.astype(bf16)
        if c == 3:
            h3[rows, :] = h2_ref[rows, :] + dot(act[rows, :], w_out[...]) + vector(vec, "outer_b")
    wait_all(slot_copies)
    gs, gs2, r2_ref = gs_in.get(), gs2_in.get(), r2_in.get()

    def slot_grad(t):
        rows = slice(t * tile, (t + 1) * tile)
        return dot_nt(gs[rows, :], w_slot[0:D, :]) + dot_nt(gs2[rows, :], w_slot[D : 2 * D, :])

    ahead = slot_grad(0)
    for t in range(tiles):
        rows = slice(t * tile, (t + 1) * tile)
        grad = ahead
        if t + 1 < tiles:
            ahead = slot_grad(t + 1)
        normal, root = normalize(h3[rows, :])
        out = normal * vector(vec, "gain_three") + vector(vec, "shift_three")
        hlow[rows, :] = out.astype(bf16)
        add_vector("gain_three", column_sum(grad * normal))
        add_vector("shift_three", column_sum(grad))
        gr3[rows, :] = normalize_back(grad, normal, root, vector(vec, "gain_three"))
    hlow_out.send()
    add_vector("slot_b", column_sum(gs[...]))
    put_grad(sink, place, ROW_SLOT, dot_tn(hlow[...], gs[...]))
    put_grad(sink, place, ROW_SLOT + D, dot_tn(hlow[...], gs2[...]))
    gf[...] = gr3[...].astype(bf16)
    add_vector("outer_b", column_sum(gf[...]))
    for c in range(4):
        put_grad(sink, place, ROW_OUT + c * D, dot_tn(act[:, c * D : (c + 1) * D], gf[...]))
    sink.send(place, range(11, 15))

    def active(t, c):
        return dot_nt(gf[t * tile : (t + 1) * tile, :], w_out[c * D : (c + 1) * D, :])

    ahead = active(0, 0)
    for place_in, (t, c) in enumerate(steps):
        rows, at = slice(t * tile, (t + 1) * tile), slice(c * D, (c + 1) * D)
        grad = ahead.astype(bf16)
        if place_in + 1 < len(steps):
            ahead = active(*steps[place_in + 1])
        pre = (grad.astype(f32) * slope[rows, at].astype(f32)).astype(bf16)
        slope[rows, at] = pre
        add_vector("inner_b", column_sum(pre), c)
        part = dot_nt(pre, w_in[c])
        total = gr3[rows, :] + part if c == 0 else total + part
        if c == 3:
            normal, root = normalize(r2_ref[rows, :])
            add_vector("gain_two", column_sum(total * normal))
            add_vector("shift_two", column_sum(total))
            gr2_ref[rows, :] = normalize_back(total, normal, root, vector(vec, "gain_two"))
    gr2.send()
    put_grad(sink, place, ROW_VEC, gv_ref[...])
    sink.send(place, [15])
    for c in range(4):
        part = dot_tn(h2b[...], slope[:, c * D : (c + 1) * D])
        for i in range(4):
            comb[i, pl.ds(c, D, 4), :] = part[:, lanes(i)]
    put_grad(sink, place, ROW_IN, jnp.concatenate([comb[i] for i in range(4)], axis=1))
    sink.send(place, range(8, 11))


def slot_forward(source, scalars, mask_in, hlow_in, *rest):
    (slots, w, vec, spread, mask, sems) = rest[source.count_all :]
    place = Place(scalars)
    weights = source(rest)
    copies = weights.load(place, ROW_SLOT, w, sems.at[0])
    copies += weights.load(place, ROW_VEC, vec, sems.at[0])
    start(mask_in, hlow_in)
    hlow = hlow_in.get()
    length = hlow.shape[0]
    tile = 256
    mask[...] = jnp.broadcast_to(mask_in.get()[...].astype(f32), (128, length)).T
    spread[0:length, :] = hlow[...].astype(f32)
    spread[length : length + 8, :] = jnp.zeros((8, D), f32)
    wait_all(copies)
    for t in range(length // tile):
        rows = slice(t * tile, (t + 1) * tile)
        later = spread[t * tile + 1 : (t + 1) * tile + 1, :]
        same = four(same_next(t * tile, tile, place.token_bounds, length))
        raw = (
            dot(hlow[rows, :], w[0:D, :])
            + dot((later * same).astype(bf16), w[D : 2 * D, :])
            + vector(vec, "slot_b")
        )
        slots.ref[rows, :] = (four(mask[rows, :]) * raw).astype(bf16)
        slots.send(pl.ds(t * tile, tile))


def attend_backward(place, key_bounds, w, gr_low, v_in, q_in, lse_in, dq, dk, dv, scratch,
                    later):
    (kx, kt, dk_sum, dv_sum, do) = scratch
    do[...] = dot_nt(gr_low[...], w).astype(bf16)
    v_ref, q_ref, lse_ref = v_in.get(), q_in.get(), lse_in.get()
    start(*later)
    attend_back(
        q_ref, kx, kt, v_ref, do, lse_ref, dq.ref, dk_sum, dv_sum, place.token_bounds, key_bounds
    )
    dk.ref[...] = (dk_sum[...] * (1.0 / LOG2E)).astype(bf16)
    dv.ref[...] = dv_sum[...].astype(bf16)
    for out in (dq, dk, dv):
        if isinstance(out, Out):
            out.send()


def keys_ready(place, key_bounds, k_in, kx, kt):
    k_ref = k_in.get()
    marked_keys(k_ref, kx, key_bounds)
    for pair in range(PAIRS):
        kt[lanes(pair), :] = k_ref[:, lanes(pair)].T


class Held:
    def __init__(self, ref):
        self.ref = ref


def cross_backward(source, make_sink, scalars, k_in, gr2_in, v_in, q_in, lse_in, ot_in, r1_in, m_in,
                   *rest):
    passed = rest[source.count_all : source.count_all + make_sink.passed]
    rest_ = rest[source.count_all + make_sink.passed :]
    dk, dv, gr1, gv = rest_[:4]
    count = make_sink.count
    sink = make_sink(rest_[4 : 4 + count])
    (wq, wo, vec, grad, h, dq, *scratch, sems) = rest_[4 + count :]
    place = Place(scalars)
    weights = source(rest)
    start(k_in, gr2_in)
    o_copies = weights.load(place, ROW_CO, wo, sems.at[0])
    keys_ready(place, place.memory_bounds, k_in, *scratch[:2])
    start(v_in, q_in, lse_in)
    q_copies = weights.load(place, ROW_CQ, wq, sems.at[1])
    q_copies += weights.load_vectors(place, vec, sems.at[1])
    gv.ref[...] = jnp.zeros_like(gv.ref)

    def set_vector(name, value):
        gv.ref[VEC[name] : VEC[name] + 1, :] = value

    gr2_ref = gr2_in.get()
    grad[...] = gr2_ref[...].astype(bf16)
    wait_all(o_copies)
    attend_backward(
        place, place.memory_bounds, wo[...], grad, v_in, q_in, lse_in, Held(dq), dk, dv, scratch,
        [r1_in, ot_in, m_in, *passed],
    )
    set_vector("cross_out_b", column_sum(grad[...]))
    ot_ref, r1_ref = ot_in.get(), r1_in.get()
    wait_all(q_copies)
    normal, root = normalize(r1_ref[...])
    gain = vector(vec, "gain_one")
    h[...] = (normal * gain + vector(vec, "shift_one")).astype(bf16)
    total = gr2_ref[...] + dot_nt(dq[...], wq[...])
    set_vector("gain_one", column_sum(total * normal))
    set_vector("shift_one", column_sum(total))
    gr1.ref[...] = normalize_back(total, normal, root, gain)
    gr1.send()
    make_sink.pass_on(sink, place, passed)
    m_ref = m_in.get()
    put_grad(sink, place, ROW_CO, dot(ot_ref[...], grad[...]))
    put_grad(sink, place, ROW_CV, dot_tn(m_ref[...], dv.ref[...]))
    sink.send(place, [6, 7])
    set_vector("cross_value_b", column_sum(dv.ref[...]))
    put_grad(sink, place, ROW_CK, dot_tn(m_ref[...], dk.ref[...]))
    sink.send(place, [5])
    put_grad(sink, place, ROW_CQ, dot_tn(h[...], dq[...]))
    sink.send(place, [4])
    set_vector("cross_query_b", column_sum(dq[...]))


def memory_gradient(source, scalars, dk_in, dv_in, *rest):
    (mgrad, w, sems) = rest[source.count_all :]
    copies = source(rest).load(Place(), ROW_CK, w, sems.at[0])
    start(dk_in, dv_in)
    dk, dv = dk_in.get(), dv_in.get()
    wait_all(copies)
    tile = 256
    for t in range(dk.shape[0] // tile):
        rows = slice(t * tile, (t + 1) * tile)
        value = dot_nt(dk[rows, :], rows_of(w, 0)) + dot_nt(dv[rows, :], rows_of(w, 1))
        mgrad.ref[rows, :] = value.astype(bf16)
        mgrad.send(pl.ds(t * tile, tile))


def self_backward(source, make_sink, scalars, k_in, gr1_in, v_in, q_in, lse_in, ot_in, x_in, gv_in,
                  *rest):
    passed = rest[source.count_all : source.count_all + make_sink.passed]
    rest_ = rest[source.count_all + make_sink.passed :]
    dq, dk, dv = rest_[:3]
    count = make_sink.count
    sink = make_sink(rest_[3 : 3 + count])
    (w, grad, gv, *scratch, sems) = rest_[3 + count :]
    place = Place(scalars)
    start(k_in, gr1_in)
    copies = source(rest).load(place, ROW_O, w, sems.at[0])
    keys_ready(place, place.token_bounds, k_in, *scratch[:2])
    start(v_in, q_in, lse_in)
    gr1_ref = gr1_in.get()
    grad[...] = gr1_ref[...].astype(bf16)
    wait_all(copies)
    attend_backward(
        place, place.token_bounds, w[...], grad, v_in, q_in, lse_in, dq, dk, dv, scratch,
        [ot_in, x_in, gv_in, *passed],
    )
    ot_ref, x_ref = ot_in.get(), x_in.get()
    gv[...] = gv_in.get()[...]

    def set_vector(name, value):
        gv[VEC[name] : VEC[name] + 1, :] = value

    make_sink.pass_on(sink, place, passed)
    put_grad(sink, place, ROW_O, dot(ot_ref[...], grad[...]))
    set_vector("out_b", column_sum(grad[...]))
    put_grad(sink, place, ROW_V, dot_tn(x_ref[...], dv.ref[...]))
    sink.send(place, [2])
    set_vector("value_b", column_sum(dv.ref[...]))
    set_vector("query_b", column_sum(dq.ref[...]))
    put_places(place, sink.vector_places(place), gv[...])
    sink.send(place, [3])
    put_grad(sink, place, ROW_K, dot_tn(x_ref[...], dk.ref[...]))
    sink.send(place, [1])
    put_grad(sink, place, ROW_Q, dot_tn(x_ref[...], dq.ref[...]))
    sink.send(place, [0])


def token_gradient(source, scalars, dq_in, dk_in, dv_in, gr1_in, *rest):
    (tgrad, w, sems) = rest[source.count_all :]
    copies = source(rest).load(Place(), ROW_Q, w, sems.at[0])
    start(dq_in, dk_in, dv_in, gr1_in)
    dq, dk, dv, gr1_ref = dq_in.get(), dk_in.get(), dv_in.get(), gr1_in.get()
    wait_all(copies)
    tile = 256
    for t in range(dq.shape[0] // tile):
        rows = slice(t * tile, (t + 1) * tile)
        tgrad.ref[rows, :] = (
            gr1_ref[rows, :]
            + dot_nt(dq[rows, :], rows_of(w, 0))
            + dot_nt(dk[rows, :], rows_of(w, 1))
            + dot_nt(dv[rows, :], rows_of(w, 2))
        ).astype(bf16)
        tgrad.send(pl.ds(t * tile, tile))


def find_bounds(segments_ref, lengths_ref, out_ref):
    segments = segments_ref[...]
    before = jnp.int32(0)
    for i in range(3):
        out_ref[i] = jnp.sum((segments <= i).astype(jnp.int32))
        before = before + lengths_ref[0, i]
        out_ref[3 + i] = before


PAD_ROWS = 304
VEC_AT = ROW_VEC - 31 * CORE_ROWS


def split_shard(slab_ref, keep_ref, send_ref, one_ref, two_ref, full):
    place = Place()
    rows = slab_ref.shape[0]
    full[0:rows, :] = slab_ref[...].astype(f32)
    full[rows : 4 * PAD_ROWS, :] = jnp.zeros((4 * PAD_ROWS - rows, 128), f32)
    for i in range(4):
        part = full[pl.ds(i, PAD_ROWS, 4), :].astype(bf16)
        few_ref = (one_ref, two_ref)[i // 2]
        for core in range(2):

            @pl.when(place.core == core)
            def _():
                (keep_ref if i // 2 == core else send_ref)[i % 2] = part
                first = core * VEC_AT
                few_ref[i % 2] = full[pl.ds(4 * first + i, 16, 4), :].astype(bf16)


def join_unit(_, keep_ref, got_ref, one_ref, two_ref, unit_ref, full):
    place = Place()
    for i in range(2):
        for core in range(2):

            @pl.when(place.core == core)
            def _():
                first, second = (keep_ref, got_ref) if core == 0 else (got_ref, keep_ref)
                full[0:PAD_ROWS, :] = first[i].astype(f32)
                full[CORE_ROWS : CORE_ROWS + PAD_ROWS, :] = second[i].astype(f32)

        ends = one_ref[i].astype(f32) + two_ref[i].astype(f32)
        full[CHIP_ROWS : CHIP_ROWS + 16, :] = ends

        @pl.when(place.y == 0)
        def _():
            unit_ref[0, i] = full[0:UNIT, :].astype(bf16)

        @pl.when(place.y == 1)
        def _():
            unit_ref[0, i, 0:576, :] = full[8:CHIP_ROWS, :].astype(bf16)
            unit_ref[0, i, 576:UNIT, :] = ends.astype(bf16)


def split_unit(here0, across0, mixed1, rest, mixed23, keep, send, far_keep, far_send, vec, full):
    place = Place()
    for i in range(2):
        plane0 = here0[i].astype(f32) + across0[i].astype(f32)

        def rows(core):
            return full[CORE_ROWS * core : CORE_ROWS * core + PAD_ROWS, :]

        full[...] = plane0
        vec[i] = plane0[CHIP_ROWS : CHIP_ROWS + 16, :]
        for core in range(2):

            @pl.when(place.core == core)
            def _():
                far_keep[i] = rows(core).astype(bf16)
                far_send[i] = rows(1 - core).astype(bf16)

        for mixed, chosen in ((mixed1, place.z == 1), (mixed23, place.z >= 2)):

            @pl.when(chosen)
            def _():
                full[...] = mixed[i].astype(f32) + rest[i].astype(f32)

        for core in range(2):

            @pl.when(place.core == core)
            def _():
                keep[i] = rows(core)
                send[i] = rows(1 - core)

        @pl.when(place.z == 0)
        def _():
            far_keep[i, 0:16, :] = vec[i].astype(bf16)
            far_send[i, 0:16, :] = vec[i].astype(bf16)


def join_shard(keep, got, far_keep, far_got, one, two, out_ref, full):
    place = Place()
    rows = out_ref.shape[0]
    last = (place.core == 1) & (place.y == 1) & (place.x == 1) & (place.z == 3)
    for i in range(4):
        for core in range(2):

            @pl.when(place.core == core)
            def _():
                part, far = (keep, far_keep) if i // 2 == core else (got, far_got)
                full[pl.ds(i, PAD_ROWS, 4), :] = part[i % 2]

                @pl.when(place.z == 0)
                def _():
                    full[pl.ds(i, PAD_ROWS, 4), :] = part[i % 2] + far[i % 2].astype(f32)

        @pl.when(last)
        def _():
            at = pl.ds(4 * VEC_AT + i, 16, 4)
            near = (far_got, far_keep)[i // 2]
            full[at, :] = (
                full[at, :] + near[i % 2, 0:16, :].astype(f32) + (one, two)[i // 2][i % 2]
            )

    out_ref[...] = full[0:rows, :]


WHOLE = pl.BlockSpec(memory_space=pltpu.VMEM)


class In:
    def __init__(self, source, buffer, sem):
        self.buffer = buffer
        self.copy = pltpu.make_async_copy(source, buffer, sem)
        self.started = False

    def start(self):
        self.copy.start()
        self.started = True

    def get(self):
        if not self.started:
            self.start()
        self.copy.wait()
        return self.buffer


def start(*arrays):
    for array in arrays:
        array.start()


class Out:
    def __init__(self, target, ref, sem):
        self.target, self.ref, self.sem = target, ref, sem
        self.copies = []

    def send(self, *index):
        source, target = (self.ref.at[index], self.target.at[index]) if index else (self.ref, self.target)
        copy = pltpu.make_async_copy(source, target, self.sem)
        copy.start()
        self.copies.append(copy)

    def finish(self):
        if not self.copies:
            self.send()
        wait_all(self.copies)


class Pair:
    def __init__(self, send, keep, ref, sem):
        self.ref = ref
        self.results = [Out(send, ref.at[0], sem), Out(keep, ref.at[1], sem)]

    def send(self, *index):
        for result in self.results:
            result.send(*index)

    def finish(self):
        for result in self.results:
            result.finish()


def call(body, name, scalars, blocks, weights, outs, scratch, microseconds, passed=(), after=(),
         pairs=()):
    ins = [*blocks, *passed]
    single = len(outs)
    buffers = [pltpu.VMEM(v.shape, v.dtype) for v in ins] + [pltpu.VMEM(s, t) for s, t in outs]
    buffers += [pltpu.VMEM((2, *s), bf16) for s in pairs]
    outs = [*outs, *[(s, bf16) for s in pairs for _ in range(2)]]
    sems = [pltpu.SemaphoreType.DMA((len(ins),))]
    sems.append(pltpu.SemaphoreType.DMA((single + len(pairs),)))

    def run(*refs):
        refs = list(refs)
        take = lambda n: [refs.pop(0) for _ in range(n)]
        scalars_ref, *in_refs = take(1 + len(ins))
        weight_refs, _, out_refs = take(len(weights)), take(len(after)), take(len(outs))
        in_buffers, out_buffers = take(len(ins)), take(single + len(pairs))
        in_sems, out_sems = take(2)
        arrays = [In(in_refs[i], in_buffers[i], in_sems.at[i]) for i in range(len(ins))]
        results = [Out(out_refs[i], out_buffers[i], out_sems.at[i]) for i in range(single)]
        for i in range(len(pairs)):
            send, keep = out_refs[single + 2 * i : single + 2 * i + 2]
            at = single + i
            results.append(Pair(send, keep, out_buffers[at], out_sems.at[at]))
        body(
            scalars_ref, *arrays[: len(blocks)], *weight_refs, *arrays[len(blocks) :], *results, *refs
        )
        for result in results:
            result.finish()

    anywhere = pl.BlockSpec(memory_space=pl.ANY)
    return pl.pallas_call(
        run,
        name=name,
        out_shape=tuple(jax.ShapeDtypeStruct(s, t) for s, t in outs),
        in_specs=[pl.BlockSpec(memory_space=pltpu.SMEM)]
        + [anywhere] * (len(ins) + len(weights) + len(after)),
        out_specs=(anywhere,) * len(outs),
        scratch_shapes=buffers + sems + scratch,
        compiler_params=pltpu.CompilerParams(vmem_limit_bytes=VMEM_LIMIT),
        cost_estimate=pl.CostEstimate(
            flops=microseconds * 1_150_000_000,
            bytes_accessed=microseconds * 3_690_000,
            transcendentals=0,
        ),
    )(scalars, *ins, *weights, *after)


class Source:
    def __init__(self, kind, groups):
        self.kind = kind
        self.groups = groups
        self.count_all = kind.count * (len(groups) if kind is Units else 1)

    def __call__(self, refs):
        return self.kind(self.groups, refs)


class Sinks:
    def __init__(self, entries, first=None, taken=()):
        self.entries = entries
        self.first = first
        self.taken = taken
        self.count = len(entries)
        self.passed = 2 * len(taken)

    def shapes(self):
        return [shape for _, shape in self.entries]

    def __call__(self, pairs):
        if self.first is not None:
            return RowSink(pairs[0], self.first)
        return UnitSink({key: pair for (key, _), pair in zip(self.entries, pairs)})

    def pass_on(self, sink, place, passed):
        for i, (unit, at, count) in enumerate(self.taken):
            far_x, far_y, low = place.turned(unit)
            arrays = [array.get() for array in passed[2 * i : 2 * i + 2]]
            target = sink.pairs[group_of(unit) + 100].ref
            for slot, source in enumerate(arrays):
                for quarter in range(2):
                    target[slot, far_x + 2 * far_y, low, quarter, at : at + count, :] = source[
                        quarter, at : at + count, :
                    ]


class Layer:
    def __init__(self, tokens, memory, slot_cotangent, slot_mask, bounds, sources, weights, sinks):
        self.tokens, self.memory = tokens, memory
        self.slot_cotangent, self.slot_mask = slot_cotangent, slot_mask
        self.bounds, self.sources, self.weights, self.sinks = bounds, sources, weights, sinks
        self.act = tokens.shape
        self.keys = memory.shape[0]
        self.sems = [pltpu.SemaphoreType.DMA((3,))]

    def call(self, body, name, which, blocks, outs, scratch, microseconds, sink=None, **more):
        parts = [self.sources[which]] + ([sink] if sink is not None else [])
        return call(
            functools.partial(body, *parts), name, self.bounds, blocks, self.weights[which], outs,
            scratch + self.sems, microseconds, **more,
        )

    def attend_outs(self, keys):
        length = self.act[0]
        return [
            (self.act, bf16), ((keys, D), bf16), ((keys, D), bf16), ((D, length), bf16),
            ((HEADS, length), f32), (self.act, f32),
        ]

    def attend_scratch(self, keys):
        return [
            wide(D, D), wide(D, D), wide(D, D), wide(D, D), wide(16, D), wide(PAIRS, keys, 256),
            wide(PAIRS, 144, keys),
            wide(*self.act),
        ]

    def self_forward(self, after=()):
        self.q, self.k, self.v, self.ot, self.lse, self.r1 = self.call(
            self_forward, "self_forward", "self", [self.tokens], self.attend_outs(self.act[0]),
            self.attend_scratch(self.act[0]), 18, after=after,
        )

    def cross_forward(self, after=()):
        self.cq, self.mk, self.mv, self.cot, self.clse, self.r2 = self.call(
            cross_forward, "cross_forward", "cross", [self.memory, self.r1],
            self.attend_outs(self.keys), self.attend_scratch(self.keys) + [full(*self.act)],
            19, after=after,
        )

    def prepare(self, after=()):
        length, act = self.act[0], self.act
        self.gs, self.gs2, self.h2 = self.call(
            prepare, "prepare", "self", [self.slot_mask, self.slot_cotangent, self.r2],
            [(act, bf16), (act, bf16), (act, f32)],
            [wide(16, D), full(length, 128), full(length + 8, D)], 5, after=after,
        )

    def ffn(self, after=()):
        length, act, sink = self.act[0], self.act, self.sinks["ffn"]
        self.hlow, self.gr2, *self.g_ffn = self.call(
            ffn, "ffn", "ffn", [self.h2, self.gs, self.gs2, self.r2],
            [(act, bf16), (act, f32)],
            [
                wide(4, D, D), wide(FF, D), wide(FF, D), wide(2 * D, D), wide(VEC_ROWS, D),
                full(4, FF, 128), wide(length, FF), wide(length, FF), full(*act), wide(*act),
                full(*act), wide(*act), full(128, D),
            ],
            34, sink, after=after, pairs=sink.shapes(),
        )

    def slot_forward(self, after=()):
        length = self.act[0]
        (self.slots,) = self.call(
            slot_forward, "slot_forward", "ffn", [self.slot_mask, self.hlow], [(self.act, bf16)],
            [wide(2 * D, D), wide(VEC_ROWS, D), full(length + 8, D), full(length, 128)], 6,
            after=after,
        )

    def back_scratch(self, keys):
        return [
            wide(PAIRS, keys, 256), wide(D, keys), full(keys, D), full(keys, D), wide(*self.act)
        ]

    def cross_backward(self, after=()):
        sink = self.sinks["cross"]
        self.mdk, self.mdv, self.gr1, self.gv, *self.g_cross = self.call(
            cross_backward, "cross_backward", "cross",
            [self.mk, self.gr2, self.mv, self.cq, self.clse, self.cot, self.r1, self.memory],
            [((self.keys, D), bf16)] * 2 + [(self.act, f32), ((16, D), f32)],
            [wide(D, D), wide(D, D), wide(16, D)] + [wide(*self.act)] * 3
            + self.back_scratch(self.keys),
            28, sink, passed=self.g_ffn[: sink.passed], after=after, pairs=sink.shapes(),
        )

    def self_backward(self, after=()):
        sink = self.sinks["self"]
        length = self.act[0]
        self.dq, self.dk, self.dv, *self.g_self = self.call(
            self_backward, "self_backward", "self",
            [self.k, self.gr1, self.v, self.q, self.lse, self.ot, self.tokens, self.gv],
            [(self.act, bf16)] * 3,
            [wide(D, D), wide(*self.act), full(16, D)] + self.back_scratch(length),
            26, sink, passed=self.g_cross[: sink.passed], after=after, pairs=sink.shapes(),
        )

    def memory_gradient(self, after=()):
        (self.memory_grad,) = self.call(
            memory_gradient, "memory_gradient", "cross", [self.mdk, self.mdv],
            [((self.keys, D), bf16)], [wide(2 * D, D)], 5, after=after,
        )

    def token_gradient(self, after=()):
        (self.tokens_grad,) = self.call(
            token_gradient, "token_gradient", "self", [self.dq, self.dk, self.dv, self.gr1],
            [(self.act, bf16)], [wide(3 * D, D)], 6, after=after,
        )


def wide(*shape):
    return pltpu.VMEM(shape, bf16)


def full(*shape):
    return pltpu.VMEM(shape, f32)


def plain_layer(args, param_slabs):
    gathered = lax.all_gather(param_slabs, AXES, axis=0, tiled=True)
    total_rows = gathered.shape[0] // 4
    rows = gathered.reshape(total_rows, 4, 128)
    pieces = [rows[:, i, :] for i in range(4)]
    shapes = {"self": 2048 + 16, "cross": 2048, "ffn": 5120 + 128}
    firsts = {"self": 0, "cross": 2048, "ffn": 4096}
    sinks = {name: Sinks([(0, (2, shapes[name], 128))], firsts[name]) for name in shapes}
    source = Source(Pieces, ())
    run = Layer(*args, {n: source for n in shapes}, {n: pieces for n in shapes}, sinks)
    run.self_forward()
    run.cross_forward()
    run.prepare()
    run.ffn()
    run.cross_backward()
    run.self_backward()
    run.slot_forward()
    run.memory_gradient()
    run.token_gradient()
    send, keep = [
        jnp.concatenate([run.g_self[i][:, :2048], run.g_cross[i], run.g_ffn[i]], axis=1)
        .at[:, ROW_VEC : ROW_VEC + 16]
        .add(run.g_self[i][:, 2048:])
        for i in range(2)
    ]
    first = lax.axis_index("narrow") % 2 == 0
    low = jnp.where(first, keep, send)
    high = jnp.where(first, send, keep)
    flat = jnp.concatenate([low, high], axis=0).transpose(1, 0, 2)
    flat = jnp.pad(flat, ((0, total_rows - flat.shape[0]), (0, 0), (0, 0))).reshape(-1, 128)
    param_grad = lax.psum_scatter(flat, AXES, scatter_dimension=0, tiled=True).astype(f32)
    return run.slots, run.tokens_grad, run.memory_grad, param_grad


def moves(rule):
    number = lambda z, x, y, c: ((z * 2 + x) * 2 + y) * 2 + c
    pairs = []
    for z in range(4):
        for x in range(2):
            for y in range(2):
                for c in range(2):
                    target = rule(z, x, y, c)
                    if target is not None:
                        pairs.append((number(z, x, y, c), number(*target)))
    return pairs


OTHER_CORE = moves(lambda z, x, y, c: (z, x, y, 1 - c))
ALONG_X = moves(lambda z, x, y, c: (z, 1 - x, y, c))
ALONG_Y = moves(lambda z, x, y, c: (z, x, 1 - y, c))
ALONG_BOTH = moves(lambda z, x, y, c: (z, 1 - x, 1 - y, c))
ALONG_Z = moves(lambda z, x, y, c: (z ^ 1, x, y, c))
TWO_ALONG_Z = moves(lambda z, x, y, c: (z ^ 2, x, y, c))


def hops(table):
    return moves(lambda z, x, y, c: (table[z], x, y, c) if z in table else None)


def permute(value, pairs):
    return lax.ppermute(value, AXES, pairs)


def total(*values):
    return sum(value.astype(f32) for value in values).astype(bf16)


def spread_plane(own):
    return [own] + [permute(own, pairs) for pairs in (ALONG_X, ALONG_Y, ALONG_BOTH)]


def to_other_core(values):
    return [permute(value, OTHER_CORE) for value in values]


def sum_plane(keep, got):
    return [
        permute(total(keep[i], got[i]), pairs)
        for i, pairs in ((1, ALONG_X), (2, ALONG_Y), (3, ALONG_BOTH))
    ]


def here(keep, got, arrived):
    return total(keep[0], got[0], *arrived)


def hold(arrays, after):
    anywhere = pl.BlockSpec(memory_space=pl.ANY)
    return pl.pallas_call(
        lambda *refs: None, name="hold",
        out_shape=tuple(jax.ShapeDtypeStruct(v.shape, v.dtype) for v in arrays),
        in_specs=[anywhere] * (len(arrays) + len(after)), out_specs=(anywhere,) * len(arrays),
        input_output_aliases={i: i for i in range(len(arrays))},
    )(*arrays, *after)


def chip_layer(args, param_slabs):
    z = lax.axis_index("wide") // 2
    shard_rows = param_slabs.shape[0]
    small = lambda *s: jax.ShapeDtypeStruct(s, bf16)
    real = lambda *s: jax.ShapeDtypeStruct(s, f32)
    keep, send, one, two = pl.pallas_call(
        split_shard, name="split_shard",
        out_shape=(small(2, PAD_ROWS, 128),) * 2 + (small(2, 16, 128),) * 2,
        in_specs=[WHOLE], out_specs=(WHOLE,) * 4, scratch_shapes=[full(4 * PAD_ROWS, 128)],
    )(param_slabs)
    got = permute(send, OTHER_CORE)

    def few(core):
        def rule(z, x, y, c):
            if (y, c) == (1, 0):
                return (z, x, 0, core)
            return (0, 1, 1, core) if (z, x, y, c) == (3, 1, 1, 1) else None

        return moves(rule)

    one, two = permute(one, few(0)), permute(two, few(1))
    (unit,) = pl.pallas_call(
        join_unit, name="join_unit", out_shape=(small(1, 2, UNIT, 128),),
        in_specs=[pl.BlockSpec(memory_space=pltpu.SMEM)] + [WHOLE] * 4, out_specs=(WHOLE,),
        scratch_shapes=[full(2 * PAD_ROWS, 128)],
    )(args[4], keep, got, one, two)

    first = permute(unit, hops({0: 2, 1: 0, 3: 1}))
    plane0 = jnp.where(z == 0, unit, first)
    second = permute(jnp.where(z == 1, unit, plane0), hops({0: 1, 1: 2, 2: 3}))
    plane0 = jnp.where(z % 2 == 1, second, plane0)
    (unit,) = hold([unit], [plane0])
    mine0 = spread_plane(plane0)
    third = permute(second, hops({2: 3}))
    fourth = permute(unit, hops({2: 0}))
    plane1 = jnp.where(z < 2, jnp.where(z == 0, first, unit), jnp.where(z == 2, second, third))
    high = jnp.where(z < 2, jnp.where(z == 0, fourth, first), unit)
    *mine0[1:], plane1, high = hold([*mine0[1:], plane1, high], [])
    groups = [mine0 + to_other_core(mine0), None, None]
    mine1 = spread_plane(plane1)
    near = permute(high, ALONG_Z)
    used = {"self": (0,), "cross": (0, 1), "ffn": (1, 2)}
    sources = {name: Source(Units, group) for name, group in used.items()}
    weights = {"self": groups[0]}
    one_unit = (2, SUM_UNIT, 128)
    sinks = {
        "ffn": Sinks([(7, one_unit), (102, (4, 2, 2, SUM_UNIT, 128))]),
        "cross": Sinks([(3, one_unit), (101, (4, 1, 2, SUM_UNIT, 128))], taken=[(7, 8, 576)]),
        "self": Sinks([(100, (4, 1, 2, SUM_UNIT, 128))], taken=[(3, 296, 288)]),
    }
    run = Layer(*args, sources, weights, sinks)
    run.self_forward()
    *mine1[1:], near = hold(mine1[1:] + [near], [run.r1])
    groups[1] = mine1 + to_other_core(mine1)
    weights["cross"] = groups[0] + groups[1]
    mine23 = spread_plane(jnp.concatenate([high, near], axis=0))
    run.cross_forward()
    run.prepare()
    mine23[1:] = hold(mine23[1:], [run.h2])
    groups[2] = mine23 + to_other_core(mine23)
    weights["ffn"] = groups[1] + groups[2]
    run.ffn()
    send23, keep23 = run.g_ffn[2:4]
    got23 = permute(send23, OTHER_CORE)
    arrived23 = sum_plane(keep23, got23)
    run.cross_backward()
    send1, keep1 = run.g_cross[2:4]
    (send1,) = hold([send1], arrived23)
    got1 = permute(send1, OTHER_CORE)
    arrived1 = sum_plane(keep1, got1)
    here23 = here(keep23, got23, arrived23)
    across23 = permute(here23[1], ALONG_Z)
    run.self_backward()
    send0, keep0 = run.g_self
    (send0,) = hold([send0], [*arrived1, across23])
    got0 = permute(send0, OTHER_CORE)
    here1 = here(keep1, got1, arrived1)[0]
    across1 = permute(here1, hops({0: 1, 3: 2}))
    arrived0 = sum_plane(keep0, got0)
    run.memory_gradient()
    run.token_gradient(after=arrived0)
    run.slot_forward()
    mixed23 = total(here23[0], across23)
    mixed1 = total(here1, across1)
    rest = permute(jnp.where(z < 2, mixed23, mixed1), hops({0: 2, 1: 3, 2: 1}))
    here0 = here(keep0, got0, arrived0)[0]
    (here0,) = hold([here0], [across1, run.memory_grad])
    across0 = permute(here0, hops({1: 0, 3: 2}))
    (across0,) = hold([across0], [rest, run.tokens_grad])
    keep, send, far_keep, far_send, vec = pl.pallas_call(
        split_unit, name="split_unit",
        out_shape=(real(2, PAD_ROWS, 128),) * 2 + (small(2, PAD_ROWS, 128),) * 2
        + (real(2, 16, 128),),
        in_specs=[WHOLE] * 5, out_specs=(WHOLE,) * 5, scratch_shapes=[full(SUM_UNIT, 128)],
    )(here0, across0, mixed1, rest, mixed23)

    def down(other):
        def rule(z, x, y, c):
            if z == 2:
                return (0, x, y, c ^ other)
            return (3, 1, 1, 1) if (z, x, y, c) == (0, 1, 1, 1 - other) else None

        return moves(rule)

    one, two = [
        permute(vec, moves(lambda z, x, y, c: (3, 1, 1, 1) if (z, x, y, c) == (2, 1, 1, core) else None))
        for core in range(2)
    ]
    far_keep, far_got = permute(far_keep, down(0)), permute(far_send, down(1))
    got = permute(send, OTHER_CORE)
    (got,) = hold([got], [run.slots])
    (param_grad,) = pl.pallas_call(
        join_shard, name="join_shard", out_shape=(real(shard_rows, 128),),
        in_specs=[WHOLE] * 6, out_specs=(WHOLE,), scratch_shapes=[full(4 * PAD_ROWS, 128)],
    )(keep, got, far_keep, far_got, one, two)
    return run.slots, run.tokens_grad, run.memory_grad, param_grad


def shards(mesh_shape, tokens, memory, slot_cotangent, param_slabs, segment_ids, memory_lengths,
           slot_mask):
    smem = pl.BlockSpec(memory_space=pltpu.SMEM)
    bounds = pl.pallas_call(
        find_bounds, name="find_bounds", out_shape=jax.ShapeDtypeStruct((8,), jnp.int32),
        in_specs=[WHOLE, smem], out_specs=smem,
    )(segment_ids, memory_lengths)
    chips = mesh_shape == (8, 4) and param_slabs.shape[0] == 4 * CORE_ROWS
    args = (tokens, memory, slot_cotangent, slot_mask, bounds)
    return (chip_layer if chips else plain_layer)(args, param_slabs)


def solution(mesh):
    spec = P(AXES, None)
    shape = tuple(mesh.shape[axis] for axis in AXES)
    return jax.shard_map(
        functools.partial(shards, shape),
        mesh=mesh,
        in_specs=(spec,) * 7,
        out_specs=(spec,) * 4,
        check_vma=False,
    )
```

```python
import functools
import math

import jax
import jax.numpy as jnp
from jax import lax
from jax.experimental import pallas as pl
from jax.experimental.pallas import tpu as pltpu
from jax.sharding import PartitionSpec as P

D = 512
HEADS = 8
HD = 64
FF = 2048
EPSILON = 1e-05
AXES = ("wide", "narrow")
QB = 128
PAIRS = HEADS // 2
BIG = -1e30
LOG2E = math.log2(math.e)
Q_SCALE = LOG2E * HD ** (-0.5)

f32 = jnp.float32
bf16 = jnp.bfloat16

ROW_Q, ROW_K, ROW_V, ROW_O = 0, 512, 1024, 1536
ROW_CQ, ROW_CK, ROW_CV, ROW_CO = 2048, 2560, 3072, 3584
ROW_IN, ROW_OUT, ROW_SLOT, ROW_VEC = 4096, 6144, 8192, 9216
VEC_ROWS = 32
VEC_NAMES = (
    "query_b", "value_b", "out_b", "cross_query_b", "cross_value_b", "cross_out_b", "gain_one",
    "shift_one", "gain_two", "shift_two", "gain_three", "shift_three", "outer_b", "slot_b", "inner_b",
)
VEC = {name: place for place, name in enumerate(VEC_NAMES)}

VMEM_LIMIT = 54 * 1024 * 1024


def dot(a, b):
    return jnp.dot(a, b, preferred_element_type=f32)


def dot_nt(a, b):
    return lax.dot_general(a, b, (((1,), (1,)), ((), ())), preferred_element_type=f32)


def dot_tn(a, b):
    return lax.dot_general(a, b, (((0,), (0,)), ((), ())), preferred_element_type=f32)


def column_sum(matrix):
    return jnp.sum(matrix.astype(f32), axis=0, keepdims=True)


def normalize(values):
    centered = values - jnp.mean(values, axis=-1, keepdims=True)
    root = lax.rsqrt(jnp.mean(centered * centered, axis=-1, keepdims=True) + EPSILON)
    return centered * root, root


def normalize_back(grad, normal, root, gain):
    scaled = grad * gain
    first = jnp.mean(scaled, axis=-1, keepdims=True)
    second = jnp.mean(scaled * normal, axis=-1, keepdims=True)
    return root * (scaled - first - normal * second)


CHIP_ROWS = 584
CORE_ROWS = 292
UNIT = 592
UNITS = 16


def unit_begin(unit):
    return 2 * CHIP_ROWS * (unit // 2) + UNIT * (unit % 2)


def unit_parts(begin, rows):
    parts = []
    for unit in range(UNITS):
        low = max(begin, unit_begin(unit))
        high = min(begin + rows, unit_begin(unit + 1))
        if low < high:
            parts.append((unit, low - unit_begin(unit), low - begin, high - low))
    return parts


SUM_UNIT = 608


def own_parts(begin, rows):
    parts = []
    for unit in range(UNITS):
        low = max(begin, CHIP_ROWS * unit)
        high = min(begin + rows, CHIP_ROWS * (unit + 1))
        if low < high:
            parts.append((unit, low - CHIP_ROWS * unit, low - begin, high - low))
    return parts


def group_of(unit):
    return min(unit // 4, 2)


class Place:
    def __init__(self, bounds=None):
        if bounds is not None:
            self.token_bounds = [bounds[i] for i in range(3)]
            self.memory_bounds = [bounds[3 + i] for i in range(3)]
        wide, narrow = lax.axis_index("wide"), lax.axis_index("narrow")
        self.z, self.x = lax.div(wide, 2), lax.rem(wide, 2)
        self.y, self.core = lax.div(narrow, 2), lax.rem(narrow, 2)

    def turned(self, unit):
        z, x, y = unit // 4, unit // 2 % 2, unit % 2
        low = jnp.bitwise_xor(lax.rem(self.z, 2), z % 2) if group_of(unit) == 2 else 0
        return jnp.bitwise_xor(self.x, x), jnp.bitwise_xor(self.y, y), low


class Units:
    count = 8

    def __init__(self, groups, refs):
        self.groups = {
            group: (refs[8 * i : 8 * i + 4], refs[8 * i + 4 : 8 * i + 8])
            for i, group in enumerate(groups)
        }

    def load(self, place, begin, buffer, sem):
        return self.load_parts(place, unit_parts(begin, buffer.shape[0]), buffer, sem)

    def load_vectors(self, place, buffer, sem):
        return self.load_parts(place, [(3, UNIT - 16, 0, 16)], buffer, sem)

    def load_parts(self, place, parts, buffer, sem):
        copies = []
        for unit, source, target, rows in parts:
            halves = self.groups[group_of(unit)]
            far_x, far_y, low = place.turned(unit)
            targets = [
                [
                    buffer.at[
                        pl.ds(target, rows),
                        pl.ds(
                            pl.multiple_of(
                                (jnp.bitwise_xor(place.core, half) * 2 + quarter) * 128, 128
                            ),
                            128,
                        ),
                    ]
                    for quarter in range(2)
                ]
                for half in range(2)
            ]

            def part(half, which, quarter):
                return halves[half][which].at[low, quarter, pl.ds(source, rows), :]

            for which in range(4):

                @pl.when((far_x == which % 2) & (far_y == which // 2))
                def _():
                    for half in range(2):
                        for quarter in range(2):
                            pltpu.make_async_copy(
                                part(half, which, quarter), targets[half][quarter], sem
                            ).start()

            copies += [
                pltpu.make_async_copy(part(half, 0, quarter), targets[half][quarter], sem)
                for half in range(2)
                for quarter in range(2)
            ]
        return copies


class Pieces:
    count = 4

    def __init__(self, groups, refs):
        self.refs = refs[:4]

    def load(self, place, begin, buffer, sem):
        copies = []
        for i, ref in enumerate(self.refs):
            copy = pltpu.make_async_copy(
                ref.at[pl.ds(begin, buffer.shape[0]), :],
                buffer.at[:, i * 128 : (i + 1) * 128],
                sem,
            )
            copy.start()
            copies.append(copy)
        return copies

    def load_vectors(self, place, buffer, sem):
        return self.load(place, ROW_VEC, buffer, sem)


def wait_all(copies):
    for copy in copies:
        copy.wait()


def vector(vec_ref, name):
    return vec_ref[VEC[name] : VEC[name] + 1, :].astype(f32)


class UnitSink:
    def __init__(self, pairs):
        self.pairs = pairs

    def places(self, place, begin, rows):
        for unit, at, source, count in own_parts(begin, rows):
            if unit in self.pairs:
                yield self.pairs[unit].ref, (), at, source, count
            elif group_of(unit) + 100 in self.pairs:
                far_x, far_y, low = place.turned(unit)
                yield self.pairs[group_of(unit) + 100].ref, (far_x + 2 * far_y, low), at, source, count

    def send(self, place, units):
        for unit in units:
            far_x, far_y, low = place.turned(unit)
            self.pairs[group_of(unit) + 100].send(far_x + 2 * far_y, low)

    def vector_places(self, place):
        far_x, far_y, low = place.turned(3)
        yield self.pairs[100].ref, (far_x + 2 * far_y, low), CHIP_ROWS, 0, 16


class RowSink:
    def __init__(self, pair, first):
        self.ref = pair.ref
        self.first = first

    def send(self, place, units):
        pass

    def places(self, place, begin, rows):
        yield self.ref, (), begin - self.first, 0, rows

    def vector_places(self, place):
        yield self.ref, (), 2048, 0, 16


def put_grad(sink, place, begin, value):
    put_places(place, sink.places(place, begin, value.shape[0]), value)


def put_places(place, places, value):
    for ref, lead, at, source, count in places:
        low = value[source : source + count, :].astype(bf16)
        for i in range(4):
            kept = 1 - jnp.bitwise_xor(place.core, i // 2)
            ref[(kept, *lead, i % 2, pl.ds(at, count), slice(None))] = low[:, lanes(i)]


def segment_of(position, bounds):
    return sum([(position >= bound).astype(jnp.int32) for bound in bounds])


def pick(index, choices):
    value = choices[-1]
    for place in range(len(choices) - 2, -1, -1):
        value = jnp.where(index == place, choices[place], value)
    return value


def key_range(first_query, query_bounds, key_bounds, length):
    low = segment_of(first_query, query_bounds)
    high = segment_of(first_query + (QB - 1), query_bounds)
    begin = pick(low, [0, *key_bounds]) // 128
    end = (pick(high, [*key_bounds, length]) + 127) // 128
    return begin * 128, end - begin


def query_marks(first_query, bounds):
    position = first_query + lax.broadcasted_iota(jnp.int32, (QB, 128), 0)
    lane = lax.broadcasted_iota(jnp.int32, (QB, 128), 1)
    hidden = (lane <= len(bounds)) & (lane != segment_of(position, bounds))
    return jnp.where(hidden, BIG, 0.0).astype(bf16)


def key_marks(length, bounds):
    position = lax.broadcasted_iota(jnp.int32, (length, 128), 0)
    lane = lax.broadcasted_iota(jnp.int32, (length, 128), 1)
    return jnp.where(lane == segment_of(position, bounds), 1.0, 0.0).astype(bf16)


def stack_heads(pair):
    lane = lax.broadcasted_iota(jnp.int32, pair.shape, 1)
    nothing = jnp.zeros_like(pair)
    return jnp.concatenate(
        [jnp.where(lane < HD, pair, nothing), jnp.where(lane >= HD, pair, nothing)], axis=0
    )


def by_count(count, most, body):
    for value in range(1, most + 1):

        @pl.when(count == value)
        def _():
            body(value)


def lanes(pair):
    return slice(pair * 128, (pair + 1) * 128)


def marked_keys(k_ref, kx, key_bounds):
    marks = key_marks(k_ref.shape[0], key_bounds)
    for pair in range(PAIRS):
        kx[pair, :, 0:128] = k_ref[:, lanes(pair)]
        kx[pair, :, 128:256] = marks


def attend(q_ref, kx, vt, ot_ref, o_ref, lse_ref, query_bounds, key_bounds):
    length = kx.shape[1]

    def block(index, carry):
        first = pl.multiple_of(index * QB, QB)
        begin, count = key_range(first, query_bounds, key_bounds, length)
        begin = pl.multiple_of(begin, 128)
        queries = pl.ds(first, QB)
        marks = query_marks(first, query_bounds)
        marks = jnp.concatenate([marks, marks], axis=0)

        def run(blocks):
            keys = pl.ds(begin, 128 * blocks)
            scores = []
            for pair in range(PAIRS):
                wide = jnp.concatenate([stack_heads(q_ref[queries, lanes(pair)]), marks], axis=1)
                scores.append(dot_nt(kx[pair, keys, :], wide))
            tops = []
            probs = []
            for pair in range(PAIRS):
                top = jnp.max(scores[pair], axis=0, keepdims=True)
                tops.append(top)
                probs.append(jnp.exp2(scores[pair] - top).astype(bf16))
            mixed = [dot(vt[pair, :, keys], probs[pair]) for pair in range(PAIRS)]
            for pair in range(PAIRS):
                total = mixed[pair][128:129, :]
                scale = 1.0 / total
                lse = tops[pair] + jnp.log2(total)
                one = mixed[pair][0:64, 0:128] * scale[:, 0:128]
                two = mixed[pair][64:128, 128:256] * scale[:, 128:256]
                out = jnp.concatenate([one, two], axis=0)
                ot_ref[lanes(pair), queries] = out.astype(bf16)
                o_ref[queries, lanes(pair)] = out.T.astype(bf16)
                lse_ref[2 * pair : 2 * pair + 1, queries] = lse[:, 0:128]
                lse_ref[2 * pair + 1 : 2 * pair + 2, queries] = lse[:, 128:256]

        by_count(count, length // 128, run)
        return carry

    lax.fori_loop(0, q_ref.shape[0] // QB, block, 0)


def attend_back(
    q_ref, kx, kt, v_ref, do_ref, lse_ref, dq_ref, dk_sum, dv_sum, query_bounds, key_bounds
):
    length = kx.shape[1]
    dk_sum[...] = jnp.zeros_like(dk_sum)
    dv_sum[...] = jnp.zeros_like(dv_sum)

    def block(index, carry):
        first = pl.multiple_of(index * QB, QB)
        begin, count = key_range(first, query_bounds, key_bounds, length)
        begin = pl.multiple_of(begin, 128)
        queries = pl.ds(first, QB)
        marks = query_marks(first, query_bounds)
        marks = jnp.concatenate([marks, marks], axis=0)

        def run(blocks):
            keys = pl.ds(begin, 128 * blocks)

            def products(pair):
                q_two = stack_heads(q_ref[queries, lanes(pair)])
                do_two = stack_heads(do_ref[queries, lanes(pair)])
                scores = dot_nt(kx[pair, keys, :], jnp.concatenate([q_two, marks], axis=1))
                grad_probs = dot_nt(v_ref[keys, lanes(pair)], do_two)
                return q_two, do_two, scores, grad_probs

            def gradients(pair):
                _, _, scores, grad_probs = ready[pair]
                lse = jnp.concatenate(
                    [
                        lse_ref[2 * pair : 2 * pair + 1, queries],
                        lse_ref[2 * pair + 1 : 2 * pair + 2, queries],
                    ],
                    axis=1,
                )
                probs = jnp.exp2(scores - lse)
                both = probs * grad_probs
                delta = jnp.sum(both, axis=0, keepdims=True)
                return (both - probs * delta).astype(bf16), probs.astype(bf16)

            ready = {pair: products(pair) for pair in (0, 1)}
            made = {0: gradients(0)}
            for pair in range(PAIRS):
                if pair + 2 < PAIRS:
                    ready[pair + 2] = products(pair + 2)
                if pair + 1 < PAIRS:
                    made[pair + 1] = gradients(pair + 1)
                q_two, do_two = ready[pair][:2]
                grad_scores, probs = made[pair]
                dqt = dot(kt[lanes(pair), keys], grad_scores)
                dk_sum[keys, lanes(pair)] += dot(grad_scores, q_two)
                dv_sum[keys, lanes(pair)] += dot(probs, do_two)
                dq = jnp.concatenate([dqt[0:64, 0:128], dqt[64:128, 128:256]], axis=0)
                dq_ref[queries, lanes(pair)] = (dq * HD ** (-0.5)).T.astype(bf16)

        by_count(count, length // 128, run)
        return carry

    lax.fori_loop(0, q_ref.shape[0] // QB, block, 0)


def values_transposed(v_ref, vt):
    for pair in range(PAIRS):
        vt[pair, 0:128, :] = v_ref[:, lanes(pair)].T
        vt[pair, 128:144, :] = jnp.ones((16, vt.shape[2]), bf16)


def four(values):
    return jnp.concatenate([values] * 4, axis=1)


def rows_of(w, i):
    return w[i * D : (i + 1) * D, :]


def add_out(r, x, o, w, bias):
    tile = 256
    for t in range(o.shape[0] // tile):
        rows = slice(t * tile, (t + 1) * tile)
        r.ref[rows, :] = x[rows, :].astype(f32) + dot(o[rows, :], w) + bias
        r.send(pl.ds(t * tile, tile))


def self_forward(source, scalars, x, *rest):
    (q, k, v, ot, lse, r, wq, wk, wv, wo, vec, kx, vt, o, sems) = rest[source.count_all :]
    place = Place(scalars)
    weights = source(rest)
    start(x)
    k_copies = weights.load(place, ROW_K, wk, sems.at[0])
    q_copies = weights.load(place, ROW_Q, wq, sems.at[1])
    q_copies += weights.load_vectors(place, vec, sems.at[1])
    v_copies = weights.load(place, ROW_V, wv, sems.at[2])
    x = x.get()
    wait_all(k_copies)
    k.ref[...] = dot(x[...], wk[...]).astype(bf16)
    k.send()
    wait_all(q_copies)
    q.ref[...] = ((dot(x[...], wq[...]) + vector(vec, "query_b")) * Q_SCALE).astype(bf16)
    q.send()
    wait_all(v_copies)
    v.ref[...] = (dot(x[...], wv[...]) + vector(vec, "value_b")).astype(bf16)
    v.send()
    o_copies = weights.load(place, ROW_O, wo, sems.at[0])
    bounds = place.token_bounds
    marked_keys(k.ref, kx, bounds)
    values_transposed(v.ref, vt)
    attend(q.ref, kx, vt, ot.ref, o, lse.ref, bounds, bounds)
    ot.send()
    wait_all(o_copies)
    add_out(r, x, o, wo[...], vector(vec, "out_b"))


def cross_forward(source, scalars, m, r1, *rest):
    (q, k, v, ot, lse, r, wq, wk, wv, wo, vec, kx, vt, o, h, sems) = rest[source.count_all :]
    place = Place(scalars)
    weights = source(rest)
    start(m)
    k_copies = weights.load(place, ROW_CK, wk, sems.at[0])
    v_copies = weights.load(place, ROW_CV, wv, sems.at[1])
    v_copies += weights.load_vectors(place, vec, sems.at[1])
    m = m.get()
    wait_all(k_copies)
    start(r1)
    q_copies = weights.load(place, ROW_CQ, wq, sems.at[2])
    k.ref[...] = dot(m[...], wk[...]).astype(bf16)
    k.send()
    wait_all(v_copies)
    v.ref[...] = (dot(m[...], wv[...]) + vector(vec, "cross_value_b")).astype(bf16)
    v.send()
    o_copies = weights.load(place, ROW_CO, wo, sems.at[0])
    r1 = r1.get()
    wait_all(q_copies)
    gain, shift = vector(vec, "gain_one"), vector(vec, "shift_one")
    tile = 256
    for t in range(h.shape[0] // tile):
        rows = slice(t * tile, (t + 1) * tile)
        part = normalize(r1[rows, :])[0] * gain + shift
        h[rows, :] = part
        q.ref[rows, :] = (
            (dot(part.astype(bf16), wq[...]) + vector(vec, "cross_query_b")) * Q_SCALE
        ).astype(bf16)
    q.send()
    marked_keys(k.ref, kx, place.memory_bounds)
    values_transposed(v.ref, vt)
    attend(q.ref, kx, vt, ot.ref, o, lse.ref, place.token_bounds, place.memory_bounds)
    ot.send()
    wait_all(o_copies)
    add_out(r, h, o, wo[...], vector(vec, "cross_out_b"))


def gelu_parts(x):
    scale = math.sqrt(2.0 / math.pi)
    square = x * x
    half = 0.5 + 0.5 * jnp.tanh(x * (scale + (scale * 0.044715) * square))
    value = x * half
    slope = half + value * (1.0 - half) * (2.0 * scale + (6.0 * scale * 0.044715) * square)
    return value, slope


def same_next(first, rows, bounds, length):
    later = first + 1 + lax.broadcasted_iota(jnp.int32, (rows, 128), 0)
    same = later != length
    for bound in bounds:
        same = same & (later != bound)
    return same.astype(f32)


def prepare(source, scalars, mask_in, cot_in, r2_in, *rest):
    (gs, gs2, h2, vec, mask, spread, sems) = rest[source.count_all :]
    place = Place(scalars)
    start(mask_in, cot_in, r2_in)
    copies = source(rest).load_vectors(place, vec, sems.at[0])
    bounds = place.token_bounds
    length = h2.ref.shape[0]
    tile = 256
    mask[...] = jnp.broadcast_to(mask_in.get()[...].astype(f32), (128, length)).T
    cot_ref = cot_in.get()
    spread[0:8, :] = jnp.zeros((8, D), f32)
    for t in range(length // tile):
        rows = slice(t * tile, (t + 1) * tile)
        part = cot_ref[rows, :].astype(f32) * four(mask[rows, :])
        gs.ref[rows, :] = part.astype(bf16)
        same = same_next(t * tile, tile, bounds, length)
        spread[8 + t * tile : 8 + (t + 1) * tile, :] = part * four(same)
        gs2.ref[rows, :] = spread[7 + t * tile : 7 + (t + 1) * tile, :].astype(bf16)
    gs.send()
    gs2.send()
    wait_all(copies)
    r2 = r2_in.get()
    gain, shift = vector(vec, "gain_two"), vector(vec, "shift_two")
    for t in range(length // tile):
        rows = slice(t * tile, (t + 1) * tile)
        h2.ref[rows, :] = normalize(r2[rows, :])[0] * gain + shift


def ffn(source, make_sink, scalars, h2_in, gs_in, gs2_in, r2_in, *rest):
    rest_ = rest[source.count_all :]
    hlow_out, gr2 = rest_[:2]
    hlow, gr2_ref = hlow_out.ref, gr2.ref
    count = make_sink.count
    sink = make_sink(rest_[2 : 2 + count])
    (w_in, w_raw, w_out, w_slot, vec, comb, act, slope, h3, gf, gr3, h2b, gv_ref, sems) = rest_[
        2 + count :
    ]
    place = Place(scalars)
    weights = source(rest)
    in_copies = weights.load(place, ROW_IN, w_raw, sems.at[0])
    in_copies += weights.load(place, ROW_VEC, vec, sems.at[0])
    start(h2_in)
    length = gr2_ref.shape[0]
    tile = 256
    tiles = length // tile
    gv_ref[...] = jnp.zeros_like(gv_ref)

    def add_vector(name, value, at=0):
        at = VEC[name] + at
        gv_ref[at : at + 1, :] += value

    wait_all(in_copies)
    for i in range(4):
        comb[i] = w_raw[:, lanes(i)].astype(f32)
        for c in range(4):
            w_in[c, :, lanes(i)] = comb[i, pl.ds(c, D, 4), :].astype(bf16)
    out_copies = weights.load(place, ROW_OUT, w_out, sems.at[1])
    h2_ref = h2_in.get()
    slot_copies = weights.load(place, ROW_SLOT, w_slot, sems.at[2])
    start(gs_in, gs2_in, r2_in)
    biases = [vec[VEC["inner_b"] + c : VEC["inner_b"] + c + 1, :].astype(f32) for c in range(4)]

    def inner(t, c):
        rows = slice(t * tile, (t + 1) * tile)
        if c == 0:
            h2b[rows, :] = h2_ref[rows, :].astype(bf16)
        return dot(h2b[rows, :], w_in[c]) + biases[c]

    steps = [(t, c) for t in range(tiles) for c in range(4)]
    ahead = inner(*steps[0])
    wait_all(out_copies)
    for place_in, (t, c) in enumerate(steps):
        pre = ahead
        if place_in + 1 < len(steps):
            ahead = inner(*steps[place_in + 1])
        rows = slice(t * tile, (t + 1) * tile)
        value, gate = gelu_parts(pre)
        act[rows, c * D : (c + 1) * D] = value.astype(bf16)
        slope[rows, c * D : (c + 1) * D] = gate.astype(bf16)
        if c == 3:
            h3[rows, :] = h2_ref[rows, :] + dot(act[rows, :], w_out[...]) + vector(vec, "outer_b")
    wait_all(slot_copies)
    gs, gs2, r2_ref = gs_in.get(), gs2_in.get(), r2_in.get()

    def slot_grad(t):
        rows = slice(t * tile, (t + 1) * tile)
        return dot_nt(gs[rows, :], w_slot[0:D, :]) + dot_nt(gs2[rows, :], w_slot[D : 2 * D, :])

    ahead = slot_grad(0)
    for t in range(tiles):
        rows = slice(t * tile, (t + 1) * tile)
        grad = ahead
        if t + 1 < tiles:
            ahead = slot_grad(t + 1)
        normal, root = normalize(h3[rows, :])
        out = normal * vector(vec, "gain_three") + vector(vec, "shift_three")
        hlow[rows, :] = out.astype(bf16)
        add_vector("gain_three", column_sum(grad * normal))
        add_vector("shift_three", column_sum(grad))
        gr3[rows, :] = normalize_back(grad, normal, root, vector(vec, "gain_three"))
    hlow_out.send()
    add_vector("slot_b", column_sum(gs[...]))
    put_grad(sink, place, ROW_SLOT, dot_tn(hlow[...], gs[...]))
    put_grad(sink, place, ROW_SLOT + D, dot_tn(hlow[...], gs2[...]))
    gf[...] = gr3[...].astype(bf16)
    add_vector("outer_b", column_sum(gf[...]))
    for c in range(4):
        put_grad(sink, place, ROW_OUT + c * D, dot_tn(act[:, c * D : (c + 1) * D], gf[...]))
    sink.send(place, range(11, 15))

    def active(t, c):
        return dot_nt(gf[t * tile : (t + 1) * tile, :], w_out[c * D : (c + 1) * D, :])

    ahead = active(0, 0)
    for place_in, (t, c) in enumerate(steps):
        rows, at = slice(t * tile, (t + 1) * tile), slice(c * D, (c + 1) * D)
        grad = ahead.astype(bf16)
        if place_in + 1 < len(steps):
            ahead = active(*steps[place_in + 1])
        pre = (grad.astype(f32) * slope[rows, at].astype(f32)).astype(bf16)
        slope[rows, at] = pre
        add_vector("inner_b", column_sum(pre), c)
        part = dot_nt(pre, w_in[c])
        total = gr3[rows, :] + part if c == 0 else total + part
        if c == 3:
            normal, root = normalize(r2_ref[rows, :])
            add_vector("gain_two", column_sum(total * normal))
            add_vector("shift_two", column_sum(total))
            gr2_ref[rows, :] = normalize_back(total, normal, root, vector(vec, "gain_two"))
    gr2.send()
    put_grad(sink, place, ROW_VEC, gv_ref[...])
    sink.send(place, [15])
    for c in range(4):
        part = dot_tn(h2b[...], slope[:, c * D : (c + 1) * D])
        for i in range(4):
            comb[i, pl.ds(c, D, 4), :] = part[:, lanes(i)]
    put_grad(sink, place, ROW_IN, jnp.concatenate([comb[i] for i in range(4)], axis=1))
    sink.send(place, range(8, 11))


def slot_forward(source, scalars, mask_in, hlow_in, *rest):
    (slots, w, vec, spread, mask, sems) = rest[source.count_all :]
    place = Place(scalars)
    weights = source(rest)
    copies = weights.load(place, ROW_SLOT, w, sems.at[0])
    copies += weights.load(place, ROW_VEC, vec, sems.at[0])
    start(mask_in, hlow_in)
    hlow = hlow_in.get()
    length = hlow.shape[0]
    tile = 256
    mask[...] = jnp.broadcast_to(mask_in.get()[...].astype(f32), (128, length)).T
    spread[0:length, :] = hlow[...].astype(f32)
    spread[length : length + 8, :] = jnp.zeros((8, D), f32)
    wait_all(copies)
    for t in range(length // tile):
        rows = slice(t * tile, (t + 1) * tile)
        later = spread[t * tile + 1 : (t + 1) * tile + 1, :]
        same = four(same_next(t * tile, tile, place.token_bounds, length))
        raw = (
            dot(hlow[rows, :], w[0:D, :])
            + dot((later * same).astype(bf16), w[D : 2 * D, :])
            + vector(vec, "slot_b")
        )
        slots.ref[rows, :] = (four(mask[rows, :]) * raw).astype(bf16)
        slots.send(pl.ds(t * tile, tile))


def attend_backward(place, key_bounds, w, gr_low, v_in, q_in, lse_in, dq, dk, dv, scratch,
                    later):
    (kx, kt, dk_sum, dv_sum, do) = scratch
    do[...] = dot_nt(gr_low[...], w).astype(bf16)
    v_ref, q_ref, lse_ref = v_in.get(), q_in.get(), lse_in.get()
    start(*later)
    attend_back(
        q_ref, kx, kt, v_ref, do, lse_ref, dq.ref, dk_sum, dv_sum, place.token_bounds, key_bounds
    )
    dk.ref[...] = (dk_sum[...] * (1.0 / LOG2E)).astype(bf16)
    dv.ref[...] = dv_sum[...].astype(bf16)
    for out in (dq, dk, dv):
        if isinstance(out, Out):
            out.send()


def keys_ready(place, key_bounds, k_in, kx, kt):
    k_ref = k_in.get()
    marked_keys(k_ref, kx, key_bounds)
    for pair in range(PAIRS):
        kt[lanes(pair), :] = k_ref[:, lanes(pair)].T


class Held:
    def __init__(self, ref):
        self.ref = ref


def cross_backward(source, make_sink, scalars, k_in, gr2_in, v_in, q_in, lse_in, ot_in, r1_in, m_in,
                   *rest):
    passed = rest[source.count_all : source.count_all + make_sink.passed]
    rest_ = rest[source.count_all + make_sink.passed :]
    dk, dv, gr1, gv = rest_[:4]
    count = make_sink.count
    sink = make_sink(rest_[4 : 4 + count])
    (wq, wo, vec, grad, h, dq, *scratch, sems) = rest_[4 + count :]
    place = Place(scalars)
    weights = source(rest)
    start(k_in, gr2_in)
    o_copies = weights.load(place, ROW_CO, wo, sems.at[0])
    keys_ready(place, place.memory_bounds, k_in, *scratch[:2])
    start(v_in, q_in, lse_in)
    q_copies = weights.load(place, ROW_CQ, wq, sems.at[1])
    q_copies += weights.load_vectors(place, vec, sems.at[1])
    gv.ref[...] = jnp.zeros_like(gv.ref)

    def set_vector(name, value):
        gv.ref[VEC[name] : VEC[name] + 1, :] = value

    gr2_ref = gr2_in.get()
    grad[...] = gr2_ref[...].astype(bf16)
    wait_all(o_copies)
    attend_backward(
        place, place.memory_bounds, wo[...], grad, v_in, q_in, lse_in, Held(dq), dk, dv, scratch,
        [r1_in, ot_in, m_in, *passed],
    )
    set_vector("cross_out_b", column_sum(grad[...]))
    ot_ref, r1_ref = ot_in.get(), r1_in.get()
    wait_all(q_copies)
    gain, shift = vector(vec, "gain_one"), vector(vec, "shift_one")
    tile = 256
    tiles = [slice(t * tile, (t + 1) * tile) for t in range(h.shape[0] // tile)]
    ahead = dot_nt(dq[tiles[0], :], wq[...])
    gain_sum = shift_sum = 0.0
    for t, rows in enumerate(tiles):
        total = gr2_ref[rows, :] + ahead
        if t + 1 < len(tiles):
            ahead = dot_nt(dq[tiles[t + 1], :], wq[...])
        normal, root = normalize(r1_ref[rows, :])
        h[rows, :] = (normal * gain + shift).astype(bf16)
        gain_sum = gain_sum + column_sum(total * normal)
        shift_sum = shift_sum + column_sum(total)
        gr1.ref[rows, :] = normalize_back(total, normal, root, gain)
    set_vector("gain_one", gain_sum)
    set_vector("shift_one", shift_sum)
    gr1.send()
    make_sink.pass_on(sink, place, passed)
    m_ref = m_in.get()
    put_grad(sink, place, ROW_CO, dot(ot_ref[...], grad[...]))
    put_grad(sink, place, ROW_CV, dot_tn(m_ref[...], dv.ref[...]))
    sink.send(place, [6, 7])
    set_vector("cross_value_b", column_sum(dv.ref[...]))
    put_grad(sink, place, ROW_CK, dot_tn(m_ref[...], dk.ref[...]))
    sink.send(place, [5])
    put_grad(sink, place, ROW_CQ, dot_tn(h[...], dq[...]))
    sink.send(place, [4])
    set_vector("cross_query_b", column_sum(dq[...]))


def memory_gradient(source, scalars, dk_in, dv_in, *rest):
    (mgrad, w, sems) = rest[source.count_all :]
    copies = source(rest).load(Place(), ROW_CK, w, sems.at[0])
    start(dk_in, dv_in)
    dk, dv = dk_in.get(), dv_in.get()
    wait_all(copies)
    tile = 256
    for t in range(dk.shape[0] // tile):
        rows = slice(t * tile, (t + 1) * tile)
        value = dot_nt(dk[rows, :], rows_of(w, 0)) + dot_nt(dv[rows, :], rows_of(w, 1))
        mgrad.ref[rows, :] = value.astype(bf16)
        mgrad.send(pl.ds(t * tile, tile))


def self_backward(source, make_sink, scalars, k_in, gr1_in, v_in, q_in, lse_in, ot_in, x_in, gv_in,
                  *rest):
    passed = rest[source.count_all : source.count_all + make_sink.passed]
    rest_ = rest[source.count_all + make_sink.passed :]
    dq, dk, dv = rest_[:3]
    count = make_sink.count
    sink = make_sink(rest_[3 : 3 + count])
    (w, grad, gv, *scratch, sems) = rest_[3 + count :]
    place = Place(scalars)
    start(k_in, gr1_in)
    copies = source(rest).load(place, ROW_O, w, sems.at[0])
    keys_ready(place, place.token_bounds, k_in, *scratch[:2])
    start(v_in, q_in, lse_in)
    gr1_ref = gr1_in.get()
    grad[...] = gr1_ref[...].astype(bf16)
    wait_all(copies)
    attend_backward(
        place, place.token_bounds, w[...], grad, v_in, q_in, lse_in, dq, dk, dv, scratch,
        [ot_in, x_in, gv_in, *passed],
    )
    ot_ref, x_ref = ot_in.get(), x_in.get()
    gv[...] = gv_in.get()[...]

    def set_vector(name, value):
        gv[VEC[name] : VEC[name] + 1, :] = value

    make_sink.pass_on(sink, place, passed)
    put_grad(sink, place, ROW_O, dot(ot_ref[...], grad[...]))
    set_vector("out_b", column_sum(grad[...]))
    put_grad(sink, place, ROW_V, dot_tn(x_ref[...], dv.ref[...]))
    sink.send(place, [2])
    set_vector("value_b", column_sum(dv.ref[...]))
    set_vector("query_b", column_sum(dq.ref[...]))
    put_places(place, sink.vector_places(place), gv[...])
    sink.send(place, [3])
    put_grad(sink, place, ROW_K, dot_tn(x_ref[...], dk.ref[...]))
    sink.send(place, [1])
    put_grad(sink, place, ROW_Q, dot_tn(x_ref[...], dq.ref[...]))
    sink.send(place, [0])


def token_gradient(source, scalars, dq_in, dk_in, dv_in, gr1_in, *rest):
    (tgrad, w, sems) = rest[source.count_all :]
    copies = source(rest).load(Place(), ROW_Q, w, sems.at[0])
    start(dq_in, dk_in, dv_in, gr1_in)
    dq, dk, dv, gr1_ref = dq_in.get(), dk_in.get(), dv_in.get(), gr1_in.get()
    wait_all(copies)
    tile = 256
    for t in range(dq.shape[0] // tile):
        rows = slice(t * tile, (t + 1) * tile)
        tgrad.ref[rows, :] = (
            gr1_ref[rows, :]
            + dot_nt(dq[rows, :], rows_of(w, 0))
            + dot_nt(dk[rows, :], rows_of(w, 1))
            + dot_nt(dv[rows, :], rows_of(w, 2))
        ).astype(bf16)
        tgrad.send(pl.ds(t * tile, tile))


def find_bounds(segments_ref, lengths_ref, out_ref):
    segments = segments_ref[...]
    before = jnp.int32(0)
    for i in range(3):
        out_ref[i] = jnp.sum((segments <= i).astype(jnp.int32))
        before = before + lengths_ref[0, i]
        out_ref[3 + i] = before


PAD_ROWS = 304
VEC_AT = ROW_VEC - 31 * CORE_ROWS


def split_shard(slab_ref, keep_ref, send_ref, one_ref, two_ref, full):
    place = Place()
    rows = slab_ref.shape[0]
    full[0:rows, :] = slab_ref[...].astype(f32)
    full[rows : 4 * PAD_ROWS, :] = jnp.zeros((4 * PAD_ROWS - rows, 128), f32)
    for i in range(4):
        part = full[pl.ds(i, PAD_ROWS, 4), :].astype(bf16)
        few_ref = (one_ref, two_ref)[i // 2]
        for core in range(2):

            @pl.when(place.core == core)
            def _():
                (keep_ref if i // 2 == core else send_ref)[i % 2] = part
                first = core * VEC_AT
                few_ref[i % 2] = full[pl.ds(4 * first + i, 16, 4), :].astype(bf16)


def join_unit(_, keep_ref, got_ref, one_ref, two_ref, unit_ref, full):
    place = Place()
    for i in range(2):
        for core in range(2):

            @pl.when(place.core == core)
            def _():
                first, second = (keep_ref, got_ref) if core == 0 else (got_ref, keep_ref)
                full[0:PAD_ROWS, :] = first[i].astype(f32)
                full[CORE_ROWS : CORE_ROWS + PAD_ROWS, :] = second[i].astype(f32)

        ends = one_ref[i].astype(f32) + two_ref[i].astype(f32)
        full[CHIP_ROWS : CHIP_ROWS + 16, :] = ends

        @pl.when(place.y == 0)
        def _():
            unit_ref[0, i] = full[0:UNIT, :].astype(bf16)

        @pl.when(place.y == 1)
        def _():
            unit_ref[0, i, 0:576, :] = full[8:CHIP_ROWS, :].astype(bf16)
            unit_ref[0, i, 576:UNIT, :] = ends.astype(bf16)


def split_unit(here0, across0, mixed1, rest, mixed23, keep, send, far_keep, far_send, vec, full):
    place = Place()
    for i in range(2):
        plane0 = here0[i].astype(f32) + across0[i].astype(f32)

        def rows(core):
            return full[CORE_ROWS * core : CORE_ROWS * core + PAD_ROWS, :]

        full[...] = plane0
        vec[i] = plane0[CHIP_ROWS : CHIP_ROWS + 16, :]
        for core in range(2):

            @pl.when(place.core == core)
            def _():
                far_keep[i] = rows(core).astype(bf16)
                far_send[i] = rows(1 - core).astype(bf16)

        for mixed, chosen in ((mixed1, place.z == 1), (mixed23, place.z >= 2)):

            @pl.when(chosen)
            def _():
                full[...] = mixed[i].astype(f32) + rest[i].astype(f32)

        for core in range(2):

            @pl.when(place.core == core)
            def _():
                keep[i] = rows(core)
                send[i] = rows(1 - core)

        @pl.when(place.z == 0)
        def _():
            far_keep[i, 0:16, :] = vec[i].astype(bf16)
            far_send[i, 0:16, :] = vec[i].astype(bf16)


def join_shard(keep, got, far_keep, far_got, one, two, out_ref, full):
    place = Place()
    rows = out_ref.shape[0]
    last = (place.core == 1) & (place.y == 1) & (place.x == 1) & (place.z == 3)
    for i in range(4):
        for core in range(2):

            @pl.when(place.core == core)
            def _():
                part, far = (keep, far_keep) if i // 2 == core else (got, far_got)
                full[pl.ds(i, PAD_ROWS, 4), :] = part[i % 2]

                @pl.when(place.z == 0)
                def _():
                    full[pl.ds(i, PAD_ROWS, 4), :] = part[i % 2] + far[i % 2].astype(f32)

        @pl.when(last)
        def _():
            at = pl.ds(4 * VEC_AT + i, 16, 4)
            near = (far_got, far_keep)[i // 2]
            full[at, :] = (
                full[at, :] + near[i % 2, 0:16, :].astype(f32) + (one, two)[i // 2][i % 2]
            )

    out_ref[...] = full[0:rows, :]


WHOLE = pl.BlockSpec(memory_space=pltpu.VMEM)


class In:
    def __init__(self, source, buffer, sem):
        self.buffer = buffer
        self.copy = pltpu.make_async_copy(source, buffer, sem)
        self.started = False

    def start(self):
        self.copy.start()
        self.started = True

    def get(self):
        if not self.started:
            self.start()
        self.copy.wait()
        return self.buffer


def start(*arrays):
    for array in arrays:
        array.start()


class Out:
    def __init__(self, target, ref, sem):
        self.target, self.ref, self.sem = target, ref, sem
        self.copies = []

    def send(self, *index):
        source, target = (self.ref.at[index], self.target.at[index]) if index else (self.ref, self.target)
        copy = pltpu.make_async_copy(source, target, self.sem)
        copy.start()
        self.copies.append(copy)

    def finish(self):
        if not self.copies:
            self.send()
        wait_all(self.copies)


class Pair:
    def __init__(self, send, keep, ref, sem):
        self.ref = ref
        self.results = [Out(send, ref.at[0], sem), Out(keep, ref.at[1], sem)]

    def send(self, *index):
        for result in self.results:
            result.send(*index)

    def finish(self):
        for result in self.results:
            result.finish()


def call(body, name, scalars, blocks, weights, outs, scratch, microseconds, passed=(), after=(),
         pairs=()):
    ins = [*blocks, *passed]
    single = len(outs)
    buffers = [pltpu.VMEM(v.shape, v.dtype) for v in ins] + [pltpu.VMEM(s, t) for s, t in outs]
    buffers += [pltpu.VMEM((2, *s), bf16) for s in pairs]
    outs = [*outs, *[(s, bf16) for s in pairs for _ in range(2)]]
    sems = [pltpu.SemaphoreType.DMA((len(ins),))]
    sems.append(pltpu.SemaphoreType.DMA((single + len(pairs),)))

    def run(*refs):
        refs = list(refs)
        take = lambda n: [refs.pop(0) for _ in range(n)]
        scalars_ref, *in_refs = take(1 + len(ins))
        weight_refs, _, out_refs = take(len(weights)), take(len(after)), take(len(outs))
        in_buffers, out_buffers = take(len(ins)), take(single + len(pairs))
        in_sems, out_sems = take(2)
        arrays = [In(in_refs[i], in_buffers[i], in_sems.at[i]) for i in range(len(ins))]
        results = [Out(out_refs[i], out_buffers[i], out_sems.at[i]) for i in range(single)]
        for i in range(len(pairs)):
            send, keep = out_refs[single + 2 * i : single + 2 * i + 2]
            at = single + i
            results.append(Pair(send, keep, out_buffers[at], out_sems.at[at]))
        body(
            scalars_ref, *arrays[: len(blocks)], *weight_refs, *arrays[len(blocks) :], *results, *refs
        )
        for result in results:
            result.finish()

    anywhere = pl.BlockSpec(memory_space=pl.ANY)
    return pl.pallas_call(
        run,
        name=name,
        out_shape=tuple(jax.ShapeDtypeStruct(s, t) for s, t in outs),
        in_specs=[pl.BlockSpec(memory_space=pltpu.SMEM)]
        + [anywhere] * (len(ins) + len(weights) + len(after)),
        out_specs=(anywhere,) * len(outs),
        scratch_shapes=buffers + sems + scratch,
        compiler_params=pltpu.CompilerParams(vmem_limit_bytes=VMEM_LIMIT),
        cost_estimate=pl.CostEstimate(
            flops=microseconds * 1_150_000_000,
            bytes_accessed=microseconds * 3_690_000,
            transcendentals=0,
        ),
    )(scalars, *ins, *weights, *after)


class Source:
    def __init__(self, kind, groups):
        self.kind = kind
        self.groups = groups
        self.count_all = kind.count * (len(groups) if kind is Units else 1)

    def __call__(self, refs):
        return self.kind(self.groups, refs)


class Sinks:
    def __init__(self, entries, first=None, taken=()):
        self.entries = entries
        self.first = first
        self.taken = taken
        self.count = len(entries)
        self.passed = 2 * len(taken)

    def shapes(self):
        return [shape for _, shape in self.entries]

    def __call__(self, pairs):
        if self.first is not None:
            return RowSink(pairs[0], self.first)
        return UnitSink({key: pair for (key, _), pair in zip(self.entries, pairs)})

    def pass_on(self, sink, place, passed):
        for i, (unit, at, count) in enumerate(self.taken):
            far_x, far_y, low = place.turned(unit)
            arrays = [array.get() for array in passed[2 * i : 2 * i + 2]]
            target = sink.pairs[group_of(unit) + 100].ref
            for slot, source in enumerate(arrays):
                for quarter in range(2):
                    target[slot, far_x + 2 * far_y, low, quarter, at : at + count, :] = source[
                        quarter, at : at + count, :
                    ]


class Layer:
    def __init__(self, tokens, memory, slot_cotangent, slot_mask, bounds, sources, weights, sinks):
        self.tokens, self.memory = tokens, memory
        self.slot_cotangent, self.slot_mask = slot_cotangent, slot_mask
        self.bounds, self.sources, self.weights, self.sinks = bounds, sources, weights, sinks
        self.act = tokens.shape
        self.keys = memory.shape[0]
        self.sems = [pltpu.SemaphoreType.DMA((3,))]

    def call(self, body, name, which, blocks, outs, scratch, microseconds, sink=None, **more):
        parts = [self.sources[which]] + ([sink] if sink is not None else [])
        return call(
            functools.partial(body, *parts), name, self.bounds, blocks, self.weights[which], outs,
            scratch + self.sems, microseconds, **more,
        )

    def attend_outs(self, keys):
        length = self.act[0]
        return [
            (self.act, bf16), ((keys, D), bf16), ((keys, D), bf16), ((D, length), bf16),
            ((HEADS, length), f32), (self.act, f32),
        ]

    def attend_scratch(self, keys):
        return [
            wide(D, D), wide(D, D), wide(D, D), wide(D, D), wide(16, D), wide(PAIRS, keys, 256),
            wide(PAIRS, 144, keys),
            wide(*self.act),
        ]

    def self_forward(self, after=()):
        self.q, self.k, self.v, self.ot, self.lse, self.r1 = self.call(
            self_forward, "self_forward", "self", [self.tokens], self.attend_outs(self.act[0]),
            self.attend_scratch(self.act[0]), 18, after=after,
        )

    def cross_forward(self, after=()):
        self.cq, self.mk, self.mv, self.cot, self.clse, self.r2 = self.call(
            cross_forward, "cross_forward", "cross", [self.memory, self.r1],
            self.attend_outs(self.keys), self.attend_scratch(self.keys) + [full(*self.act)],
            19, after=after,
        )

    def prepare(self, after=()):
        length, act = self.act[0], self.act
        self.gs, self.gs2, self.h2 = self.call(
            prepare, "prepare", "self", [self.slot_mask, self.slot_cotangent, self.r2],
            [(act, bf16), (act, bf16), (act, f32)],
            [wide(16, D), full(length, 128), full(length + 8, D)], 5, after=after,
        )

    def ffn(self, after=()):
        length, act, sink = self.act[0], self.act, self.sinks["ffn"]
        self.hlow, self.gr2, *self.g_ffn = self.call(
            ffn, "ffn", "ffn", [self.h2, self.gs, self.gs2, self.r2],
            [(act, bf16), (act, f32)],
            [
                wide(4, D, D), wide(FF, D), wide(FF, D), wide(2 * D, D), wide(VEC_ROWS, D),
                full(4, FF, 128), wide(length, FF), wide(length, FF), full(*act), wide(*act),
                full(*act), wide(*act), full(128, D),
            ],
            34, sink, after=after, pairs=sink.shapes(),
        )

    def slot_forward(self, after=()):
        length = self.act[0]
        (self.slots,) = self.call(
            slot_forward, "slot_forward", "ffn", [self.slot_mask, self.hlow], [(self.act, bf16)],
            [wide(2 * D, D), wide(VEC_ROWS, D), full(length + 8, D), full(length, 128)], 6,
            after=after,
        )

    def back_scratch(self, keys):
        return [
            wide(PAIRS, keys, 256), wide(D, keys), full(keys, D), full(keys, D), wide(*self.act)
        ]

    def cross_backward(self, after=()):
        sink = self.sinks["cross"]
        self.mdk, self.mdv, self.gr1, self.gv, *self.g_cross = self.call(
            cross_backward, "cross_backward", "cross",
            [self.mk, self.gr2, self.mv, self.cq, self.clse, self.cot, self.r1, self.memory],
            [((self.keys, D), bf16)] * 2 + [(self.act, f32), ((16, D), f32)],
            [wide(D, D), wide(D, D), wide(16, D)] + [wide(*self.act)] * 3
            + self.back_scratch(self.keys),
            28, sink, passed=self.g_ffn[: sink.passed], after=after, pairs=sink.shapes(),
        )

    def self_backward(self, after=()):
        sink = self.sinks["self"]
        length = self.act[0]
        self.dq, self.dk, self.dv, *self.g_self = self.call(
            self_backward, "self_backward", "self",
            [self.k, self.gr1, self.v, self.q, self.lse, self.ot, self.tokens, self.gv],
            [(self.act, bf16)] * 3,
            [wide(D, D), wide(*self.act), full(16, D)] + self.back_scratch(length),
            26, sink, passed=self.g_cross[: sink.passed], after=after, pairs=sink.shapes(),
        )

    def memory_gradient(self, after=()):
        (self.memory_grad,) = self.call(
            memory_gradient, "memory_gradient", "cross", [self.mdk, self.mdv],
            [((self.keys, D), bf16)], [wide(2 * D, D)], 5, after=after,
        )

    def token_gradient(self, after=()):
        (self.tokens_grad,) = self.call(
            token_gradient, "token_gradient", "self", [self.dq, self.dk, self.dv, self.gr1],
            [(self.act, bf16)], [wide(3 * D, D)], 6, after=after,
        )


def wide(*shape):
    return pltpu.VMEM(shape, bf16)


def full(*shape):
    return pltpu.VMEM(shape, f32)


def plain_layer(args, param_slabs):
    gathered = lax.all_gather(param_slabs, AXES, axis=0, tiled=True)
    total_rows = gathered.shape[0] // 4
    rows = gathered.reshape(total_rows, 4, 128)
    pieces = [rows[:, i, :] for i in range(4)]
    shapes = {"self": 2048 + 16, "cross": 2048, "ffn": 5120 + 128}
    firsts = {"self": 0, "cross": 2048, "ffn": 4096}
    sinks = {name: Sinks([(0, (2, shapes[name], 128))], firsts[name]) for name in shapes}
    source = Source(Pieces, ())
    run = Layer(*args, {n: source for n in shapes}, {n: pieces for n in shapes}, sinks)
    run.self_forward()
    run.cross_forward()
    run.prepare()
    run.ffn()
    run.cross_backward()
    run.self_backward()
    run.slot_forward()
    run.memory_gradient()
    run.token_gradient()
    send, keep = [
        jnp.concatenate([run.g_self[i][:, :2048], run.g_cross[i], run.g_ffn[i]], axis=1)
        .at[:, ROW_VEC : ROW_VEC + 16]
        .add(run.g_self[i][:, 2048:])
        for i in range(2)
    ]
    first = lax.axis_index("narrow") % 2 == 0
    low = jnp.where(first, keep, send)
    high = jnp.where(first, send, keep)
    flat = jnp.concatenate([low, high], axis=0).transpose(1, 0, 2)
    flat = jnp.pad(flat, ((0, total_rows - flat.shape[0]), (0, 0), (0, 0))).reshape(-1, 128)
    param_grad = lax.psum_scatter(flat, AXES, scatter_dimension=0, tiled=True).astype(f32)
    return run.slots, run.tokens_grad, run.memory_grad, param_grad


def moves(rule):
    number = lambda z, x, y, c: ((z * 2 + x) * 2 + y) * 2 + c
    pairs = []
    for z in range(4):
        for x in range(2):
            for y in range(2):
                for c in range(2):
                    target = rule(z, x, y, c)
                    if target is not None:
                        pairs.append((number(z, x, y, c), number(*target)))
    return pairs


OTHER_CORE = moves(lambda z, x, y, c: (z, x, y, 1 - c))
ALONG_X = moves(lambda z, x, y, c: (z, 1 - x, y, c))
ALONG_Y = moves(lambda z, x, y, c: (z, x, 1 - y, c))
ALONG_BOTH = moves(lambda z, x, y, c: (z, 1 - x, 1 - y, c))
ALONG_Z = moves(lambda z, x, y, c: (z ^ 1, x, y, c))
TWO_ALONG_Z = moves(lambda z, x, y, c: (z ^ 2, x, y, c))


def hops(table):
    return moves(lambda z, x, y, c: (table[z], x, y, c) if z in table else None)


def permute(value, pairs):
    return lax.ppermute(value, AXES, pairs)


def total(*values):
    return sum(value.astype(f32) for value in values).astype(bf16)


def spread_plane(own):
    return [own] + [permute(own, pairs) for pairs in (ALONG_X, ALONG_Y, ALONG_BOTH)]


def to_other_core(values):
    return [permute(value, OTHER_CORE) for value in values]


def sum_plane(keep, got):
    return [
        permute(total(keep[i], got[i]), pairs)
        for i, pairs in ((1, ALONG_X), (2, ALONG_Y), (3, ALONG_BOTH))
    ]


def here(keep, got, arrived):
    return total(keep[0], got[0], *arrived)


def hold(arrays, after):
    anywhere = pl.BlockSpec(memory_space=pl.ANY)
    return pl.pallas_call(
        lambda *refs: None, name="hold",
        out_shape=tuple(jax.ShapeDtypeStruct(v.shape, v.dtype) for v in arrays),
        in_specs=[anywhere] * (len(arrays) + len(after)), out_specs=(anywhere,) * len(arrays),
        input_output_aliases={i: i for i in range(len(arrays))},
    )(*arrays, *after)


def chip_layer(args, param_slabs):
    z = lax.axis_index("wide") // 2
    shard_rows = param_slabs.shape[0]
    small = lambda *s: jax.ShapeDtypeStruct(s, bf16)
    real = lambda *s: jax.ShapeDtypeStruct(s, f32)
    keep, send, one, two = pl.pallas_call(
        split_shard, name="split_shard",
        out_shape=(small(2, PAD_ROWS, 128),) * 2 + (small(2, 16, 128),) * 2,
        in_specs=[WHOLE], out_specs=(WHOLE,) * 4, scratch_shapes=[full(4 * PAD_ROWS, 128)],
    )(param_slabs)
    got = permute(send, OTHER_CORE)

    def few(core):
        def rule(z, x, y, c):
            if (y, c) == (1, 0):
                return (z, x, 0, core)
            return (0, 1, 1, core) if (z, x, y, c) == (3, 1, 1, 1) else None

        return moves(rule)

    one, two = permute(one, few(0)), permute(two, few(1))
    (unit,) = pl.pallas_call(
        join_unit, name="join_unit", out_shape=(small(1, 2, UNIT, 128),),
        in_specs=[pl.BlockSpec(memory_space=pltpu.SMEM)] + [WHOLE] * 4, out_specs=(WHOLE,),
        scratch_shapes=[full(2 * PAD_ROWS, 128)],
    )(args[4], keep, got, one, two)

    first = permute(unit, hops({0: 2, 1: 0, 3: 1}))
    plane0 = jnp.where(z == 0, unit, first)
    second = permute(jnp.where(z == 1, unit, plane0), hops({0: 1, 1: 2, 2: 3}))
    plane0 = jnp.where(z % 2 == 1, second, plane0)
    (unit,) = hold([unit], [plane0])
    mine0 = spread_plane(plane0)
    third = permute(second, hops({2: 3}))
    fourth = permute(unit, hops({2: 0}))
    plane1 = jnp.where(z < 2, jnp.where(z == 0, first, unit), jnp.where(z == 2, second, third))
    high = jnp.where(z < 2, jnp.where(z == 0, fourth, first), unit)
    *mine0[1:], plane1, high = hold([*mine0[1:], plane1, high], [])
    groups = [mine0 + to_other_core(mine0), None, None]
    mine1 = spread_plane(plane1)
    near = permute(high, ALONG_Z)
    used = {"self": (0,), "cross": (0, 1), "ffn": (1, 2)}
    sources = {name: Source(Units, group) for name, group in used.items()}
    weights = {"self": groups[0]}
    one_unit = (2, SUM_UNIT, 128)
    sinks = {
        "ffn": Sinks([(7, one_unit), (102, (4, 2, 2, SUM_UNIT, 128))]),
        "cross": Sinks([(3, one_unit), (101, (4, 1, 2, SUM_UNIT, 128))], taken=[(7, 0, 592)]),
        "self": Sinks([(100, (4, 1, 2, SUM_UNIT, 128))], taken=[(3, 288, 304)]),
    }
    run = Layer(*args, sources, weights, sinks)
    run.self_forward()
    *mine1[1:], near = hold(mine1[1:] + [near], [run.r1])
    groups[1] = mine1 + to_other_core(mine1)
    weights["cross"] = groups[0] + groups[1]
    mine23 = spread_plane(jnp.concatenate([high, near], axis=0))
    run.cross_forward()
    run.prepare()
    mine23[1:] = hold(mine23[1:], [run.h2])
    groups[2] = mine23 + to_other_core(mine23)
    weights["ffn"] = groups[1] + groups[2]
    run.ffn()
    send23, keep23 = run.g_ffn[2:4]
    got23 = permute(send23, OTHER_CORE)
    arrived23 = sum_plane(keep23, got23)
    run.cross_backward()
    send1, keep1 = run.g_cross[2:4]
    (send1,) = hold([send1], arrived23)
    got1 = permute(send1, OTHER_CORE)
    arrived1 = sum_plane(keep1, got1)
    here23 = here(keep23, got23, arrived23)
    across23 = permute(here23[1], ALONG_Z)
    run.self_backward()
    send0, keep0 = run.g_self
    (send0,) = hold([send0], [*arrived1, across23])
    got0 = permute(send0, OTHER_CORE)
    here1 = here(keep1, got1, arrived1)[0]
    across1 = permute(here1, hops({0: 1, 3: 2}))
    arrived0 = sum_plane(keep0, got0)
    run.memory_gradient()
    run.token_gradient(after=arrived0)
    run.slot_forward()
    mixed23 = total(here23[0], across23)
    mixed1 = total(here1, across1)
    rest = permute(jnp.where(z < 2, mixed23, mixed1), hops({0: 2, 1: 3, 2: 1}))
    here0 = here(keep0, got0, arrived0)[0]
    (here0,) = hold([here0], [across1, run.memory_grad])
    across0 = permute(here0, hops({1: 0, 3: 2}))
    (across0,) = hold([across0], [rest, run.tokens_grad])
    keep, send, far_keep, far_send, vec = pl.pallas_call(
        split_unit, name="split_unit",
        out_shape=(real(2, PAD_ROWS, 128),) * 2 + (small(2, PAD_ROWS, 128),) * 2
        + (real(2, 16, 128),),
        in_specs=[WHOLE] * 5, out_specs=(WHOLE,) * 5, scratch_shapes=[full(SUM_UNIT, 128)],
    )(here0, across0, mixed1, rest, mixed23)

    def down(other):
        def rule(z, x, y, c):
            if z == 2:
                return (0, x, y, c ^ other)
            return (3, 1, 1, 1) if (z, x, y, c) == (0, 1, 1, 1 - other) else None

        return moves(rule)

    one, two = [
        permute(vec, moves(lambda z, x, y, c: (3, 1, 1, 1) if (z, x, y, c) == (2, 1, 1, core) else None))
        for core in range(2)
    ]
    far_keep, far_got = permute(far_keep, down(0)), permute(far_send, down(1))
    got = permute(send, OTHER_CORE)
    (got,) = hold([got], [run.slots])
    (param_grad,) = pl.pallas_call(
        join_shard, name="join_shard", out_shape=(real(shard_rows, 128),),
        in_specs=[WHOLE] * 6, out_specs=(WHOLE,), scratch_shapes=[full(4 * PAD_ROWS, 128)],
    )(keep, got, far_keep, far_got, one, two)
    return run.slots, run.tokens_grad, run.memory_grad, param_grad


def shards(mesh_shape, tokens, memory, slot_cotangent, param_slabs, segment_ids, memory_lengths,
           slot_mask):
    smem = pl.BlockSpec(memory_space=pltpu.SMEM)
    bounds = pl.pallas_call(
        find_bounds, name="find_bounds", out_shape=jax.ShapeDtypeStruct((8,), jnp.int32),
        in_specs=[WHOLE, smem], out_specs=smem,
    )(segment_ids, memory_lengths)
    chips = mesh_shape == (8, 4) and param_slabs.shape[0] == 4 * CORE_ROWS
    args = (tokens, memory, slot_cotangent, slot_mask, bounds)
    return (chip_layer if chips else plain_layer)(args, param_slabs)


def solution(mesh):
    spec = P(AXES, None)
    shape = tuple(mesh.shape[axis] for axis in AXES)
    return jax.shard_map(
        functools.partial(shards, shape),
        mesh=mesh,
        in_specs=(spec,) * 7,
        out_specs=(spec,) * 4,
        check_vma=False,
    )
```
